32 devices in a mesh: blocks: 32 (over z, y, x, core).
Axes of the slice: x: 2, y: 2, z: 4, core: 2. Of those that a mesh axis runs over, the one named last changes fastest.
Arguments:
- old_pdfs: float32 [64, 19, 32768], P('blocks'), may hold values from 0 to 0.5
- old_slot: int32 [32], replicated, may hold values from 0 to 63, as said below
- neighbours: int32 [32, 18], P('blocks'), may hold values from -1 to 31, as said below
- cell_flags: int32 [32, 32768], P('blocks'), may hold values from 0 to 3, as said below
Outputs:
- new_pdfs: float32 [32, 19, 32768], P('blocks')
The draws below stay inside these ranges and needn't reach their ends.
Inputs may be any that keep to these rules, and one draw needn't show every extreme that they name: `old_slot`: distinct slots; slot s lies on device s // 2 before migration; in every draw some device has all 2 of its slots in use. `neighbours`: the blocks form 8 layers of 2 x 2 blocks along a vessel, blocks 4 * l to 4 * l + 3 making layer l; column d names the block at block offset c_(d+1), or -1 where there is none; the relation is mutual. `cell_flags`: 0 fluid, 1 wall, 2 inlet, 3 outlet; the cells on the outermost layer of every block are fluid.
All inputs are finite; a program needn't handle non-finite values.
Results may differ from the reference program's by a relative error of at most 0.0003.
Values sent between devices are 32-bit elements; how exact they have to be, the bound alone decides.
A program may use at most 192 MiB of HBM per device.

```python
import jax
import jax.numpy as jnp
import numpy as np
from jax import lax

EDGE = 32
STEPS = 2
SLOT_DEV = 2
FLUID_BLOCKS = 32
ALL_SLOTS = 64
CELLS = 32768


VELOCITY = ((0, 0, 0), (1, 0, 0), (-1, 0, 0), (0, 1, 0), (0, -1, 0), (0, 0, 1), (0, 0, -1), (1, 1, 0), (-1, -1, 0), (1, -1, 0), (-1, 1, 0), (1, 0, 1), (-1, 0, -1), (1, 0, -1), (-1, 0, 1), (0, 1, 1), (0, -1, -1), (0, 1, -1), (0, -1, 1))


WEIGHT_LIST = (1.0 / 3.0,) + (1.0 / 18.0,) * 6 + (1.0 / 36.0,) * 12


def draw_old_pdfs(key, part):
    weights = jnp.asarray(WEIGHT_LIST, jnp.float32)[None, :, None]
    normal_noise = jax.random.normal(key, (ALL_SLOTS, 19, CELLS), jnp.float32)
    return weights * (1.0 + 0.2 * jnp.clip(normal_noise, -2.0, 2.0))


def draw_old_slot(key, part):
    choose_key, score_key, order_key = jax.random.split(key, 3)
    full_device = jax.random.randint(choose_key, (), 0, ALL_SLOTS // SLOT_DEV)
    slot_index = jnp.arange(ALL_SLOTS, dtype=jnp.int32)
    scores = jax.random.randint(score_key, (ALL_SLOTS,), 0, 2 ** 20) * ALL_SLOTS + slot_index
    ordering = jnp.argsort(scores)
    elsewhere_flag = (ordering // SLOT_DEV != full_device).astype(jnp.int32)
    ordering = ordering[jnp.argsort(elsewhere_flag, stable=True)]
    chosen = ordering[:FLUID_BLOCKS]
    return jax.random.permutation(order_key, chosen).astype(jnp.int32)


def draw_neighbours(key, part):
    layer_count = FLUID_BLOCKS // 4
    scores = jax.random.randint(key, (layer_count, 4), 0, 2 ** 20) * 4 + jnp.arange(4, dtype=jnp.int32)
    placement = jnp.argsort(scores, axis=1).astype(jnp.int32)
    inverse = jnp.argsort(placement, axis=1).astype(jnp.int32)
    layer_index = jnp.arange(FLUID_BLOCKS, dtype=jnp.int32) // 4
    block_spot = placement.reshape(-1)
    across_x = block_spot % 2
    across_y = block_spot // 2
    columns = []
    for direction in VELOCITY[1:]:
        target_x = across_x + direction[0]
        target_y = across_y + direction[1]
        target_layer = layer_index + direction[2]
        inside = (target_x >= 0) & (target_x <= 1) & (target_y >= 0) & (target_y <= 1) & (target_layer >= 0) & (target_layer < layer_count)
        clipped_layer = jnp.clip(target_layer, 0, layer_count - 1)
        target_spot = jnp.clip(target_x, 0, 1) + 2 * jnp.clip(target_y, 0, 1)
        target = 4 * clipped_layer + inverse[clipped_layer, target_spot]
        columns.append(jnp.where(inside, target, -1))
    return jnp.stack(columns, axis=1).astype(jnp.int32)


def draw_cell_flags(key, part):
    raw_draw = jax.random.randint(key, (FLUID_BLOCKS, CELLS), 0, 100)
    cell_kind = jnp.where(raw_draw < 76, 0, jnp.where(raw_draw < 90, 1, jnp.where(raw_draw < 95, 2, 3)))
    cell_index = jnp.arange(CELLS, dtype=jnp.int32)
    coord_x = cell_index // (EDGE * EDGE)
    coord_y = cell_index // EDGE % EDGE
    coord_z = cell_index % EDGE
    outer_cell = (coord_x == 0) | (coord_x == EDGE - 1) | (coord_y == 0) | (coord_y == EDGE - 1) | (coord_z == 0) | (coord_z == EDGE - 1)
    return jnp.where(outer_cell[None, :], 0, cell_kind).astype(jnp.int32)


def setup_inputs(seed: int = 0) -> dict:
    keys = jax.random.split(jax.random.key(seed), 5)
    old_pdfs = draw_old_pdfs(jax.random.fold_in(keys[4], 71), 0)
    old_slot = draw_old_slot(jax.random.fold_in(keys[4], 71), 0)
    neighbours = draw_neighbours(jax.random.fold_in(keys[4], 71), 0)
    cell_flags = draw_cell_flags(jax.random.fold_in(keys[4], 71), 0)
    return dict(old_pdfs=old_pdfs, old_slot=old_slot, neighbours=neighbours, cell_flags=cell_flags)


VELOCITY = ((0, 0, 0), (1, 0, 0), (-1, 0, 0), (0, 1, 0), (0, -1, 0), (0, 0, 1), (0, 0, -1), (1, 1, 0), (-1, -1, 0), (1, -1, 0), (-1, 1, 0), (1, 0, 1), (-1, 0, -1), (1, 0, -1), (-1, 0, 1), (0, 1, 1), (0, -1, -1), (0, 1, -1), (0, -1, 1))
WEIGHT_LIST = (1.0 / 3.0,) + (1.0 / 18.0,) * 6 + (1.0 / 36.0,) * 12
RELAXATION = (0.0, 0.0, 0.0, 0.0, 1.19, 1.4, 1.2, 1.2, 1.2, 1.6, 1.6, 1.6, 1.6, 1.6, 1.4, 1.4, 1.98, 1.98, 1.98)
INLET_SPEED = (0.0, 0.0, 0.05)

def collision_table():
    lattice = np.array(VELOCITY) * 1.0
    along_x, along_y, along_z = (lattice[:, 0], lattice[:, 1], lattice[:, 2])
    squared = along_x * along_x + along_y * along_y + along_z * along_z
    monomials = [np.ones(19), along_x, along_y, along_z, squared, squared * squared, squared * along_x, squared * along_y, squared * along_z, 3.0 * along_x * along_x - squared, along_y * along_y - along_z * along_z, along_x * along_y, along_y * along_z, along_x * along_z, squared * (3.0 * along_x * along_x - squared), squared * (along_y * along_y - along_z * along_z), (along_y * along_y - along_z * along_z) * along_x, (along_z * along_z - along_x * along_x) * along_y, (along_x * along_x - along_y * along_y) * along_z]
    orthonormal = []
    for vector in monomials:
        for earlier in orthonormal:
            vector = vector - np.dot(vector, earlier) * earlier
        orthonormal.append(vector / np.sqrt(np.dot(vector, vector)))
    stacked = np.stack(orthonormal)
    return stacked.T * np.array(RELAXATION) @ stacked

def opposite(index_value):
    if index_value == 0:
        return 0
    return index_value + 1 if index_value % 2 == 1 else index_value - 1

def ghost_region(offset, edge_size):
    return tuple((slice(0, 1) if component < 0 else slice(edge_size + 1, edge_size + 2) if component > 0 else slice(1, edge_size + 1) for component in offset))

def outer_layer(offset, edge_size):
    return tuple((slice(edge_size - 1, edge_size) if component > 0 else slice(0, 1) if component < 0 else slice(0, edge_size) for component in offset))

def collide(values, collision):
    lattice = jnp.asarray(VELOCITY, jnp.float32).T
    weights = jnp.asarray(WEIGHT_LIST, jnp.float32)[None, :, None]
    density = lax.optimization_barrier(jnp.sum(values, axis=1, keepdims=True))
    momentum = jnp.einsum('ki,bin->bkn', lattice, values, precision=lax.Precision.HIGHEST)
    projected = jnp.einsum('ki,bkn->bin', lattice, momentum, precision=lax.Precision.HIGHEST)
    speed_square = lax.optimization_barrier(jnp.sum(momentum * momentum, axis=1, keepdims=True))
    balance = weights * (density + 3.0 * projected + 4.5 * projected * projected - 1.5 * speed_square)
    return values - jnp.einsum('pq,bqn->bpn', collision, values - balance, precision=lax.Precision.HIGHEST)

def propagate(padded, source_flags, collided_cells, block_flags):
    edge_size = block_flags.shape[-1]
    momentum = []
    for axis_index in range(3):
        running_sum = jnp.zeros_like(collided_cells[:, 0])
        for index_value in range(19):
            component = VELOCITY[index_value][axis_index]
            if component != 0:
                running_sum = running_sum + component * collided_cells[:, index_value]
        momentum.append(running_sum)
    speed_square = momentum[0] * momentum[0] + momentum[1] * momentum[1] + momentum[2] * momentum[2]
    inlet_square = sum((component * component for component in INLET_SPEED))
    results = []
    for index_value in range(19):
        offset = VELOCITY[index_value]
        weight = WEIGHT_LIST[index_value]
        window_slice = tuple((slice(1 - component, 1 - component + edge_size) for component in offset))
        pulled = padded[(slice(None), index_value) + window_slice]
        source_kind = source_flags[(slice(None),) + window_slice]
        bounce = collided_cells[:, opposite(index_value)]
        inlet_along = sum((component * inlet_part for component, inlet_part in zip(offset, INLET_SPEED)))
        inlet_value = weight * (1.0 + 3.0 * inlet_along + 4.5 * inlet_along * inlet_along - 1.5 * inlet_square)
        outlet_along = offset[0] * momentum[0] + offset[1] * momentum[1] + offset[2] * momentum[2]
        outlet_value = weight * (1.0 + 3.0 * outlet_along + 4.5 * outlet_along * outlet_along - 1.5 * speed_square)
        new_value = jnp.where(source_kind == 0, pulled, jnp.where(source_kind == 1, bounce, jnp.where(source_kind == 2, inlet_value, outlet_value)))
        results.append(jnp.where(block_flags == 0, new_value, 0.0))
    return jnp.stack(results, axis=1)

def advance_block(collided_all, block_id, block_flags, neighbour_row):
    own_block = collided_all[block_id]
    padded = jnp.zeros((19, EDGE + 2, EDGE + 2, EDGE + 2), jnp.float32).at[:, 1:-1, 1:-1, 1:-1].set(own_block)
    source_flags = jnp.ones((EDGE + 2, EDGE + 2, EDGE + 2), jnp.int32).at[1:-1, 1:-1, 1:-1].set(block_flags)
    for direction_code in range(18):
        offset = VELOCITY[direction_code + 1]
        target = neighbour_row[direction_code]
        present = target >= 0
        other_block = collided_all[jnp.maximum(target, 0)]
        region = ghost_region(offset, EDGE)
        facing = outer_layer(tuple((-component for component in offset)), EDGE)
        padded = padded.at[(slice(None),) + region].set(other_block[(slice(None),) + facing])
        source_flags = source_flags.at[region].set(jnp.where(present, 0, 1).astype(jnp.int32))
    return propagate(padded[None], source_flags[None], own_block[None], block_flags[None])[0]

def reference(old_pdfs, old_slot, neighbours, cell_flags):
    collision = jnp.asarray(collision_table(), jnp.float32)
    pdf_state = jnp.take(old_pdfs, old_slot.astype(jnp.int32), axis=0)
    flags_all = cell_flags.reshape(FLUID_BLOCKS, EDGE, EDGE, EDGE)
    block_ids = jnp.arange(FLUID_BLOCKS, dtype=jnp.int32)
    for step_index in range(STEPS):
        collided = lax.map(lambda single_block: collide(single_block[None], collision)[0], pdf_state)
        collided_all = collided.reshape(FLUID_BLOCKS, 19, EDGE, EDGE, EDGE)

        def advance(entry_tuple):
            return advance_block(collided_all, entry_tuple[0], entry_tuple[1], entry_tuple[2])
        pdf_state = lax.map(advance, (block_ids, flags_all, neighbours)).reshape(FLUID_BLOCKS, 19, CELLS)
    return pdf_state
```

```python
import functools

import jax
import jax.numpy as jnp
import numpy as np
from jax import lax
from jax.experimental import pallas as pl
from jax.experimental.pallas import tpu as pltpu
from jax.sharding import PartitionSpec as P

EDGE = 32
STEPS = 2
MESH = pl.DeviceIdType.MESH

VELOCITY = (
    (0, 0, 0),
    (1, 0, 0),
    (-1, 0, 0),
    (0, 1, 0),
    (0, -1, 0),
    (0, 0, 1),
    (0, 0, -1),
    (1, 1, 0),
    (-1, -1, 0),
    (1, -1, 0),
    (-1, 1, 0),
    (1, 0, 1),
    (-1, 0, -1),
    (1, 0, -1),
    (-1, 0, 1),
    (0, 1, 1),
    (0, -1, -1),
    (0, 1, -1),
    (0, -1, 1),
)
WEIGHT_LIST = (1.0 / 3.0,) + (1.0 / 18.0,) * 6 + (1.0 / 36.0,) * 12
RELAXATION = (
    0.0,
    0.0,
    0.0,
    0.0,
    1.19,
    1.4,
    1.2,
    1.2,
    1.2,
    1.6,
    1.6,
    1.6,
    1.6,
    1.6,
    1.4,
    1.4,
    1.98,
    1.98,
    1.98,
)
INLET_SPEED = (0.0, 0.0, 0.05)

X_PLUS, X_MINUS = (1, 7, 9, 11, 13), (2, 8, 10, 12, 14)
Y_PLUS, Y_MINUS = (3, 7, 10, 15, 17), (4, 8, 9, 16, 18)
Z_PLUS, Z_MINUS = (5, 11, 14, 15, 18), (6, 12, 13, 16, 17)
ORBITS = ((0,), (1, 2), (3, 4), (5, 6), (7, 8, 9, 10), (11, 12, 13, 14), (15, 16, 17, 18))


def collision_table():
    lattice = np.array(VELOCITY) * 1.0
    along_x, along_y, along_z = (lattice[:, 0], lattice[:, 1], lattice[:, 2])
    squared = along_x * along_x + along_y * along_y + along_z * along_z
    monomials = [
        np.ones(19),
        along_x,
        along_y,
        along_z,
        squared,
        squared * squared,
        squared * along_x,
        squared * along_y,
        squared * along_z,
        3.0 * along_x * along_x - squared,
        along_y * along_y - along_z * along_z,
        along_x * along_y,
        along_y * along_z,
        along_x * along_z,
        squared * (3.0 * along_x * along_x - squared),
        squared * (along_y * along_y - along_z * along_z),
        (along_y * along_y - along_z * along_z) * along_x,
        (along_z * along_z - along_x * along_x) * along_y,
        (along_x * along_x - along_y * along_y) * along_z,
    ]
    orthonormal = []
    for vector in monomials:
        for earlier in orthonormal:
            vector = vector - np.dot(vector, earlier) * earlier
        orthonormal.append(vector / np.sqrt(np.dot(vector, vector)))
    stacked = np.stack(orthonormal)
    return stacked.T * np.array(RELAXATION) @ stacked


def opposite(index_value):
    if index_value == 0:
        return 0
    return index_value + 1 if index_value % 2 == 1 else index_value - 1


def code_of(offset):
    return VELOCITY.index(tuple(offset)) - 1


def collision_blocks():
    matrix = collision_table().astype(np.float32).astype(np.float64)
    even = [[float(np.mean([matrix[a[0], b] for b in group])) for group in ORBITS] for a in ORBITS]
    odd = []
    for axis in range(3):
        groups = [g for g in ORBITS if any(VELOCITY[b][axis] for b in g)]
        rows = []
        for a in groups:
            first = next(c for c in a if VELOCITY[c][axis] > 0)
            rows.append(
                [float(np.mean([VELOCITY[b][axis] * matrix[first, b] for b in g])) for g in groups]
            )
        odd.append(rows)
    mixed = []
    for group in ORBITS[4:]:
        signs = [1.0, 1.0, -1.0, -1.0]
        mixed.append(float(np.mean([s * matrix[group[0], b] for s, b in zip(signs, group)])))
    return even, odd, mixed


def dot(coefficients, terms):
    total = None
    for coefficient, term in zip(coefficients, terms):
        part = term * np.float32(coefficient)
        total = part if total is None else total + part
    return total


def collide(f):
    even, odd, mixed = collision_blocks()
    pair_sum = [f[i] + f[i + 1] for i in (1, 3, 5)]
    pair_dif = [f[i] - f[i + 1] for i in (1, 3, 5)]
    quad_sum, quad_mix, quad_one, quad_two = [], [], [], []
    for i in (7, 11, 15):
        sum_a, sum_b = f[i] + f[i + 1], f[i + 2] + f[i + 3]
        dif_a, dif_b = f[i] - f[i + 1], f[i + 2] - f[i + 3]
        quad_sum.append(sum_a + sum_b)
        quad_mix.append(sum_a - sum_b)
        quad_one.append(dif_a + dif_b)
        quad_two.append(dif_a - dif_b)
    odd_terms = [
        [pair_dif[0], quad_one[0], quad_one[1]],
        [pair_dif[1], quad_two[0], quad_one[2]],
        [pair_dif[2], quad_two[1], quad_two[2]],
    ]
    rho = f[0] + (pair_sum[0] + pair_sum[1] + pair_sum[2]) + (quad_sum[0] + quad_sum[1] + quad_sum[2])
    j = [t[0] + t[1] + t[2] for t in odd_terms]
    sq = [c * c for c in j]
    base = rho - 1.5 * (sq[0] + sq[1] + sq[2])
    sq45 = [4.5 * s for s in sq]
    w0, w1, w2 = 1.0 / 3.0, 1.0 / 18.0, 1.0 / 36.0
    even_terms = [f[0] - w0 * base]
    for a in range(3):
        even_terms.append(pair_sum[a] - (2.0 * w1) * (base + sq45[a]))
    for q, (a, b) in enumerate(((0, 1), (0, 2), (1, 2))):
        even_terms.append(quad_sum[q] - (4.0 * w2) * (base + sq45[a] + sq45[b]))
    mix = [
        (quad_mix[q] - j[a] * j[b]) * np.float32(mixed[q])
        for q, (a, b) in enumerate(((0, 1), (0, 2), (1, 2)))
    ]
    odd_out = []
    for a in range(3):
        third = j[a] * np.float32(1.0 / 3.0)
        terms = [t - third for t in odd_terms[a]]
        odd_out.append([dot(row, terms) for row in odd[a]])
    even_out = [dot(row, even_terms) for row in even]
    out = [f[0] - even_out[0]]
    for a in range(3):
        out.append(f[1 + 2 * a] - (even_out[1 + a] + odd_out[a][0]))
        out.append(f[2 + 2 * a] - (even_out[1 + a] - odd_out[a][0]))
    for q, (one, two) in enumerate(
        (
            (odd_out[0][1], odd_out[1][1]),
            (odd_out[0][2], odd_out[2][1]),
            (odd_out[1][2], odd_out[2][2]),
        )
    ):
        i = 7 + 4 * q
        plus, minus = even_out[4 + q] + mix[q], even_out[4 + q] - mix[q]
        both, apart = one + two, one - two
        out.append(f[i] - (plus + both))
        out.append(f[i + 1] - (plus - both))
        out.append(f[i + 2] - (minus + apart))
        out.append(f[i + 3] - (minus - apart))
    return out


def positions():
    lane = lax.broadcasted_iota(jnp.int32, (8, 128), 1)
    sub = lax.broadcasted_iota(jnp.int32, (8, 128), 0)
    return lane, sub


def shift_y(v, step, ghost, lane, sub):
    if step > 0:
        moved = pltpu.roll(v, 32, 1)
        out = jnp.where(lane < 32, pltpu.roll(moved, 1, 0), moved)
        return jnp.where((lane < 32) & (sub == 0), ghost, out)
    moved = pltpu.roll(v, 96, 1)
    out = jnp.where(lane >= 96, pltpu.roll(moved, 7, 0), moved)
    return jnp.where((lane >= 96) & (sub == 7), ghost, out)


def shift_z(v, step, ghost, z):
    moved = pltpu.roll(v, 1 if step > 0 else 127, 1)
    return jnp.where(z == (0 if step > 0 else 31), ghost, moved)


def unpack_ghosts(nbr, rxy, gy):
    lane, _ = positions()
    jy = jnp.maximum(nbr[0, 2], nbr[0, 3]) & 3
    jd = jnp.maximum(jnp.maximum(nbr[0, 6], nbr[0, 7]), jnp.maximum(nbr[0, 8], nbr[0, 9])) & 3
    for k in range(5):
        packed = rxy[jy, 5 + k]
        for g in range(4):
            low = pltpu.roll(packed, (128 - 32 * g) % 128, 1)
            high = pltpu.roll(packed, (96 - 32 * g) % 128, 1)
            gy[k, 1 + 8 * g : 9 + 8 * g, :] = jnp.where(lane < 64, low, high)
    for channel in (7, 8, 9, 10):
        cx, cy, _ = VELOCITY[channel]
        kx = (X_PLUS if cx > 0 else X_MINUS).index(channel)
        ky = (Y_PLUS if cy > 0 else Y_MINUS).index(channel)
        plane = rxy[jd, kx]
        row = pltpu.roll(plane, 32 if cy > 0 else 96, 1)
        row = row[7:8, :] if cy > 0 else row[0:1, :]
        spot = 0 if cx > 0 else 33
        gy[ky, spot : spot + 1, :] = row


def pull(x, nbr, c, rxy, rb, ra, flags, gy):
    lane, sub = positions()
    z = lane & 31
    jx = jnp.maximum(nbr[0, 0], nbr[0, 1]) & 3

    def wall(offset):
        return jnp.where(nbr[0, code_of(offset)] >= 0, 0, 1).astype(jnp.int32)

    def spot(offset):
        return nbr[0, code_of(offset)] & 3

    own = flags[x]
    values = [c[x, i] for i in range(19)]
    j = []
    for axis in range(3):
        plus = sum(values[i] for i in range(19) if VELOCITY[i][axis] > 0)
        minus = sum(values[i] for i in range(19) if VELOCITY[i][axis] < 0)
        j.append(plus - minus)
    calm = 1.0 - 1.5 * (j[0] * j[0] + j[1] * j[1] + j[2] * j[2])
    inlet_square = sum(p * p for p in INLET_SPEED)
    out = [jnp.where(own == 0, values[0], 0.0)]
    for i in range(1, 19):
        cx, cy, cz = VELOCITY[i]
        if cx:
            outside = x == (0 if cx > 0 else EDGE - 1)
            from_x = jnp.clip(x - cx, 0, EDGE - 1)
            kx = (X_PLUS if cx > 0 else X_MINUS).index(i)
            v = jnp.where(outside, rxy[jx, kx], c[from_x, i])
            kind = jnp.where(outside, wall((-cx, 0, 0)), flags[from_x])
        else:
            v, kind = values[i], own
        if cz:
            beyond = rb if cz > 0 else ra
            kz = (Z_PLUS if cz > 0 else Z_MINUS).index(i)
            block, blocked = spot((0, 0, -cz)), wall((0, 0, -cz))
            at = x
            if cx:
                block = jnp.where(outside, spot((-cx, 0, -cz)), block)
                blocked = jnp.where(outside, wall((-cx, 0, -cz)), blocked)
                at = (x - cx) & 31
            message = beyond[block, kz]
            amount = (128 - at) & 127 if cz > 0 else 31 - at
            v = shift_z(v, cz, pltpu.roll(message, amount, 1), z)
            kind = shift_z(kind, cz, blocked, z)
        if cy:
            ky = (Y_PLUS if cy > 0 else Y_MINUS).index(i)
            row = jnp.broadcast_to(gy[ky, pl.ds(x - cx + 1, 1), :], (8, 128))
            blocked = wall((0, -cy, 0))
            if cx:
                blocked = jnp.where(outside, wall((-cx, -cy, 0)), blocked)
            if cz:
                corner = beyond[spot((0, -cy, -cz)), kz]
                target = (0 if cy > 0 else 96) + (0 if cz > 0 else 31)
                source = (96 if cy > 0 else 0) + x
                corner = pltpu.roll(corner, (target - source + 256) & 127, 1)
                corner = corner[7:8, :] if cy > 0 else corner[0:1, :]
                row = shift_z(row, cz, jnp.broadcast_to(corner, (8, 128)), z)
                blocked = jnp.where(z == (0 if cz > 0 else 31), wall((0, -cy, -cz)), blocked)
            v = shift_y(v, cy, row, lane, sub)
            kind = shift_y(kind, cy, blocked, lane, sub)
        weight = WEIGHT_LIST[i]
        along = sum(a * b for a, b in zip(VELOCITY[i], INLET_SPEED))
        inlet = weight * (1.0 + 3.0 * along + 4.5 * along * along - 1.5 * inlet_square)
        speed = sum(a * b for a, b in zip(VELOCITY[i], j) if a)
        outlet = weight * (calm + speed * (3.0 + 4.5 * speed))
        new = jnp.where(
            kind == 0,
            v,
            jnp.where(kind == 1, values[opposite(i)], jnp.where(kind == 2, np.float32(inlet), outlet)),
        )
        out.append(jnp.where(own == 0, new, 0.0))
    return out


def note_faces(x, nbr, collided, zu, zd, rows):
    lane, _ = positions()
    here = (lane & 31) == x
    for k in range(5):
        up = pltpu.roll(collided[Z_PLUS[k]], (x + 97) & 127, 1)
        zu[k] = jnp.where(here, up, zu[k])
        zd[k] = jnp.where(here, pltpu.roll(collided[Z_MINUS[k]], x, 1), zd[k])
        high = collided[Y_PLUS[k]][7:8, :]
        low = collided[Y_MINUS[k]][0:1, :]
        rows[k, pl.ds(x, 1), :] = jnp.where(nbr[0, 2] >= 0, high, low)


def finish_faces(nbr, c, rows, xy):
    lane, _ = positions()
    ahead_x, ahead_y = nbr[0, 0] >= 0, nbr[0, 2] >= 0
    for k in range(5):
        xy[k] = jnp.where(ahead_x, c[EDGE - 1, X_PLUS[k]], c[0, X_MINUS[k]])
        packed = jnp.zeros((8, 128), jnp.float32)
        for g in range(4):
            part = rows[k, 8 * g : 8 * g + 8, :]
            high = pltpu.roll(part, (32 * (g + 1)) % 128, 1)
            low = pltpu.roll(part, 32 * g, 1)
            packed = jnp.where((lane >> 5) == g, jnp.where(ahead_y, high, low), packed)
        xy[5 + k] = packed


def first_kernel(nbr, f, c, xy, zu, zd, rows):
    zu[...] = jnp.zeros_like(zu)
    zd[...] = jnp.zeros_like(zd)

    def plane(x, carry):
        collided = collide([f[x, i] for i in range(19)])
        for i in range(19):
            c[x, i] = collided[i]
        note_faces(x, nbr, collided, zu, zd, rows)
        return carry

    lax.fori_loop(0, EDGE, plane, 0)
    finish_faces(nbr, c, rows, xy)


def middle_kernel(nbr, flags, c_in, rxy, rb, ra, c, xy, zu, zd, rows, gy):
    zu[...] = jnp.zeros_like(zu)
    zd[...] = jnp.zeros_like(zd)
    unpack_ghosts(nbr, rxy, gy)

    def plane(x, carry):
        collided = collide(pull(x, nbr, c_in, rxy, rb, ra, flags, gy))
        for i in range(19):
            c[x, i] = collided[i]
        note_faces(x, nbr, collided, zu, zd, rows)
        return carry

    lax.fori_loop(0, EDGE, plane, 0)
    finish_faces(nbr, c, rows, xy)


def last_kernel(nbr, flags, c_in, rxy, rb, ra, out, gy, lines):
    unpack_ghosts(nbr, rxy, gy)

    def plane(x, carry):
        f = pull(x, nbr, c_in, rxy, rb, ra, flags, gy)
        for i in range(19):
            lines[8 * i : 8 * i + 8, :] = f[i]
        for s in range(8):
            at = pl.multiple_of(x * 1024 + s * 128, 128)
            out[0, :, pl.ds(at, 128)] = lines[pl.ds(s, 19, stride=8), :]
        return carry

    lax.fori_loop(0, EDGE, plane, 0)


def spread_kernel(planes, slots, old, out):
    def plane(x, carry):
        for slot in range(slots):
            for s in range(8):
                at = pl.multiple_of(x * 1024 + s * 128, 128)
                out[x, pl.ds(slot * 152 + s, 19, stride=8), :] = old[slot, :, pl.ds(at, 128)]
        return carry

    lax.fori_loop(0, planes, plane, 0)


def exchange_kernel(layers, xy, zu, zd, rxy, rb, ra, send_sem, recv_sem):
    me = lax.axis_index("blocks")
    layer, place = me // 4, me % 4
    above, below = layer + 1 < layers, layer > 0
    barrier = pltpu.get_barrier_semaphore()

    def greet(first, k):
        pl.semaphore_signal(
            barrier, inc=1, device_id=(first * 4 + (place + k) % 4,), device_id_type=MESH
        )

    for k in range(1, 4):
        greet(layer, k)

    @pl.when(above)
    def _():
        for k in range(4):
            greet(layer + 1, k)

    @pl.when(below)
    def _():
        for k in range(4):
            greet(layer - 1, k)

    peers = 3 + 4 * above.astype(jnp.int32) + 4 * below.astype(jnp.int32)
    pl.semaphore_wait(barrier, peers)

    def copy(source, target, spot, number, first, k):
        return pltpu.make_async_remote_copy(
            src_ref=source,
            dst_ref=target.at[spot],
            send_sem=send_sem.at[number],
            recv_sem=recv_sem.at[number],
            device_id=(first * 4 + (place + k) % 4,),
            device_id_type=MESH,
        )

    @pl.when(above)
    def _():
        for k in range(4):
            copy(zu, rb, place, 3 + k, layer + 1, k).start()

    @pl.when(below)
    def _():
        for k in range(4):
            copy(zd, ra, place, 7 + k, layer - 1, k).start()

    for k in range(1, 4):
        copy(xy, rxy, place, k - 1, layer, k).start()
    for k in range(1, 4):
        copy(xy, rxy, (place + 4 - k) % 4, k - 1, layer, k).wait_recv()

    @pl.when(below)
    def _():
        for k in range(4):
            copy(zu, rb, (place + 4 - k) % 4, 3 + k, layer - 1, k).wait_recv()

    @pl.when(above)
    def _():
        for k in range(4):
            copy(zd, ra, (place + 4 - k) % 4, 7 + k, layer + 1, k).wait_recv()

    @pl.when(above)
    def _():
        for k in range(4):
            copy(zu, rb, place, 3 + k, layer + 1, k).wait_send()

    @pl.when(below)
    def _():
        for k in range(4):
            copy(zd, ra, place, 7 + k, layer - 1, k).wait_send()

    for k in range(1, 4):
        copy(xy, rxy, place, k - 1, layer, k).wait_send()


VMEM = pl.BlockSpec(memory_space=pltpu.VMEM)
SMEM = pl.BlockSpec(memory_space=pltpu.SMEM)
FACE = jax.ShapeDtypeStruct((5, 8, 128), jnp.float32)
FACES = jax.ShapeDtypeStruct((10, 8, 128), jnp.float32)
STATE = jax.ShapeDtypeStruct((EDGE, 19, 8, 128), jnp.float32)
ROWS = pltpu.VMEM((5, EDGE, 128), jnp.float32)
GHOSTS = pltpu.VMEM((5, EDGE + 8, 128), jnp.float32)
LIMIT = pltpu.CompilerParams(vmem_limit_bytes=40 * 2**20)


def exchange(xy, zu, zd):
    layers = lax.axis_size("blocks") // 4
    return pl.pallas_call(
        functools.partial(exchange_kernel, layers),
        out_shape=[
            jax.ShapeDtypeStruct((4, 10, 8, 128), jnp.float32),
            jax.ShapeDtypeStruct((4, 5, 8, 128), jnp.float32),
            jax.ShapeDtypeStruct((4, 5, 8, 128), jnp.float32),
        ],
        in_specs=[VMEM] * 3,
        out_specs=[VMEM] * 3,
        scratch_shapes=[pltpu.SemaphoreType.DMA((11,)), pltpu.SemaphoreType.DMA((11,))],
        compiler_params=pltpu.CompilerParams(collective_id=0, has_side_effects=True),
    )(xy, zu, zd)


def migrate(old_pdfs, old_slot):
    peers = lax.axis_size("blocks")
    slots = old_pdfs.shape[0]
    blocks = old_slot.shape[0]
    planes = 4
    tiles = pl.pallas_call(
        functools.partial(spread_kernel, planes, slots),
        grid=(EDGE // planes,),
        out_shape=jax.ShapeDtypeStruct((EDGE, slots * 152, 128), jnp.float32),
        in_specs=[pl.BlockSpec((slots, 19, planes * 1024), lambda g: (0, 0, g))],
        out_specs=pl.BlockSpec((planes, slots * 152, 128), lambda g: (g, 0, 0)),
        compiler_params=LIMIT,
    )(old_pdfs)
    parts = peers // EDGE
    rows = 8 // parts
    if parts > 1:
        tiles = tiles.reshape(EDGE, slots * 19, parts, rows, 128).transpose(0, 2, 1, 3, 4)
        tiles = tiles.reshape(peers, slots * 19 * rows, 128)
    spread = lax.all_to_all(tiles, "blocks", split_axis=0, concat_axis=0, tiled=True)
    spread = spread.reshape(peers * slots, 19 * rows, 128)
    ordered = spread.at[old_slot].get(mode="promise_in_bounds")
    arrived = lax.all_to_all(ordered, "blocks", split_axis=0, concat_axis=0, tiled=True)
    if parts > 1:
        arrived = arrived.reshape(EDGE, parts, 19, rows, 128).transpose(0, 2, 1, 3, 4)
    return arrived.reshape(EDGE, 19, 8, 128)


def per_device(old_pdfs, old_slot, neighbours, cell_flags):
    state = migrate(old_pdfs, old_slot)
    flags = cell_flags.reshape(EDGE, 8, 128)
    c, xy, zu, zd = pl.pallas_call(
        first_kernel,
        out_shape=[STATE, FACES, FACE, FACE],
        in_specs=[SMEM, VMEM],
        out_specs=[VMEM] * 4,
        scratch_shapes=[ROWS],
        compiler_params=LIMIT,
    )(neighbours, state)
    for _ in range(STEPS - 1):
        rxy, rb, ra = exchange(xy, zu, zd)
        c, xy, zu, zd = pl.pallas_call(
            middle_kernel,
            out_shape=[STATE, FACES, FACE, FACE],
            in_specs=[SMEM] + [VMEM] * 5,
            out_specs=[VMEM] * 4,
            scratch_shapes=[ROWS, GHOSTS],
            compiler_params=LIMIT,
        )(neighbours, flags, c, rxy, rb, ra)
    rxy, rb, ra = exchange(xy, zu, zd)
    return pl.pallas_call(
        last_kernel,
        out_shape=jax.ShapeDtypeStruct((1, 19, EDGE * EDGE * EDGE), jnp.float32),
        in_specs=[SMEM] + [VMEM] * 5,
        out_specs=VMEM,
        scratch_shapes=[GHOSTS, pltpu.VMEM((152, 128), jnp.float32)],
        compiler_params=LIMIT,
    )(neighbours, flags, c, rxy, rb, ra)


def solution(mesh):
    in_specs = (P("blocks", None, None), P(), P("blocks", None), P("blocks", None))
    out_specs = P("blocks", None, None)
    return jax.shard_map(
        per_device, mesh=mesh, in_specs=in_specs, out_specs=out_specs, check_vma=False
    )
```

```python
import functools

import jax
import jax.numpy as jnp
import numpy as np
from jax import lax
from jax.experimental import pallas as pl
from jax.experimental.pallas import tpu as pltpu
from jax.sharding import PartitionSpec as P

EDGE = 32
STEPS = 2
MESH = pl.DeviceIdType.MESH

VELOCITY = (
    (0, 0, 0),
    (1, 0, 0),
    (-1, 0, 0),
    (0, 1, 0),
    (0, -1, 0),
    (0, 0, 1),
    (0, 0, -1),
    (1, 1, 0),
    (-1, -1, 0),
    (1, -1, 0),
    (-1, 1, 0),
    (1, 0, 1),
    (-1, 0, -1),
    (1, 0, -1),
    (-1, 0, 1),
    (0, 1, 1),
    (0, -1, -1),
    (0, 1, -1),
    (0, -1, 1),
)
WEIGHT_LIST = (1.0 / 3.0,) + (1.0 / 18.0,) * 6 + (1.0 / 36.0,) * 12
RELAXATION = (
    0.0,
    0.0,
    0.0,
    0.0,
    1.19,
    1.4,
    1.2,
    1.2,
    1.2,
    1.6,
    1.6,
    1.6,
    1.6,
    1.6,
    1.4,
    1.4,
    1.98,
    1.98,
    1.98,
)
INLET_SPEED = (0.0, 0.0, 0.05)

X_PLUS, X_MINUS = (1, 7, 9, 11, 13), (2, 8, 10, 12, 14)
Y_PLUS, Y_MINUS = (3, 7, 10, 15, 17), (4, 8, 9, 16, 18)
Z_PLUS, Z_MINUS = (5, 11, 14, 15, 18), (6, 12, 13, 16, 17)
ORBITS = ((0,), (1, 2), (3, 4), (5, 6), (7, 8, 9, 10), (11, 12, 13, 14), (15, 16, 17, 18))


def collision_table():
    lattice = np.array(VELOCITY) * 1.0
    along_x, along_y, along_z = (lattice[:, 0], lattice[:, 1], lattice[:, 2])
    squared = along_x * along_x + along_y * along_y + along_z * along_z
    monomials = [
        np.ones(19),
        along_x,
        along_y,
        along_z,
        squared,
        squared * squared,
        squared * along_x,
        squared * along_y,
        squared * along_z,
        3.0 * along_x * along_x - squared,
        along_y * along_y - along_z * along_z,
        along_x * along_y,
        along_y * along_z,
        along_x * along_z,
        squared * (3.0 * along_x * along_x - squared),
        squared * (along_y * along_y - along_z * along_z),
        (along_y * along_y - along_z * along_z) * along_x,
        (along_z * along_z - along_x * along_x) * along_y,
        (along_x * along_x - along_y * along_y) * along_z,
    ]
    orthonormal = []
    for vector in monomials:
        for earlier in orthonormal:
            vector = vector - np.dot(vector, earlier) * earlier
        orthonormal.append(vector / np.sqrt(np.dot(vector, vector)))
    stacked = np.stack(orthonormal)
    return stacked.T * np.array(RELAXATION) @ stacked


def opposite(index_value):
    if index_value == 0:
        return 0
    return index_value + 1 if index_value % 2 == 1 else index_value - 1


def code_of(offset):
    return VELOCITY.index(tuple(offset)) - 1


def collision_blocks():
    matrix = collision_table().astype(np.float32).astype(np.float64)
    even = [[float(np.mean([matrix[a[0], b] for b in group])) for group in ORBITS] for a in ORBITS]
    odd = []
    for axis in range(3):
        groups = [g for g in ORBITS if any(VELOCITY[b][axis] for b in g)]
        rows = []
        for a in groups:
            first = next(c for c in a if VELOCITY[c][axis] > 0)
            rows.append(
                [float(np.mean([VELOCITY[b][axis] * matrix[first, b] for b in g])) for g in groups]
            )
        odd.append(rows)
    mixed = []
    for group in ORBITS[4:]:
        signs = [1.0, 1.0, -1.0, -1.0]
        mixed.append(float(np.mean([s * matrix[group[0], b] for s, b in zip(signs, group)])))
    return even, odd, mixed


def dot(coefficients, terms):
    total = None
    for coefficient, term in zip(coefficients, terms):
        part = term * np.float32(coefficient)
        total = part if total is None else total + part
    return total


def collide(f):
    even, odd, mixed = collision_blocks()
    pair_sum = [f[i] + f[i + 1] for i in (1, 3, 5)]
    pair_dif = [f[i] - f[i + 1] for i in (1, 3, 5)]
    quad_sum, quad_mix, quad_one, quad_two = [], [], [], []
    for i in (7, 11, 15):
        sum_a, sum_b = f[i] + f[i + 1], f[i + 2] + f[i + 3]
        dif_a, dif_b = f[i] - f[i + 1], f[i + 2] - f[i + 3]
        quad_sum.append(sum_a + sum_b)
        quad_mix.append(sum_a - sum_b)
        quad_one.append(dif_a + dif_b)
        quad_two.append(dif_a - dif_b)
    odd_terms = [
        [pair_dif[0], quad_one[0], quad_one[1]],
        [pair_dif[1], quad_two[0], quad_one[2]],
        [pair_dif[2], quad_two[1], quad_two[2]],
    ]
    rho = f[0] + (pair_sum[0] + pair_sum[1] + pair_sum[2]) + (quad_sum[0] + quad_sum[1] + quad_sum[2])
    j = [t[0] + t[1] + t[2] for t in odd_terms]
    sq = [c * c for c in j]
    base = rho - 1.5 * (sq[0] + sq[1] + sq[2])
    sq45 = [4.5 * s for s in sq]
    w0, w1, w2 = 1.0 / 3.0, 1.0 / 18.0, 1.0 / 36.0
    even_terms = [f[0] - w0 * base]
    for a in range(3):
        even_terms.append(pair_sum[a] - (2.0 * w1) * (base + sq45[a]))
    for q, (a, b) in enumerate(((0, 1), (0, 2), (1, 2))):
        even_terms.append(quad_sum[q] - (4.0 * w2) * (base + sq45[a] + sq45[b]))
    mix = [
        (quad_mix[q] - j[a] * j[b]) * np.float32(mixed[q])
        for q, (a, b) in enumerate(((0, 1), (0, 2), (1, 2)))
    ]
    odd_out = []
    for a in range(3):
        third = j[a] * np.float32(1.0 / 3.0)
        terms = [t - third for t in odd_terms[a]]
        odd_out.append([dot(row, terms) for row in odd[a]])
    even_out = [dot(row, even_terms) for row in even]
    out = [f[0] - even_out[0]]
    for a in range(3):
        out.append(f[1 + 2 * a] - (even_out[1 + a] + odd_out[a][0]))
        out.append(f[2 + 2 * a] - (even_out[1 + a] - odd_out[a][0]))
    for q, (one, two) in enumerate(
        (
            (odd_out[0][1], odd_out[1][1]),
            (odd_out[0][2], odd_out[2][1]),
            (odd_out[1][2], odd_out[2][2]),
        )
    ):
        i = 7 + 4 * q
        plus, minus = even_out[4 + q] + mix[q], even_out[4 + q] - mix[q]
        both, apart = one + two, one - two
        out.append(f[i] - (plus + both))
        out.append(f[i + 1] - (plus - both))
        out.append(f[i + 2] - (minus + apart))
        out.append(f[i + 3] - (minus - apart))
    return out


def positions():
    lane = lax.broadcasted_iota(jnp.int32, (8, 128), 1)
    sub = lax.broadcasted_iota(jnp.int32, (8, 128), 0)
    return lane, sub


def shift_y(v, step, ghost, lane, sub):
    if step > 0:
        moved = pltpu.roll(v, 32, 1)
        out = jnp.where(lane < 32, pltpu.roll(moved, 1, 0), moved)
        return jnp.where((lane < 32) & (sub == 0), ghost, out)
    moved = pltpu.roll(v, 96, 1)
    out = jnp.where(lane >= 96, pltpu.roll(moved, 7, 0), moved)
    return jnp.where((lane >= 96) & (sub == 7), ghost, out)


def shift_z(v, step, ghost, z):
    moved = pltpu.roll(v, 1 if step > 0 else 127, 1)
    return jnp.where(z == (0 if step > 0 else 31), ghost, moved)


def unpack_ghosts(nbr, rxy, gy):
    lane, _ = positions()
    jy = jnp.maximum(nbr[0, 2], nbr[0, 3]) & 3
    jd = jnp.maximum(jnp.maximum(nbr[0, 6], nbr[0, 7]), jnp.maximum(nbr[0, 8], nbr[0, 9])) & 3
    for k in range(5):
        packed = rxy[jy, 5 + k]
        for g in range(4):
            low = pltpu.roll(packed, (128 - 32 * g) % 128, 1)
            high = pltpu.roll(packed, (96 - 32 * g) % 128, 1)
            gy[k, 1 + 8 * g : 9 + 8 * g, :] = jnp.where(lane < 64, low, high)
    for channel in (7, 8, 9, 10):
        cx, cy, _ = VELOCITY[channel]
        kx = (X_PLUS if cx > 0 else X_MINUS).index(channel)
        ky = (Y_PLUS if cy > 0 else Y_MINUS).index(channel)
        plane = rxy[jd, kx]
        row = pltpu.roll(plane, 32 if cy > 0 else 96, 1)
        row = row[7:8, :] if cy > 0 else row[0:1, :]
        spot = 0 if cx > 0 else 33
        gy[ky, spot : spot + 1, :] = row


def pull(x, nbr, c, rxy, rb, ra, flags, gy):
    lane, sub = positions()
    z = lane & 31
    jx = jnp.maximum(nbr[0, 0], nbr[0, 1]) & 3

    def wall(offset):
        return jnp.where(nbr[0, code_of(offset)] >= 0, 0, 1).astype(jnp.int32)

    def spot(offset):
        return nbr[0, code_of(offset)] & 3

    own = flags[x]
    values = [c[x, i] for i in range(19)]
    j = []
    for axis in range(3):
        plus = sum(values[i] for i in range(19) if VELOCITY[i][axis] > 0)
        minus = sum(values[i] for i in range(19) if VELOCITY[i][axis] < 0)
        j.append(plus - minus)
    calm = 1.0 - 1.5 * (j[0] * j[0] + j[1] * j[1] + j[2] * j[2])
    inlet_square = sum(p * p for p in INLET_SPEED)
    out = [jnp.where(own == 0, values[0], 0.0)]
    for i in range(1, 19):
        cx, cy, cz = VELOCITY[i]
        if cx:
            outside = x == (0 if cx > 0 else EDGE - 1)
            from_x = jnp.clip(x - cx, 0, EDGE - 1)
            kx = (X_PLUS if cx > 0 else X_MINUS).index(i)
            v = jnp.where(outside, rxy[jx, kx], c[from_x, i])
            kind = jnp.where(outside, wall((-cx, 0, 0)), flags[from_x])
        else:
            v, kind = values[i], own
        if cz:
            beyond = rb if cz > 0 else ra
            kz = (Z_PLUS if cz > 0 else Z_MINUS).index(i)
            block, blocked = spot((0, 0, -cz)), wall((0, 0, -cz))
            at = x
            if cx:
                block = jnp.where(outside, spot((-cx, 0, -cz)), block)
                blocked = jnp.where(outside, wall((-cx, 0, -cz)), blocked)
                at = (x - cx) & 31
            message = beyond[block, kz]
            amount = (128 - at) & 127 if cz > 0 else 31 - at
            v = shift_z(v, cz, pltpu.roll(message, amount, 1), z)
            kind = shift_z(kind, cz, blocked, z)
        if cy:
            ky = (Y_PLUS if cy > 0 else Y_MINUS).index(i)
            row = jnp.broadcast_to(gy[ky, pl.ds(x - cx + 1, 1), :], (8, 128))
            blocked = wall((0, -cy, 0))
            if cx:
                blocked = jnp.where(outside, wall((-cx, -cy, 0)), blocked)
            if cz:
                corner = beyond[spot((0, -cy, -cz)), kz]
                target = (0 if cy > 0 else 96) + (0 if cz > 0 else 31)
                source = (96 if cy > 0 else 0) + x
                corner = pltpu.roll(corner, (target - source + 256) & 127, 1)
                corner = corner[7:8, :] if cy > 0 else corner[0:1, :]
                row = shift_z(row, cz, jnp.broadcast_to(corner, (8, 128)), z)
                blocked = jnp.where(z == (0 if cz > 0 else 31), wall((0, -cy, -cz)), blocked)
            v = shift_y(v, cy, row, lane, sub)
            kind = shift_y(kind, cy, blocked, lane, sub)
        weight = WEIGHT_LIST[i]
        along = sum(a * b for a, b in zip(VELOCITY[i], INLET_SPEED))
        inlet = weight * (1.0 + 3.0 * along + 4.5 * along * along - 1.5 * inlet_square)
        speed = sum(a * b for a, b in zip(VELOCITY[i], j) if a)
        outlet = weight * (calm + speed * (3.0 + 4.5 * speed))
        new = jnp.where(
            kind == 0,
            v,
            jnp.where(kind == 1, values[opposite(i)], jnp.where(kind == 2, np.float32(inlet), outlet)),
        )
        out.append(jnp.where(own == 0, new, 0.0))
    return out


def note_faces(x, nbr, collided, zu, zd, rows):
    lane, _ = positions()
    here = (lane & 31) == x
    for k in range(5):
        up = pltpu.roll(collided[Z_PLUS[k]], (x + 97) & 127, 1)
        zu[k] = jnp.where(here, up, zu[k])
        zd[k] = jnp.where(here, pltpu.roll(collided[Z_MINUS[k]], x, 1), zd[k])
        high = collided[Y_PLUS[k]][7:8, :]
        low = collided[Y_MINUS[k]][0:1, :]
        rows[k, pl.ds(x, 1), :] = jnp.where(nbr[0, 2] >= 0, high, low)


def finish_faces(nbr, c, rows, xy):
    lane, _ = positions()
    ahead_x, ahead_y = nbr[0, 0] >= 0, nbr[0, 2] >= 0
    for k in range(5):
        xy[k] = jnp.where(ahead_x, c[EDGE - 1, X_PLUS[k]], c[0, X_MINUS[k]])
        packed = jnp.zeros((8, 128), jnp.float32)
        for g in range(4):
            part = rows[k, 8 * g : 8 * g + 8, :]
            high = pltpu.roll(part, (32 * (g + 1)) % 128, 1)
            low = pltpu.roll(part, 32 * g, 1)
            packed = jnp.where((lane >> 5) == g, jnp.where(ahead_y, high, low), packed)
        xy[5 + k] = packed


def first_kernel(nbr, f, c, xy, zu, zd, rows):
    zu[...] = jnp.zeros_like(zu)
    zd[...] = jnp.zeros_like(zd)

    def plane(x, carry):
        collided = collide([f[x, i] for i in range(19)])
        for i in range(19):
            c[x, i] = collided[i]
        note_faces(x, nbr, collided, zu, zd, rows)
        return carry

    lax.fori_loop(0, EDGE, plane, 0)
    finish_faces(nbr, c, rows, xy)


def middle_kernel(nbr, flags, c_in, rxy, rb, ra, c, xy, zu, zd, rows, gy):
    zu[...] = jnp.zeros_like(zu)
    zd[...] = jnp.zeros_like(zd)
    unpack_ghosts(nbr, rxy, gy)

    def plane(x, carry):
        collided = collide(pull(x, nbr, c_in, rxy, rb, ra, flags, gy))
        for i in range(19):
            c[x, i] = collided[i]
        note_faces(x, nbr, collided, zu, zd, rows)
        return carry

    lax.fori_loop(0, EDGE, plane, 0)
    finish_faces(nbr, c, rows, xy)


def last_kernel(nbr, flags, c_in, rxy, rb, ra, out, gy, lines):
    unpack_ghosts(nbr, rxy, gy)

    def plane(x, carry):
        f = pull(x, nbr, c_in, rxy, rb, ra, flags, gy)
        for i in range(19):
            lines[8 * i : 8 * i + 8, :] = f[i]
        for s in range(8):
            at = pl.multiple_of(x * 1024 + s * 128, 128)
            out[0, :, pl.ds(at, 128)] = lines[pl.ds(s, 19, stride=8), :]
        return carry

    lax.fori_loop(0, EDGE, plane, 0)


def spread_kernel(planes, slots, old, out):
    def plane(x, carry):
        for slot in range(slots):
            for s in range(8):
                at = pl.multiple_of(x * 1024 + s * 128, 128)
                out[x, pl.ds(slot * 152 + s, 19, stride=8), :] = old[slot, :, pl.ds(at, 128)]
        return carry

    lax.fori_loop(0, planes, plane, 0)


def exchange_kernel(layers, xy, zu, zd, rxy, rb, ra, send_sem, recv_sem):
    me = lax.axis_index("blocks")
    layer, place = me // 4, me % 4
    above, below = layer + 1 < layers, layer > 0
    barrier = pltpu.get_barrier_semaphore()

    def greet(first, k):
        pl.semaphore_signal(
            barrier, inc=1, device_id=(first * 4 + (place + k) % 4,), device_id_type=MESH
        )

    for k in range(1, 4):
        greet(layer, k)

    @pl.when(above)
    def _():
        for k in range(4):
            greet(layer + 1, k)

    @pl.when(below)
    def _():
        for k in range(4):
            greet(layer - 1, k)

    peers = 3 + 4 * above.astype(jnp.int32) + 4 * below.astype(jnp.int32)
    pl.semaphore_wait(barrier, peers)

    def copy(source, target, spot, number, first, k):
        return pltpu.make_async_remote_copy(
            src_ref=source,
            dst_ref=target.at[spot],
            send_sem=send_sem.at[number],
            recv_sem=recv_sem.at[number],
            device_id=(first * 4 + (place + k) % 4,),
            device_id_type=MESH,
        )

    @pl.when(above)
    def _():
        for k in range(4):
            copy(zu, rb, place, 3 + k, layer + 1, k).start()

    @pl.when(below)
    def _():
        for k in range(4):
            copy(zd, ra, place, 7 + k, layer - 1, k).start()

    for k in range(1, 4):
        copy(xy, rxy, place, k - 1, layer, k).start()
    for k in range(1, 4):
        copy(xy, rxy, (place + 4 - k) % 4, k - 1, layer, k).wait_recv()

    @pl.when(below)
    def _():
        for k in range(4):
            copy(zu, rb, (place + 4 - k) % 4, 3 + k, layer - 1, k).wait_recv()

    @pl.when(above)
    def _():
        for k in range(4):
            copy(zd, ra, (place + 4 - k) % 4, 7 + k, layer + 1, k).wait_recv()

    @pl.when(above)
    def _():
        for k in range(4):
            copy(zu, rb, place, 3 + k, layer + 1, k).wait_send()

    @pl.when(below)
    def _():
        for k in range(4):
            copy(zd, ra, place, 7 + k, layer - 1, k).wait_send()

    for k in range(1, 4):
        copy(xy, rxy, place, k - 1, layer, k).wait_send()


VMEM = pl.BlockSpec(memory_space=pltpu.VMEM)
SMEM = pl.BlockSpec(memory_space=pltpu.SMEM)
FACE = jax.ShapeDtypeStruct((5, 8, 128), jnp.float32)
FACES = jax.ShapeDtypeStruct((10, 8, 128), jnp.float32)
STATE = jax.ShapeDtypeStruct((EDGE, 19, 8, 128), jnp.float32)
ROWS = pltpu.VMEM((5, EDGE, 128), jnp.float32)
GHOSTS = pltpu.VMEM((5, EDGE + 8, 128), jnp.float32)
LIMIT = pltpu.CompilerParams(vmem_limit_bytes=40 * 2**20)


def exchange(xy, zu, zd):
    layers = lax.axis_size("blocks") // 4
    return pl.pallas_call(
        functools.partial(exchange_kernel, layers),
        out_shape=[
            jax.ShapeDtypeStruct((4, 10, 8, 128), jnp.float32),
            jax.ShapeDtypeStruct((4, 5, 8, 128), jnp.float32),
            jax.ShapeDtypeStruct((4, 5, 8, 128), jnp.float32),
        ],
        in_specs=[VMEM] * 3,
        out_specs=[VMEM] * 3,
        scratch_shapes=[pltpu.SemaphoreType.DMA((11,)), pltpu.SemaphoreType.DMA((11,))],
        compiler_params=pltpu.CompilerParams(collective_id=0, has_side_effects=True),
    )(xy, zu, zd)


CHUNKS = ((0, 0, 10), (1, 0, 10), (0, 10, 19), (1, 10, 19))
CAPACITIES = (10, 12, 16)


def migrate_kernel(room, plan, tiles, out, *scratch):
    parts = len(CHUNKS)
    held, wanted, given, sorted_ = (scratch[parts * n : parts * n + parts] for n in range(4))
    own_sem, send_one, recv_one, send_two, recv_two, send_three, recv_three = scratch[4 * parts :]
    me = lax.axis_index("blocks")
    half, place = me // 16, me % 16
    partner = (1 - half) * 16 + place

    def peer(d):
        return (place + d) % 16

    def device(d):
        return (half * 16 + peer(d),)

    barrier = pltpu.get_barrier_semaphore()

    def greet(d, carry):
        pl.semaphore_signal(barrier, inc=1, device_id=device(d), device_id_type=MESH)
        return carry

    lax.fori_loop(1, 16, greet, 0)
    pl.semaphore_signal(barrier, inc=1, device_id=(partner,), device_id_type=MESH)
    pl.semaphore_wait(barrier, 16)

    def spread(k, d, owner):
        plane, low, high = CHUNKS[k]
        return pltpu.make_async_remote_copy(
            src_ref=tiles.at[2 * peer(d) + plane, :, low:high],
            dst_ref=held[k].at[pl.ds(2 * owner, 2)],
            send_sem=send_one.at[k, d],
            recv_sem=recv_one.at[k, d],
            device_id=device(d),
            device_id_type=MESH,
        )

    def keep(k):
        plane, low, high = CHUNKS[k]
        return pltpu.make_async_copy(
            tiles.at[2 * place + plane, :, low:high], held[k].at[pl.ds(2 * place, 2)], own_sem.at[k]
        )

    def swap(k):
        return pltpu.make_async_remote_copy(
            src_ref=wanted[k],
            dst_ref=given[k],
            send_sem=send_two.at[k],
            recv_sem=recv_two.at[k],
            device_id=(partner,),
            device_id_type=MESH,
        )

    def hand(k, d, owner):
        plane, low, high = CHUNKS[k]
        return pltpu.make_async_remote_copy(
            src_ref=sorted_[k].at[peer(d)],
            dst_ref=out.at[2 * owner + plane, low:high],
            send_sem=send_three.at[k, d],
            recv_sem=recv_three.at[k, d],
            device_id=device(d),
            device_id_type=MESH,
        )

    def each(body):
        def step(d, carry):
            body(d)
            return carry

        lax.fori_loop(1, 16, step, 0)

    def deliver(k):
        plane, low, high = CHUNKS[k]
        swap(k).wait_recv()

        def choose(b, carry):
            near, far = held[k][plan[2, b]], given[k][plan[3, b]]
            sorted_[k][b] = jnp.where(plan[1, b] > 0, near, far)
            return carry

        lax.fori_loop(0, 16, choose, 0)
        each(lambda d: hand(k, d, place).start())
        out[2 * place + plane, low:high] = sorted_[k][place]

    for k in range(parts):
        keep(k).start()
        each(lambda d: spread(k, d, place).start())
    for k in range(parts):
        keep(k).wait()
        each(lambda d: spread(k, d, peer(16 - d)).wait_recv())

        def pick(e, carry):
            wanted[k][e] = held[k][plan[0, e]]
            return carry

        lax.fori_loop(0, room, pick, 0)
        swap(k).start()
        if k > 0:
            deliver(k - 1)
    deliver(parts - 1)
    for k in range(parts):
        each(lambda d: hand(k, d, peer(16 - d)).wait_recv())
    for k in range(parts):
        each(lambda d: spread(k, d, place).wait_send())
        swap(k).wait_send()
        each(lambda d: hand(k, d, place).wait_send())


def migrate_with(room, number, plan, tiles):
    parts = len(CHUNKS)

    def buffers(count):
        return [pltpu.VMEM((count, high - low, 8, 128), jnp.float32) for _, low, high in CHUNKS]

    dma = pltpu.SemaphoreType.DMA
    return pl.pallas_call(
        functools.partial(migrate_kernel, room),
        out_shape=STATE,
        in_specs=[SMEM, VMEM],
        out_specs=VMEM,
        scratch_shapes=buffers(32)
        + buffers(room)
        + buffers(room)
        + buffers(16)
        + [dma((parts,)), dma((parts, 16)), dma((parts, 16)), dma((parts,)), dma((parts,))]
        + [dma((parts, 16)), dma((parts, 16))],
        compiler_params=pltpu.CompilerParams(
            collective_id=number, has_side_effects=True, vmem_limit_bytes=40 * 2**20
        ),
    )(plan, tiles)


def migration_plan(old_slot):
    half = lax.axis_index("blocks") // 16
    block = jnp.arange(32, dtype=jnp.int32)
    from_half, to_half = old_slot // 32, block // 16
    crosses = from_half != to_half
    same = (to_half[None, :] == to_half[:, None]) & (block[None, :] < block[:, None])
    rank = jnp.sum((same & crosses[None, :]).astype(jnp.int32), axis=1)
    leaves = crosses & (from_half == half)
    entry = jnp.arange(16, dtype=jnp.int32)
    chosen = leaves[None, :] & (rank[None, :] == entry[:, None])
    local = old_slot % 32
    wanted = jnp.sum(jnp.where(chosen, local[None, :], 0), axis=1)
    mine = lax.dynamic_slice_in_dim(jnp.stack([1 - crosses.astype(jnp.int32), local, rank]), half * 16, 16, 1)
    stays = mine[0]
    plan = jnp.stack([wanted, stays, mine[1] * stays, mine[2] * (1 - stays)])
    counts = [jnp.sum((crosses & (to_half == h)).astype(jnp.int32)) for h in range(2)]
    return plan, jnp.maximum(counts[0], counts[1])


def migrate(old_pdfs, old_slot):
    peers = lax.axis_size("blocks")
    slots = old_pdfs.shape[0]
    blocks = old_slot.shape[0]
    planes = 4
    tiles = pl.pallas_call(
        functools.partial(spread_kernel, planes, slots),
        grid=(EDGE // planes,),
        out_shape=jax.ShapeDtypeStruct((EDGE, slots * 152, 128), jnp.float32),
        in_specs=[pl.BlockSpec((slots, 19, planes * 1024), lambda g: (0, 0, g))],
        out_specs=pl.BlockSpec((planes, slots * 152, 128), lambda g: (g, 0, 0)),
        compiler_params=LIMIT,
    )(old_pdfs)
    if peers == EDGE and slots == 2:
        plan, most = migration_plan(old_slot)
        branch = sum((most > room).astype(jnp.int32) for room in CAPACITIES[:-1])
        tiles = tiles.reshape(EDGE, slots, 19, 8, 128)
        calls = [
            functools.partial(migrate_with, room, 1 + number)
            for number, room in enumerate(CAPACITIES)
        ]
        return lax.switch(branch, calls, plan, tiles)
    parts = peers // EDGE
    rows = 8 // parts
    if parts > 1:
        tiles = tiles.reshape(EDGE, slots * 19, parts, rows, 128).transpose(0, 2, 1, 3, 4)
        tiles = tiles.reshape(peers, slots * 19 * rows, 128)
    spread = lax.all_to_all(tiles, "blocks", split_axis=0, concat_axis=0, tiled=True)
    spread = spread.reshape(peers * slots, 19 * rows, 128)
    ordered = spread.at[old_slot].get(mode="promise_in_bounds")
    arrived = lax.all_to_all(ordered, "blocks", split_axis=0, concat_axis=0, tiled=True)
    if parts > 1:
        arrived = arrived.reshape(EDGE, parts, 19, rows, 128).transpose(0, 2, 1, 3, 4)
    return arrived.reshape(EDGE, 19, 8, 128)


def per_device(old_pdfs, old_slot, neighbours, cell_flags):
    state = migrate(old_pdfs, old_slot)
    flags = cell_flags.reshape(EDGE, 8, 128)
    c, xy, zu, zd = pl.pallas_call(
        first_kernel,
        out_shape=[STATE, FACES, FACE, FACE],
        in_specs=[SMEM, VMEM],
        out_specs=[VMEM] * 4,
        scratch_shapes=[ROWS],
        compiler_params=LIMIT,
    )(neighbours, state)
    for _ in range(STEPS - 1):
        rxy, rb, ra = exchange(xy, zu, zd)
        c, xy, zu, zd = pl.pallas_call(
            middle_kernel,
            out_shape=[STATE, FACES, FACE, FACE],
            in_specs=[SMEM] + [VMEM] * 5,
            out_specs=[VMEM] * 4,
            scratch_shapes=[ROWS, GHOSTS],
            compiler_params=LIMIT,
        )(neighbours, flags, c, rxy, rb, ra)
    rxy, rb, ra = exchange(xy, zu, zd)
    return pl.pallas_call(
        last_kernel,
        out_shape=jax.ShapeDtypeStruct((1, 19, EDGE * EDGE * EDGE), jnp.float32),
        in_specs=[SMEM] + [VMEM] * 5,
        out_specs=VMEM,
        scratch_shapes=[GHOSTS, pltpu.VMEM((152, 128), jnp.float32)],
        compiler_params=LIMIT,
    )(neighbours, flags, c, rxy, rb, ra)


def solution(mesh):
    in_specs = (P("blocks", None, None), P(), P("blocks", None), P("blocks", None))
    out_specs = P("blocks", None, None)
    return jax.shard_map(
        per_device, mesh=mesh, in_specs=in_specs, out_specs=out_specs, check_vma=False
    )
```

```python
import functools

import jax
import jax.numpy as jnp
import numpy as np
from jax import lax
from jax.experimental import pallas as pl
from jax.experimental.pallas import tpu as pltpu
from jax.sharding import PartitionSpec as P

EDGE = 32
STEPS = 2
MESH = pl.DeviceIdType.MESH

VELOCITY = (
    (0, 0, 0),
    (1, 0, 0),
    (-1, 0, 0),
    (0, 1, 0),
    (0, -1, 0),
    (0, 0, 1),
    (0, 0, -1),
    (1, 1, 0),
    (-1, -1, 0),
    (1, -1, 0),
    (-1, 1, 0),
    (1, 0, 1),
    (-1, 0, -1),
    (1, 0, -1),
    (-1, 0, 1),
    (0, 1, 1),
    (0, -1, -1),
    (0, 1, -1),
    (0, -1, 1),
)
WEIGHT_LIST = (1.0 / 3.0,) + (1.0 / 18.0,) * 6 + (1.0 / 36.0,) * 12
RELAXATION = (
    0.0,
    0.0,
    0.0,
    0.0,
    1.19,
    1.4,
    1.2,
    1.2,
    1.2,
    1.6,
    1.6,
    1.6,
    1.6,
    1.6,
    1.4,
    1.4,
    1.98,
    1.98,
    1.98,
)
INLET_SPEED = (0.0, 0.0, 0.05)

X_PLUS, X_MINUS = (1, 7, 9, 11, 13), (2, 8, 10, 12, 14)
Y_PLUS, Y_MINUS = (3, 7, 10, 15, 17), (4, 8, 9, 16, 18)
Z_PLUS, Z_MINUS = (5, 11, 14, 15, 18), (6, 12, 13, 16, 17)
ORBITS = ((0,), (1, 2), (3, 4), (5, 6), (7, 8, 9, 10), (11, 12, 13, 14), (15, 16, 17, 18))


def collision_table():
    lattice = np.array(VELOCITY) * 1.0
    along_x, along_y, along_z = (lattice[:, 0], lattice[:, 1], lattice[:, 2])
    squared = along_x * along_x + along_y * along_y + along_z * along_z
    monomials = [
        np.ones(19),
        along_x,
        along_y,
        along_z,
        squared,
        squared * squared,
        squared * along_x,
        squared * along_y,
        squared * along_z,
        3.0 * along_x * along_x - squared,
        along_y * along_y - along_z * along_z,
        along_x * along_y,
        along_y * along_z,
        along_x * along_z,
        squared * (3.0 * along_x * along_x - squared),
        squared * (along_y * along_y - along_z * along_z),
        (along_y * along_y - along_z * along_z) * along_x,
        (along_z * along_z - along_x * along_x) * along_y,
        (along_x * along_x - along_y * along_y) * along_z,
    ]
    orthonormal = []
    for vector in monomials:
        for earlier in orthonormal:
            vector = vector - np.dot(vector, earlier) * earlier
        orthonormal.append(vector / np.sqrt(np.dot(vector, vector)))
    stacked = np.stack(orthonormal)
    return stacked.T * np.array(RELAXATION) @ stacked


def opposite(index_value):
    if index_value == 0:
        return 0
    return index_value + 1 if index_value % 2 == 1 else index_value - 1


def code_of(offset):
    return VELOCITY.index(tuple(offset)) - 1


def collision_blocks():
    matrix = collision_table().astype(np.float32).astype(np.float64)
    even = [[float(np.mean([matrix[a[0], b] for b in group])) for group in ORBITS] for a in ORBITS]
    odd = []
    for axis in range(3):
        groups = [g for g in ORBITS if any(VELOCITY[b][axis] for b in g)]
        rows = []
        for a in groups:
            first = next(c for c in a if VELOCITY[c][axis] > 0)
            rows.append(
                [float(np.mean([VELOCITY[b][axis] * matrix[first, b] for b in g])) for g in groups]
            )
        odd.append(rows)
    mixed = []
    for group in ORBITS[4:]:
        signs = [1.0, 1.0, -1.0, -1.0]
        mixed.append(float(np.mean([s * matrix[group[0], b] for s, b in zip(signs, group)])))
    return even, odd, mixed


def dot(coefficients, terms):
    total = None
    for coefficient, term in zip(coefficients, terms):
        part = term * np.float32(coefficient)
        total = part if total is None else total + part
    return total


def collide(f):
    even, odd, mixed = collision_blocks()
    pair_sum = [f[i] + f[i + 1] for i in (1, 3, 5)]
    pair_dif = [f[i] - f[i + 1] for i in (1, 3, 5)]
    quad_sum, quad_mix, quad_one, quad_two = [], [], [], []
    for i in (7, 11, 15):
        sum_a, sum_b = f[i] + f[i + 1], f[i + 2] + f[i + 3]
        dif_a, dif_b = f[i] - f[i + 1], f[i + 2] - f[i + 3]
        quad_sum.append(sum_a + sum_b)
        quad_mix.append(sum_a - sum_b)
        quad_one.append(dif_a + dif_b)
        quad_two.append(dif_a - dif_b)
    odd_terms = [
        [pair_dif[0], quad_one[0], quad_one[1]],
        [pair_dif[1], quad_two[0], quad_one[2]],
        [pair_dif[2], quad_two[1], quad_two[2]],
    ]
    rho = f[0] + (pair_sum[0] + pair_sum[1] + pair_sum[2]) + (quad_sum[0] + quad_sum[1] + quad_sum[2])
    j = [t[0] + t[1] + t[2] for t in odd_terms]
    sq = [c * c for c in j]
    base = rho - 1.5 * (sq[0] + sq[1] + sq[2])
    sq45 = [4.5 * s for s in sq]
    w0, w1, w2 = 1.0 / 3.0, 1.0 / 18.0, 1.0 / 36.0
    even_terms = [f[0] - w0 * base]
    for a in range(3):
        even_terms.append(pair_sum[a] - (2.0 * w1) * (base + sq45[a]))
    for q, (a, b) in enumerate(((0, 1), (0, 2), (1, 2))):
        even_terms.append(quad_sum[q] - (4.0 * w2) * (base + sq45[a] + sq45[b]))
    mix = [
        (quad_mix[q] - j[a] * j[b]) * np.float32(mixed[q])
        for q, (a, b) in enumerate(((0, 1), (0, 2), (1, 2)))
    ]
    odd_out = []
    for a in range(3):
        third = j[a] * np.float32(1.0 / 3.0)
        terms = [t - third for t in odd_terms[a]]
        odd_out.append([dot(row, terms) for row in odd[a]])
    even_out = [dot(row, even_terms) for row in even]
    out = [f[0] - even_out[0]]
    for a in range(3):
        out.append(f[1 + 2 * a] - (even_out[1 + a] + odd_out[a][0]))
        out.append(f[2 + 2 * a] - (even_out[1 + a] - odd_out[a][0]))
    for q, (one, two) in enumerate(
        (
            (odd_out[0][1], odd_out[1][1]),
            (odd_out[0][2], odd_out[2][1]),
            (odd_out[1][2], odd_out[2][2]),
        )
    ):
        i = 7 + 4 * q
        plus, minus = even_out[4 + q] + mix[q], even_out[4 + q] - mix[q]
        both, apart = one + two, one - two
        out.append(f[i] - (plus + both))
        out.append(f[i + 1] - (plus - both))
        out.append(f[i + 2] - (minus + apart))
        out.append(f[i + 3] - (minus - apart))
    return out


def positions():
    lane = lax.broadcasted_iota(jnp.int32, (8, 128), 1)
    sub = lax.broadcasted_iota(jnp.int32, (8, 128), 0)
    return lane, sub


def shift_y(v, step, ghost, lane, sub):
    if step > 0:
        moved = pltpu.roll(v, 32, 1)
        out = jnp.where(lane < 32, pltpu.roll(moved, 1, 0), moved)
        return jnp.where((lane < 32) & (sub == 0), ghost, out)
    moved = pltpu.roll(v, 96, 1)
    out = jnp.where(lane >= 96, pltpu.roll(moved, 7, 0), moved)
    return jnp.where((lane >= 96) & (sub == 7), ghost, out)


def shift_z(v, step, ghost, z):
    moved = pltpu.roll(v, 1 if step > 0 else 127, 1)
    return jnp.where(z == (0 if step > 0 else 31), ghost, moved)


def unpack_ghosts(nbr, rxy, gy):
    lane, _ = positions()
    jy = jnp.maximum(nbr[0, 2], nbr[0, 3]) & 3
    jd = jnp.maximum(jnp.maximum(nbr[0, 6], nbr[0, 7]), jnp.maximum(nbr[0, 8], nbr[0, 9])) & 3
    for k in range(5):
        packed = rxy[jy, 5 + k]
        for g in range(4):
            low = pltpu.roll(packed, (128 - 32 * g) % 128, 1)
            high = pltpu.roll(packed, (96 - 32 * g) % 128, 1)
            gy[k, 1 + 8 * g : 9 + 8 * g, :] = jnp.where(lane < 64, low, high)
    for channel in (7, 8, 9, 10):
        cx, cy, _ = VELOCITY[channel]
        kx = (X_PLUS if cx > 0 else X_MINUS).index(channel)
        ky = (Y_PLUS if cy > 0 else Y_MINUS).index(channel)
        plane = rxy[jd, kx]
        row = pltpu.roll(plane, 32 if cy > 0 else 96, 1)
        row = row[7:8, :] if cy > 0 else row[0:1, :]
        spot = 0 if cx > 0 else 33
        gy[ky, spot : spot + 1, :] = row


def pull(x, nbr, c, rxy, rb, ra, flags, gy):
    lane, sub = positions()
    z = lane & 31
    jx = jnp.maximum(nbr[0, 0], nbr[0, 1]) & 3

    def wall(offset):
        return jnp.where(nbr[0, code_of(offset)] >= 0, 0, 1).astype(jnp.int32)

    def spot(offset):
        return nbr[0, code_of(offset)] & 3

    own = flags[x]
    values = [c[x, i] for i in range(19)]
    j = []
    for axis in range(3):
        plus = sum(values[i] for i in range(19) if VELOCITY[i][axis] > 0)
        minus = sum(values[i] for i in range(19) if VELOCITY[i][axis] < 0)
        j.append(plus - minus)
    calm = 1.0 - 1.5 * (j[0] * j[0] + j[1] * j[1] + j[2] * j[2])
    inlet_square = sum(p * p for p in INLET_SPEED)
    out = [jnp.where(own == 0, values[0], 0.0)]
    for i in range(1, 19):
        cx, cy, cz = VELOCITY[i]
        if cx:
            outside = x == (0 if cx > 0 else EDGE - 1)
            from_x = jnp.clip(x - cx, 0, EDGE - 1)
            kx = (X_PLUS if cx > 0 else X_MINUS).index(i)
            v = jnp.where(outside, rxy[jx, kx], c[from_x, i])
            kind = jnp.where(outside, wall((-cx, 0, 0)), flags[from_x])
        else:
            v, kind = values[i], own
        if cz:
            beyond = rb if cz > 0 else ra
            kz = (Z_PLUS if cz > 0 else Z_MINUS).index(i)
            block, blocked = spot((0, 0, -cz)), wall((0, 0, -cz))
            at = x
            if cx:
                block = jnp.where(outside, spot((-cx, 0, -cz)), block)
                blocked = jnp.where(outside, wall((-cx, 0, -cz)), blocked)
                at = (x - cx) & 31
            message = beyond[block, kz]
            amount = (128 - at) & 127 if cz > 0 else 31 - at
            v = shift_z(v, cz, pltpu.roll(message, amount, 1), z)
            kind = shift_z(kind, cz, blocked, z)
        if cy:
            ky = (Y_PLUS if cy > 0 else Y_MINUS).index(i)
            row = jnp.broadcast_to(gy[ky, pl.ds(x - cx + 1, 1), :], (8, 128))
            blocked = wall((0, -cy, 0))
            if cx:
                blocked = jnp.where(outside, wall((-cx, -cy, 0)), blocked)
            if cz:
                corner = beyond[spot((0, -cy, -cz)), kz]
                target = (0 if cy > 0 else 96) + (0 if cz > 0 else 31)
                source = (96 if cy > 0 else 0) + x
                corner = pltpu.roll(corner, (target - source + 256) & 127, 1)
                corner = corner[7:8, :] if cy > 0 else corner[0:1, :]
                row = shift_z(row, cz, jnp.broadcast_to(corner, (8, 128)), z)
                blocked = jnp.where(z == (0 if cz > 0 else 31), wall((0, -cy, -cz)), blocked)
            v = shift_y(v, cy, row, lane, sub)
            kind = shift_y(kind, cy, blocked, lane, sub)
        weight = WEIGHT_LIST[i]
        along = sum(a * b for a, b in zip(VELOCITY[i], INLET_SPEED))
        inlet = weight * (1.0 + 3.0 * along + 4.5 * along * along - 1.5 * inlet_square)
        speed = sum(a * b for a, b in zip(VELOCITY[i], j) if a)
        outlet = weight * (calm + speed * (3.0 + 4.5 * speed))
        new = jnp.where(
            kind == 0,
            v,
            jnp.where(kind == 1, values[opposite(i)], jnp.where(kind == 2, np.float32(inlet), outlet)),
        )
        out.append(jnp.where(own == 0, new, 0.0))
    return out


def note_faces(x, nbr, collided, zu, zd, rows):
    lane, _ = positions()
    here = (lane & 31) == x
    for k in range(5):
        up = pltpu.roll(collided[Z_PLUS[k]], (x + 97) & 127, 1)
        zu[k] = jnp.where(here, up, zu[k])
        zd[k] = jnp.where(here, pltpu.roll(collided[Z_MINUS[k]], x, 1), zd[k])
        high = collided[Y_PLUS[k]][7:8, :]
        low = collided[Y_MINUS[k]][0:1, :]
        rows[k, pl.ds(x, 1), :] = jnp.where(nbr[0, 2] >= 0, high, low)


def finish_faces(nbr, c, rows, xy):
    lane, _ = positions()
    ahead_x, ahead_y = nbr[0, 0] >= 0, nbr[0, 2] >= 0
    for k in range(5):
        xy[k] = jnp.where(ahead_x, c[EDGE - 1, X_PLUS[k]], c[0, X_MINUS[k]])
        packed = jnp.zeros((8, 128), jnp.float32)
        for g in range(4):
            part = rows[k, 8 * g : 8 * g + 8, :]
            high = pltpu.roll(part, (32 * (g + 1)) % 128, 1)
            low = pltpu.roll(part, 32 * g, 1)
            packed = jnp.where((lane >> 5) == g, jnp.where(ahead_y, high, low), packed)
        xy[5 + k] = packed


def steps_kernel(layers, nbr, flags, f, out, *scratch):
    c, messages, landed = scratch[:2], scratch[2 : 2 + 3 * STEPS], scratch[2 + 3 * STEPS : 2 + 6 * STEPS]
    rows, gy, lines, send_sem, recv_sem = scratch[2 + 6 * STEPS :]
    wait_entry, send, receive, finish = exchanges(layers, messages, landed, send_sem, recv_sem)
    for step in range(STEPS):
        now, before = c[step % 2], c[(step + 1) % 2]
        xy, zu, zd = messages[3 * step : 3 * step + 3]
        zu[...] = jnp.zeros_like(zu)
        zd[...] = jnp.zeros_like(zd)
        if step > 0:
            rxy, rb, ra = landed[3 * step - 3 : 3 * step]
            unpack_ghosts(nbr, rxy, gy)

        def plane(x, carry):
            if step == 0:
                old = [f[x, i] for i in range(19)]
            else:
                old = pull(x, nbr, before, rxy, rb, ra, flags, gy)
            collided = collide(old)
            for i in range(19):
                now[x, i] = collided[i]
            note_faces(x, nbr, collided, zu, zd, rows)
            return carry

        lax.fori_loop(0, EDGE, plane, 0)
        finish_faces(nbr, now, rows, xy)
        if step == 0:
            wait_entry()
        send(step)
        receive(step)
    rxy, rb, ra = landed[3 * STEPS - 3 :]
    unpack_ghosts(nbr, rxy, gy)

    def last_plane(x, carry):
        new = pull(x, nbr, now, rxy, rb, ra, flags, gy)
        for i in range(19):
            lines[8 * i : 8 * i + 8, :] = new[i]
        for s in range(8):
            at = pl.multiple_of(x * 1024 + s * 128, 128)
            out[0, :, pl.ds(at, 128)] = lines[pl.ds(s, 19, stride=8), :]
        return carry

    lax.fori_loop(0, EDGE, last_plane, 0)
    for step in range(STEPS):
        finish(step)


def spread_kernel(planes, slots, old, out):
    def plane(x, carry):
        for slot in range(slots):
            for s in range(8):
                at = pl.multiple_of(x * 1024 + s * 128, 128)
                out[x, pl.ds(slot * 152 + s, 19, stride=8), :] = old[slot, :, pl.ds(at, 128)]
        return carry

    lax.fori_loop(0, planes, plane, 0)


def exchanges(layers, messages, landed, send_sem, recv_sem):
    me = lax.axis_index("blocks")
    layer, place = me // 4, me % 4
    above, below = layer + 1 < layers, layer > 0
    barrier = pltpu.get_barrier_semaphore()

    def greet(first, k):
        pl.semaphore_signal(
            barrier, inc=1, device_id=(first * 4 + (place + k) % 4,), device_id_type=MESH
        )

    for k in range(1, 4):
        greet(layer, k)

    @pl.when(above)
    def _():
        for k in range(4):
            greet(layer + 1, k)

    @pl.when(below)
    def _():
        for k in range(4):
            greet(layer - 1, k)

    def wait_entry():
        peers = 3 + 4 * above.astype(jnp.int32) + 4 * below.astype(jnp.int32)
        pl.semaphore_wait(barrier, peers)

    def copy(step, group, spot, first, k):
        return pltpu.make_async_remote_copy(
            src_ref=messages[3 * step + group],
            dst_ref=landed[3 * step + group].at[spot],
            send_sem=send_sem.at[step, 4 * group + k],
            recv_sem=recv_sem.at[step, 4 * group + k],
            device_id=(first * 4 + (place + k) % 4,),
            device_id_type=MESH,
        )

    def send(step):
        @pl.when(above)
        def _():
            for k in range(4):
                copy(step, 1, place, layer + 1, k).start()

        @pl.when(below)
        def _():
            for k in range(4):
                copy(step, 2, place, layer - 1, k).start()

        for k in range(1, 4):
            copy(step, 0, place, layer, k).start()

    def receive(step):
        for k in range(1, 4):
            copy(step, 0, (place + 4 - k) % 4, layer, k).wait_recv()

        @pl.when(below)
        def _():
            for k in range(4):
                copy(step, 1, (place + 4 - k) % 4, layer - 1, k).wait_recv()

        @pl.when(above)
        def _():
            for k in range(4):
                copy(step, 2, (place + 4 - k) % 4, layer + 1, k).wait_recv()

    def finish(step):
        @pl.when(above)
        def _():
            for k in range(4):
                copy(step, 1, place, layer + 1, k).wait_send()

        @pl.when(below)
        def _():
            for k in range(4):
                copy(step, 2, place, layer - 1, k).wait_send()

        for k in range(1, 4):
            copy(step, 0, place, layer, k).wait_send()

    return wait_entry, send, receive, finish


VMEM = pl.BlockSpec(memory_space=pltpu.VMEM)
SMEM = pl.BlockSpec(memory_space=pltpu.SMEM)
STATE = jax.ShapeDtypeStruct((EDGE, 19, 8, 128), jnp.float32)


CHUNKS = ((0, 0, 10), (1, 0, 10), (0, 10, 19), (1, 10, 19))
CAPACITIES = (10, 12, 16)


def migrate_kernel(room, plan, tiles, out, *scratch):
    parts = len(CHUNKS)
    held, wanted, given, sorted_ = (scratch[parts * n : parts * n + parts] for n in range(4))
    own_sem, send_one, recv_one, send_two, recv_two, send_three, recv_three = scratch[4 * parts :]
    me = lax.axis_index("blocks")
    half, place = me // 16, me % 16
    partner = (1 - half) * 16 + place

    def peer(d):
        return (place + d) % 16

    def device(d):
        return (half * 16 + peer(d),)

    barrier = pltpu.get_barrier_semaphore()

    def greet(d, carry):
        pl.semaphore_signal(barrier, inc=1, device_id=device(d), device_id_type=MESH)
        return carry

    lax.fori_loop(1, 16, greet, 0)
    pl.semaphore_signal(barrier, inc=1, device_id=(partner,), device_id_type=MESH)
    pl.semaphore_wait(barrier, 16)

    def spread(k, d, owner):
        plane, low, high = CHUNKS[k]
        return pltpu.make_async_remote_copy(
            src_ref=tiles.at[2 * peer(d) + plane, :, low:high],
            dst_ref=held[k].at[pl.ds(2 * owner, 2)],
            send_sem=send_one.at[k, d],
            recv_sem=recv_one.at[k, d],
            device_id=device(d),
            device_id_type=MESH,
        )

    def keep(k):
        plane, low, high = CHUNKS[k]
        return pltpu.make_async_copy(
            tiles.at[2 * place + plane, :, low:high], held[k].at[pl.ds(2 * place, 2)], own_sem.at[k]
        )

    def swap(k):
        return pltpu.make_async_remote_copy(
            src_ref=wanted[k],
            dst_ref=given[k],
            send_sem=send_two.at[k],
            recv_sem=recv_two.at[k],
            device_id=(partner,),
            device_id_type=MESH,
        )

    def hand(k, d, owner):
        plane, low, high = CHUNKS[k]
        return pltpu.make_async_remote_copy(
            src_ref=sorted_[k].at[peer(d)],
            dst_ref=out.at[2 * owner + plane, low:high],
            send_sem=send_three.at[k, d],
            recv_sem=recv_three.at[k, d],
            device_id=device(d),
            device_id_type=MESH,
        )

    def each(body):
        def step(d, carry):
            body(d)
            return carry

        lax.fori_loop(1, 16, step, 0)

    def deliver(k):
        plane, low, high = CHUNKS[k]
        swap(k).wait_recv()

        def choose(b, carry):
            near, far = held[k][plan[2, b]], given[k][plan[3, b]]
            sorted_[k][b] = jnp.where(plan[1, b] > 0, near, far)
            return carry

        lax.fori_loop(0, 16, choose, 0)
        each(lambda d: hand(k, d, place).start())
        out[2 * place + plane, low:high] = sorted_[k][place]

    def begin(k):
        keep(k).start()
        each(lambda d: spread(k, d, place).start())

    begin(0)
    begin(1)
    for k in range(parts):
        keep(k).wait()
        each(lambda d: spread(k, d, peer(16 - d)).wait_recv())

        def pick(e, carry):
            wanted[k][e] = held[k][plan[0, e]]
            return carry

        lax.fori_loop(0, room, pick, 0)
        swap(k).start()
        if k + 2 < parts:
            begin(k + 2)
        if k > 0:
            deliver(k - 1)
    deliver(parts - 1)
    for k in range(parts):
        each(lambda d: hand(k, d, peer(16 - d)).wait_recv())
    for k in range(parts):
        each(lambda d: spread(k, d, place).wait_send())
        swap(k).wait_send()
        each(lambda d: hand(k, d, place).wait_send())


def migrate_with(room, number, plan, tiles):
    parts = len(CHUNKS)

    def buffers(count):
        return [pltpu.VMEM((count, high - low, 8, 128), jnp.float32) for _, low, high in CHUNKS]

    dma = pltpu.SemaphoreType.DMA
    return pl.pallas_call(
        functools.partial(migrate_kernel, room),
        out_shape=STATE,
        in_specs=[SMEM, VMEM],
        out_specs=VMEM,
        scratch_shapes=buffers(32)
        + buffers(room)
        + buffers(room)
        + buffers(16)
        + [dma((parts,)), dma((parts, 16)), dma((parts, 16)), dma((parts,)), dma((parts,))]
        + [dma((parts, 16)), dma((parts, 16))],
        compiler_params=pltpu.CompilerParams(
            collective_id=number, has_side_effects=True, vmem_limit_bytes=40 * 2**20
        ),
    )(plan, tiles)


def migration_plan(old_slot):
    half = lax.axis_index("blocks") // 16
    block = jnp.arange(32, dtype=jnp.int32)
    from_half, to_half = old_slot // 32, block // 16
    crosses = from_half != to_half
    same = (to_half[None, :] == to_half[:, None]) & (block[None, :] < block[:, None])
    rank = jnp.sum((same & crosses[None, :]).astype(jnp.int32), axis=1)
    leaves = crosses & (from_half == half)
    entry = jnp.arange(16, dtype=jnp.int32)
    chosen = leaves[None, :] & (rank[None, :] == entry[:, None])
    local = old_slot % 32
    wanted = jnp.sum(jnp.where(chosen, local[None, :], 0), axis=1)
    mine = lax.dynamic_slice_in_dim(jnp.stack([1 - crosses.astype(jnp.int32), local, rank]), half * 16, 16, 1)
    stays = mine[0]
    plan = jnp.stack([wanted, stays, mine[1] * stays, mine[2] * (1 - stays)])
    counts = [jnp.sum((crosses & (to_half == h)).astype(jnp.int32)) for h in range(2)]
    return plan, jnp.maximum(counts[0], counts[1])


def migrate(old_pdfs, old_slot):
    peers = lax.axis_size("blocks")
    slots = old_pdfs.shape[0]
    blocks = old_slot.shape[0]
    planes = 4
    tiles = pl.pallas_call(
        functools.partial(spread_kernel, planes, slots),
        grid=(EDGE // planes,),
        out_shape=jax.ShapeDtypeStruct((EDGE, slots * 152, 128), jnp.float32),
        in_specs=[pl.BlockSpec((slots, 19, planes * 1024), lambda g: (0, 0, g))],
        out_specs=pl.BlockSpec((planes, slots * 152, 128), lambda g: (g, 0, 0)),
        compiler_params=pltpu.CompilerParams(vmem_limit_bytes=58 * 2**20),
    )(old_pdfs)
    if peers == EDGE and slots == 2:
        plan, most = migration_plan(old_slot)
        branch = sum((most > room).astype(jnp.int32) for room in CAPACITIES[:-1])
        tiles = tiles.reshape(EDGE, slots, 19, 8, 128)
        calls = [
            functools.partial(migrate_with, room, 1 + number)
            for number, room in enumerate(CAPACITIES)
        ]
        return lax.switch(branch, calls, plan, tiles)
    parts = peers // EDGE
    rows = 8 // parts
    if parts > 1:
        tiles = tiles.reshape(EDGE, slots * 19, parts, rows, 128).transpose(0, 2, 1, 3, 4)
        tiles = tiles.reshape(peers, slots * 19 * rows, 128)
    spread = lax.all_to_all(tiles, "blocks", split_axis=0, concat_axis=0, tiled=True)
    spread = spread.reshape(peers * slots, 19 * rows, 128)
    ordered = spread.at[old_slot].get(mode="promise_in_bounds")
    arrived = lax.all_to_all(ordered, "blocks", split_axis=0, concat_axis=0, tiled=True)
    if parts > 1:
        arrived = arrived.reshape(EDGE, parts, 19, rows, 128).transpose(0, 2, 1, 3, 4)
    return arrived.reshape(EDGE, 19, 8, 128)


def per_device(old_pdfs, old_slot, neighbours, cell_flags):
    state = migrate(old_pdfs, old_slot)
    flags = cell_flags.reshape(EDGE, 8, 128)
    layers = lax.axis_size("blocks") // 4

    def tiles(*lead):
        return pltpu.VMEM(lead + (8, 128), jnp.float32)

    return pl.pallas_call(
        functools.partial(steps_kernel, layers),
        out_shape=jax.ShapeDtypeStruct((1, 19, EDGE * EDGE * EDGE), jnp.float32),
        in_specs=[SMEM, VMEM, VMEM],
        out_specs=VMEM,
        scratch_shapes=[tiles(EDGE, 19)] * 2
        + [tiles(10), tiles(5), tiles(5)] * STEPS
        + [tiles(4, 10), tiles(4, 5), tiles(4, 5)] * STEPS
        + [
            pltpu.VMEM((5, EDGE, 128), jnp.float32),
            pltpu.VMEM((5, EDGE + 8, 128), jnp.float32),
            pltpu.VMEM((152, 128), jnp.float32),
            pltpu.SemaphoreType.DMA((STEPS, 12)),
            pltpu.SemaphoreType.DMA((STEPS, 12)),
        ],
        compiler_params=pltpu.CompilerParams(
            collective_id=0, has_side_effects=True, vmem_limit_bytes=40 * 2**20
        ),
    )(neighbours, flags, state)


def solution(mesh):
    in_specs = (P("blocks", None, None), P(), P("blocks", None), P("blocks", None))
    out_specs = P("blocks", None, None)
    return jax.shard_map(
        per_device, mesh=mesh, in_specs=in_specs, out_specs=out_specs, check_vma=False
    )
```

```python
import functools

import jax
import jax.numpy as jnp
import numpy as np
from jax import lax
from jax.experimental import pallas as pl
from jax.experimental.pallas import tpu as pltpu
from jax.sharding import PartitionSpec as P

EDGE = 32
STEPS = 2
MESH = pl.DeviceIdType.MESH

VELOCITY = (
    (0, 0, 0),
    (1, 0, 0),
    (-1, 0, 0),
    (0, 1, 0),
    (0, -1, 0),
    (0, 0, 1),
    (0, 0, -1),
    (1, 1, 0),
    (-1, -1, 0),
    (1, -1, 0),
    (-1, 1, 0),
    (1, 0, 1),
    (-1, 0, -1),
    (1, 0, -1),
    (-1, 0, 1),
    (0, 1, 1),
    (0, -1, -1),
    (0, 1, -1),
    (0, -1, 1),
)
WEIGHT_LIST = (1.0 / 3.0,) + (1.0 / 18.0,) * 6 + (1.0 / 36.0,) * 12
RELAXATION = (
    0.0,
    0.0,
    0.0,
    0.0,
    1.19,
    1.4,
    1.2,
    1.2,
    1.2,
    1.6,
    1.6,
    1.6,
    1.6,
    1.6,
    1.4,
    1.4,
    1.98,
    1.98,
    1.98,
)
INLET_SPEED = (0.0, 0.0, 0.05)

X_PLUS, X_MINUS = (1, 7, 9, 11, 13), (2, 8, 10, 12, 14)
Y_PLUS, Y_MINUS = (3, 7, 10, 15, 17), (4, 8, 9, 16, 18)
Z_PLUS, Z_MINUS = (5, 11, 14, 15, 18), (6, 12, 13, 16, 17)
ORBITS = ((0,), (1, 2), (3, 4), (5, 6), (7, 8, 9, 10), (11, 12, 13, 14), (15, 16, 17, 18))


def collision_table():
    lattice = np.array(VELOCITY) * 1.0
    along_x, along_y, along_z = (lattice[:, 0], lattice[:, 1], lattice[:, 2])
    squared = along_x * along_x + along_y * along_y + along_z * along_z
    monomials = [
        np.ones(19),
        along_x,
        along_y,
        along_z,
        squared,
        squared * squared,
        squared * along_x,
        squared * along_y,
        squared * along_z,
        3.0 * along_x * along_x - squared,
        along_y * along_y - along_z * along_z,
        along_x * along_y,
        along_y * along_z,
        along_x * along_z,
        squared * (3.0 * along_x * along_x - squared),
        squared * (along_y * along_y - along_z * along_z),
        (along_y * along_y - along_z * along_z) * along_x,
        (along_z * along_z - along_x * along_x) * along_y,
        (along_x * along_x - along_y * along_y) * along_z,
    ]
    orthonormal = []
    for vector in monomials:
        for earlier in orthonormal:
            vector = vector - np.dot(vector, earlier) * earlier
        orthonormal.append(vector / np.sqrt(np.dot(vector, vector)))
    stacked = np.stack(orthonormal)
    return stacked.T * np.array(RELAXATION) @ stacked


def opposite(index_value):
    if index_value == 0:
        return 0
    return index_value + 1 if index_value % 2 == 1 else index_value - 1


def code_of(offset):
    return VELOCITY.index(tuple(offset)) - 1


def collision_blocks():
    matrix = collision_table().astype(np.float32).astype(np.float64)
    even = [[float(np.mean([matrix[a[0], b] for b in group])) for group in ORBITS] for a in ORBITS]
    odd = []
    for axis in range(3):
        groups = [g for g in ORBITS if any(VELOCITY[b][axis] for b in g)]
        rows = []
        for a in groups:
            first = next(c for c in a if VELOCITY[c][axis] > 0)
            rows.append(
                [float(np.mean([VELOCITY[b][axis] * matrix[first, b] for b in g])) for g in groups]
            )
        odd.append(rows)
    mixed = []
    for group in ORBITS[4:]:
        signs = [1.0, 1.0, -1.0, -1.0]
        mixed.append(float(np.mean([s * matrix[group[0], b] for s, b in zip(signs, group)])))
    return even, odd, mixed


def dot(coefficients, terms):
    total = None
    for coefficient, term in zip(coefficients, terms):
        part = term * np.float32(coefficient)
        total = part if total is None else total + part
    return total


def collide(f):
    even, odd, mixed = collision_blocks()
    pair_sum = [f[i] + f[i + 1] for i in (1, 3, 5)]
    pair_dif = [f[i] - f[i + 1] for i in (1, 3, 5)]
    quad_sum, quad_mix, quad_one, quad_two = [], [], [], []
    for i in (7, 11, 15):
        sum_a, sum_b = f[i] + f[i + 1], f[i + 2] + f[i + 3]
        dif_a, dif_b = f[i] - f[i + 1], f[i + 2] - f[i + 3]
        quad_sum.append(sum_a + sum_b)
        quad_mix.append(sum_a - sum_b)
        quad_one.append(dif_a + dif_b)
        quad_two.append(dif_a - dif_b)
    odd_terms = [
        [pair_dif[0], quad_one[0], quad_one[1]],
        [pair_dif[1], quad_two[0], quad_one[2]],
        [pair_dif[2], quad_two[1], quad_two[2]],
    ]
    rho = f[0] + (pair_sum[0] + pair_sum[1] + pair_sum[2]) + (quad_sum[0] + quad_sum[1] + quad_sum[2])
    j = [t[0] + t[1] + t[2] for t in odd_terms]
    sq = [c * c for c in j]
    base = rho - 1.5 * (sq[0] + sq[1] + sq[2])
    sq45 = [4.5 * s for s in sq]
    w0, w1, w2 = 1.0 / 3.0, 1.0 / 18.0, 1.0 / 36.0
    even_terms = [f[0] - w0 * base]
    for a in range(3):
        even_terms.append(pair_sum[a] - (2.0 * w1) * (base + sq45[a]))
    for q, (a, b) in enumerate(((0, 1), (0, 2), (1, 2))):
        even_terms.append(quad_sum[q] - (4.0 * w2) * (base + sq45[a] + sq45[b]))
    mix = [
        (quad_mix[q] - j[a] * j[b]) * np.float32(mixed[q])
        for q, (a, b) in enumerate(((0, 1), (0, 2), (1, 2)))
    ]
    odd_out = []
    for a in range(3):
        third = j[a] * np.float32(1.0 / 3.0)
        terms = [t - third for t in odd_terms[a]]
        odd_out.append([dot(row, terms) for row in odd[a]])
    even_out = [dot(row, even_terms) for row in even]
    out = [f[0] - even_out[0]]
    for a in range(3):
        out.append(f[1 + 2 * a] - (even_out[1 + a] + odd_out[a][0]))
        out.append(f[2 + 2 * a] - (even_out[1 + a] - odd_out[a][0]))
    for q, (one, two) in enumerate(
        (
            (odd_out[0][1], odd_out[1][1]),
            (odd_out[0][2], odd_out[2][1]),
            (odd_out[1][2], odd_out[2][2]),
        )
    ):
        i = 7 + 4 * q
        plus, minus = even_out[4 + q] + mix[q], even_out[4 + q] - mix[q]
        both, apart = one + two, one - two
        out.append(f[i] - (plus + both))
        out.append(f[i + 1] - (plus - both))
        out.append(f[i + 2] - (minus + apart))
        out.append(f[i + 3] - (minus - apart))
    return out


def positions():
    lane = lax.broadcasted_iota(jnp.int32, (8, 128), 1)
    sub = lax.broadcasted_iota(jnp.int32, (8, 128), 0)
    return lane, sub


def shift_y(v, step, ghost, lane, sub):
    if step > 0:
        moved = pltpu.roll(v, 32, 1)
        out = jnp.where(lane < 32, pltpu.roll(moved, 1, 0), moved)
        return jnp.where((lane < 32) & (sub == 0), ghost, out)
    moved = pltpu.roll(v, 96, 1)
    out = jnp.where(lane >= 96, pltpu.roll(moved, 7, 0), moved)
    return jnp.where((lane >= 96) & (sub == 7), ghost, out)


def shift_z(v, step, ghost, z):
    moved = pltpu.roll(v, 1 if step > 0 else 127, 1)
    return jnp.where(z == (0 if step > 0 else 31), ghost, moved)


def unpack_ghosts(nbr, rxy, gy):
    lane, _ = positions()
    jy = jnp.maximum(nbr[0, 2], nbr[0, 3]) & 3
    jd = jnp.maximum(jnp.maximum(nbr[0, 6], nbr[0, 7]), jnp.maximum(nbr[0, 8], nbr[0, 9])) & 3
    for k in range(5):
        packed = rxy[jy, 5 + k]
        for g in range(4):
            low = pltpu.roll(packed, (128 - 32 * g) % 128, 1)
            high = pltpu.roll(packed, (96 - 32 * g) % 128, 1)
            gy[k, 1 + 8 * g : 9 + 8 * g, :] = jnp.where(lane < 64, low, high)
    for channel in (7, 8, 9, 10):
        cx, cy, _ = VELOCITY[channel]
        kx = (X_PLUS if cx > 0 else X_MINUS).index(channel)
        ky = (Y_PLUS if cy > 0 else Y_MINUS).index(channel)
        plane = rxy[jd, kx]
        row = pltpu.roll(plane, 32 if cy > 0 else 96, 1)
        row = row[7:8, :] if cy > 0 else row[0:1, :]
        spot = 0 if cx > 0 else 33
        gy[ky, spot : spot + 1, :] = row


def pull(x, nbr, c, rxy, rb, ra, flags, gy):
    lane, sub = positions()
    z = lane & 31
    jx = jnp.maximum(nbr[0, 0], nbr[0, 1]) & 3

    def wall(offset):
        return jnp.where(nbr[0, code_of(offset)] >= 0, 0, 1).astype(jnp.int32)

    def spot(offset):
        return nbr[0, code_of(offset)] & 3

    own = flags[x]
    values = [c[x, i] for i in range(19)]
    j = []
    for axis in range(3):
        plus = sum(values[i] for i in range(19) if VELOCITY[i][axis] > 0)
        minus = sum(values[i] for i in range(19) if VELOCITY[i][axis] < 0)
        j.append(plus - minus)
    calm = 1.0 - 1.5 * (j[0] * j[0] + j[1] * j[1] + j[2] * j[2])
    inlet_square = sum(p * p for p in INLET_SPEED)
    out = [jnp.where(own == 0, values[0], 0.0)]
    for i in range(1, 19):
        cx, cy, cz = VELOCITY[i]
        if cx:
            outside = x == (0 if cx > 0 else EDGE - 1)
            from_x = jnp.clip(x - cx, 0, EDGE - 1)
            kx = (X_PLUS if cx > 0 else X_MINUS).index(i)
            v = jnp.where(outside, rxy[jx, kx], c[from_x, i])
            kind = jnp.where(outside, wall((-cx, 0, 0)), flags[from_x])
        else:
            v, kind = values[i], own
        if cz:
            beyond = rb if cz > 0 else ra
            kz = (Z_PLUS if cz > 0 else Z_MINUS).index(i)
            block, blocked = spot((0, 0, -cz)), wall((0, 0, -cz))
            at = x
            if cx:
                block = jnp.where(outside, spot((-cx, 0, -cz)), block)
                blocked = jnp.where(outside, wall((-cx, 0, -cz)), blocked)
                at = (x - cx) & 31
            message = beyond[block, kz]
            amount = (128 - at) & 127 if cz > 0 else 31 - at
            v = shift_z(v, cz, pltpu.roll(message, amount, 1), z)
            kind = shift_z(kind, cz, blocked, z)
        if cy:
            ky = (Y_PLUS if cy > 0 else Y_MINUS).index(i)
            row = jnp.broadcast_to(gy[ky, pl.ds(x - cx + 1, 1), :], (8, 128))
            blocked = wall((0, -cy, 0))
            if cx:
                blocked = jnp.where(outside, wall((-cx, -cy, 0)), blocked)
            if cz:
                corner = beyond[spot((0, -cy, -cz)), kz]
                target = (0 if cy > 0 else 96) + (0 if cz > 0 else 31)
                source = (96 if cy > 0 else 0) + x
                corner = pltpu.roll(corner, (target - source + 256) & 127, 1)
                corner = corner[7:8, :] if cy > 0 else corner[0:1, :]
                row = shift_z(row, cz, jnp.broadcast_to(corner, (8, 128)), z)
                blocked = jnp.where(z == (0 if cz > 0 else 31), wall((0, -cy, -cz)), blocked)
            v = shift_y(v, cy, row, lane, sub)
            kind = shift_y(kind, cy, blocked, lane, sub)
        weight = WEIGHT_LIST[i]
        along = sum(a * b for a, b in zip(VELOCITY[i], INLET_SPEED))
        inlet = weight * (1.0 + 3.0 * along + 4.5 * along * along - 1.5 * inlet_square)
        speed = sum(a * b for a, b in zip(VELOCITY[i], j) if a)
        outlet = weight * (calm + speed * (3.0 + 4.5 * speed))
        new = jnp.where(
            kind == 0,
            v,
            jnp.where(kind == 1, values[opposite(i)], jnp.where(kind == 2, np.float32(inlet), outlet)),
        )
        out.append(jnp.where(own == 0, new, 0.0))
    return out


def note_faces(x, nbr, collided, zu, zd, rows):
    lane, _ = positions()
    here = (lane & 31) == x
    for k in range(5):
        up = pltpu.roll(collided[Z_PLUS[k]], (x + 97) & 127, 1)
        zu[k] = jnp.where(here, up, zu[k])
        zd[k] = jnp.where(here, pltpu.roll(collided[Z_MINUS[k]], x, 1), zd[k])
        high = collided[Y_PLUS[k]][7:8, :]
        low = collided[Y_MINUS[k]][0:1, :]
        rows[k, pl.ds(x, 1), :] = jnp.where(nbr[0, 2] >= 0, high, low)


def finish_faces(nbr, c, rows, xy):
    lane, _ = positions()
    ahead_x, ahead_y = nbr[0, 0] >= 0, nbr[0, 2] >= 0
    for k in range(5):
        xy[k] = jnp.where(ahead_x, c[EDGE - 1, X_PLUS[k]], c[0, X_MINUS[k]])
        packed = jnp.zeros((8, 128), jnp.float32)
        for g in range(4):
            part = rows[k, 8 * g : 8 * g + 8, :]
            high = pltpu.roll(part, (32 * (g + 1)) % 128, 1)
            low = pltpu.roll(part, 32 * g, 1)
            packed = jnp.where((lane >> 5) == g, jnp.where(ahead_y, high, low), packed)
        xy[5 + k] = packed


def steps_kernel(layers, nbr, flags, f, out, *scratch):
    c, messages, landed = scratch[:2], scratch[2 : 2 + 3 * STEPS], scratch[2 + 3 * STEPS : 2 + 6 * STEPS]
    rows, gy, send_sem, recv_sem = scratch[2 + 6 * STEPS :]
    wait_entry, send, receive, finish = exchanges(layers, messages, landed, send_sem, recv_sem)
    for step in range(STEPS):
        now, before = c[step % 2], c[(step + 1) % 2]
        xy, zu, zd = messages[3 * step : 3 * step + 3]
        zu[...] = jnp.zeros_like(zu)
        zd[...] = jnp.zeros_like(zd)
        if step > 0:
            rxy, rb, ra = landed[3 * step - 3 : 3 * step]
            unpack_ghosts(nbr, rxy, gy)

        def plane(x, carry):
            if step == 0:
                old = [f[x, i] for i in range(19)]
            else:
                old = pull(x, nbr, before, rxy, rb, ra, flags, gy)
            collided = collide(old)
            for i in range(19):
                now[x, i] = collided[i]
            note_faces(x, nbr, collided, zu, zd, rows)
            return carry

        lax.fori_loop(0, EDGE, plane, 0)
        finish_faces(nbr, now, rows, xy)
        if step == 0:
            wait_entry()
        send(step)
        receive(step)
    rxy, rb, ra = landed[3 * STEPS - 3 :]
    unpack_ghosts(nbr, rxy, gy)

    def last_plane(x, carry):
        new = pull(x, nbr, now, rxy, rb, ra, flags, gy)
        for i in range(19):
            out[i, x] = new[i]
        return carry

    lax.fori_loop(0, EDGE, last_plane, 0)
    for step in range(STEPS):
        finish(step)


def spread_kernel(planes, slots, old, out):
    def plane(x, carry):
        for slot in range(slots):
            for s in range(8):
                at = pl.multiple_of(x * 1024 + s * 128, 128)
                out[x, pl.ds(slot * 152 + s, 19, stride=8), :] = old[slot, :, pl.ds(at, 128)]
        return carry

    lax.fori_loop(0, planes, plane, 0)


def exchanges(layers, messages, landed, send_sem, recv_sem):
    me = lax.axis_index("blocks")
    layer, place = me // 4, me % 4
    above, below = layer + 1 < layers, layer > 0
    barrier = pltpu.get_barrier_semaphore()

    def greet(first, k):
        pl.semaphore_signal(
            barrier, inc=1, device_id=(first * 4 + (place + k) % 4,), device_id_type=MESH
        )

    for k in range(1, 4):
        greet(layer, k)

    @pl.when(above)
    def _():
        for k in range(4):
            greet(layer + 1, k)

    @pl.when(below)
    def _():
        for k in range(4):
            greet(layer - 1, k)

    def wait_entry():
        peers = 3 + 4 * above.astype(jnp.int32) + 4 * below.astype(jnp.int32)
        pl.semaphore_wait(barrier, peers)

    def copy(step, group, spot, first, k):
        return pltpu.make_async_remote_copy(
            src_ref=messages[3 * step + group],
            dst_ref=landed[3 * step + group].at[spot],
            send_sem=send_sem.at[step, 4 * group + k],
            recv_sem=recv_sem.at[step, 4 * group + k],
            device_id=(first * 4 + (place + k) % 4,),
            device_id_type=MESH,
        )

    def send(step):
        @pl.when(above)
        def _():
            for k in range(4):
                copy(step, 1, place, layer + 1, k).start()

        @pl.when(below)
        def _():
            for k in range(4):
                copy(step, 2, place, layer - 1, k).start()

        for k in range(1, 4):
            copy(step, 0, place, layer, k).start()

    def receive(step):
        for k in range(1, 4):
            copy(step, 0, (place + 4 - k) % 4, layer, k).wait_recv()

        @pl.when(below)
        def _():
            for k in range(4):
                copy(step, 1, (place + 4 - k) % 4, layer - 1, k).wait_recv()

        @pl.when(above)
        def _():
            for k in range(4):
                copy(step, 2, (place + 4 - k) % 4, layer + 1, k).wait_recv()

    def finish(step):
        @pl.when(above)
        def _():
            for k in range(4):
                copy(step, 1, place, layer + 1, k).wait_send()

        @pl.when(below)
        def _():
            for k in range(4):
                copy(step, 2, place, layer - 1, k).wait_send()

        for k in range(1, 4):
            copy(step, 0, place, layer, k).wait_send()

    return wait_entry, send, receive, finish


VMEM = pl.BlockSpec(memory_space=pltpu.VMEM)
SMEM = pl.BlockSpec(memory_space=pltpu.SMEM)
STATE = jax.ShapeDtypeStruct((EDGE, 19, 8, 128), jnp.float32)


CHUNKS = ((0, 0, 10), (1, 0, 10), (0, 10, 19), (1, 10, 19))
CAPACITIES = (10, 12, 16)


def migrate_kernel(room, plan, old, out, *scratch):
    parts = len(CHUNKS)
    held, wanted, given, sorted_ = (scratch[parts * n : parts * n + parts] for n in range(4))
    own_sem, send_one, recv_one, send_two, recv_two, send_three, recv_three = scratch[4 * parts :]
    me = lax.axis_index("blocks")
    half, place = me // 16, me % 16
    partner = (1 - half) * 16 + place

    def peer(d):
        return (place + d) % 16

    def device(d):
        return (half * 16 + peer(d),)

    barrier = pltpu.get_barrier_semaphore()

    def greet(d, carry):
        pl.semaphore_signal(barrier, inc=1, device_id=device(d), device_id_type=MESH)
        return carry

    lax.fori_loop(1, 16, greet, 0)
    pl.semaphore_signal(barrier, inc=1, device_id=(partner,), device_id_type=MESH)
    pl.semaphore_wait(barrier, 16)

    def spread(k, d, owner):
        plane, low, high = CHUNKS[k]
        return pltpu.make_async_remote_copy(
            src_ref=old.at[low:high, pl.ds(pl.multiple_of(32 * peer(d) + 16 * plane, 16), 16)],
            dst_ref=held[k].at[owner],
            send_sem=send_one.at[k, d],
            recv_sem=recv_one.at[k, d],
            device_id=device(d),
            device_id_type=MESH,
        )

    def keep(k):
        plane, low, high = CHUNKS[k]
        return pltpu.make_async_copy(
            old.at[low:high, pl.ds(pl.multiple_of(32 * place + 16 * plane, 16), 16)],
            held[k].at[place],
            own_sem.at[k],
        )

    def swap(k):
        return pltpu.make_async_remote_copy(
            src_ref=wanted[k],
            dst_ref=given[k],
            send_sem=send_two.at[k],
            recv_sem=recv_two.at[k],
            device_id=(partner,),
            device_id_type=MESH,
        )

    def hand(k, d, owner):
        plane, low, high = CHUNKS[k]
        return pltpu.make_async_remote_copy(
            src_ref=sorted_[k].at[peer(d)],
            dst_ref=out.at[2 * owner + plane, low:high],
            send_sem=send_three.at[k, d],
            recv_sem=recv_three.at[k, d],
            device_id=device(d),
            device_id_type=MESH,
        )

    def each(body):
        def step(d, carry):
            body(d)
            return carry

        lax.fori_loop(1, 16, step, 0)

    def slot_of(k, slot):
        first = held[k][slot // 2, :, pl.ds(0, 8, stride=2), :]
        second = held[k][slot // 2, :, pl.ds(1, 8, stride=2), :]
        return jnp.where(slot % 2 > 0, second, first)

    def deliver(k):
        plane, low, high = CHUNKS[k]
        swap(k).wait_recv()

        def choose(b, carry):
            near, far = slot_of(k, plan[2, b]), given[k][plan[3, b]]
            sorted_[k][b] = jnp.where(plan[1, b] > 0, near, far)
            return carry

        lax.fori_loop(0, 16, choose, 0)
        each(lambda d: hand(k, d, place).start())
        out[2 * place + plane, low:high] = sorted_[k][place]

    def begin(k):
        keep(k).start()
        each(lambda d: spread(k, d, place).start())

    begin(0)
    begin(1)
    for k in range(parts):
        keep(k).wait()
        each(lambda d: spread(k, d, peer(16 - d)).wait_recv())

        def pick(e, carry):
            wanted[k][e] = slot_of(k, plan[0, e])
            return carry

        lax.fori_loop(0, room, pick, 0)
        swap(k).start()
        if k + 2 < parts:
            begin(k + 2)
        if k > 0:
            deliver(k - 1)
    deliver(parts - 1)
    for k in range(parts):
        each(lambda d: hand(k, d, peer(16 - d)).wait_recv())
    for k in range(parts):
        each(lambda d: spread(k, d, place).wait_send())
        swap(k).wait_send()
        each(lambda d: hand(k, d, place).wait_send())


def migrate_with(room, number, plan, old):
    parts = len(CHUNKS)

    def buffers(count, rows=8):
        return [pltpu.VMEM((count, high - low, rows, 128), jnp.float32) for _, low, high in CHUNKS]

    dma = pltpu.SemaphoreType.DMA
    return pl.pallas_call(
        functools.partial(migrate_kernel, room),
        out_shape=STATE,
        in_specs=[SMEM, pl.BlockSpec(memory_space=pl.ANY)],
        out_specs=VMEM,
        scratch_shapes=buffers(16, 16)
        + buffers(room)
        + buffers(room)
        + buffers(16)
        + [dma((parts,)), dma((parts, 16)), dma((parts, 16)), dma((parts,)), dma((parts,))]
        + [dma((parts, 16)), dma((parts, 16))],
        compiler_params=pltpu.CompilerParams(
            collective_id=number, has_side_effects=True, vmem_limit_bytes=40 * 2**20
        ),
    )(plan, old)


def plan_kernel(old_slot, plan, branch):
    half = lax.axis_index("blocks") // 16
    for e in range(16):
        plan[0, e] = 0

    def block(b, counts):
        slot = old_slot[b]
        source, target = slot >> 5, b >> 4
        crosses = (source != target).astype(jnp.int32)
        rank = jnp.where(target == 0, counts[0], counts[1])

        @pl.when(target == half)
        def _():
            plan[1, b & 15] = 1 - crosses
            plan[2, b & 15] = (slot & 31) * (1 - crosses)
            plan[3, b & 15] = rank * crosses

        @pl.when((source == half) & (target != half))
        def _():
            plan[0, rank] = slot & 31

        low = jnp.where(target == 0, crosses, 0)
        return counts[0] + low, counts[1] + crosses - low

    counts = lax.fori_loop(0, 32, block, (jnp.int32(0), jnp.int32(0)))
    most = jnp.maximum(counts[0], counts[1])
    branch[0] = sum((most > room).astype(jnp.int32) for room in CAPACITIES[:-1])


def migrate(old_pdfs, old_slot):
    peers = lax.axis_size("blocks")
    slots = old_pdfs.shape[0]
    blocks = old_slot.shape[0]
    if peers == EDGE and slots == 2:
        plan, branch = pl.pallas_call(
            plan_kernel,
            out_shape=[
                jax.ShapeDtypeStruct((4, 16), jnp.int32),
                jax.ShapeDtypeStruct((1,), jnp.int32),
            ],
            in_specs=[SMEM],
            out_specs=[SMEM, SMEM],
        )(old_slot)
        old = old_pdfs.reshape(slots, 19, 256, 128).transpose(1, 2, 0, 3).reshape(19, 512, 128)
        calls = [
            functools.partial(migrate_with, room, 1 + number)
            for number, room in enumerate(CAPACITIES)
        ]
        return lax.switch(branch[0], calls, plan, old)
    planes = 4
    tiles = pl.pallas_call(
        functools.partial(spread_kernel, planes, slots),
        grid=(EDGE // planes,),
        out_shape=jax.ShapeDtypeStruct((EDGE, slots * 152, 128), jnp.float32),
        in_specs=[pl.BlockSpec((slots, 19, planes * 1024), lambda g: (0, 0, g))],
        out_specs=pl.BlockSpec((planes, slots * 152, 128), lambda g: (g, 0, 0)),
        compiler_params=pltpu.CompilerParams(vmem_limit_bytes=58 * 2**20),
    )(old_pdfs)
    parts = peers // EDGE
    rows = 8 // parts
    if parts > 1:
        tiles = tiles.reshape(EDGE, slots * 19, parts, rows, 128).transpose(0, 2, 1, 3, 4)
        tiles = tiles.reshape(peers, slots * 19 * rows, 128)
    spread = lax.all_to_all(tiles, "blocks", split_axis=0, concat_axis=0, tiled=True)
    spread = spread.reshape(peers * slots, 19 * rows, 128)
    ordered = spread.at[old_slot].get(mode="promise_in_bounds")
    arrived = lax.all_to_all(ordered, "blocks", split_axis=0, concat_axis=0, tiled=True)
    if parts > 1:
        arrived = arrived.reshape(EDGE, parts, 19, rows, 128).transpose(0, 2, 1, 3, 4)
    return arrived.reshape(EDGE, 19, 8, 128)


def per_device(old_pdfs, old_slot, neighbours, cell_flags):
    state = migrate(old_pdfs, old_slot)
    flags = cell_flags.reshape(EDGE, 8, 128)
    layers = lax.axis_size("blocks") // 4

    def tiles(*lead):
        return pltpu.VMEM(lead + (8, 128), jnp.float32)

    out = pl.pallas_call(
        functools.partial(steps_kernel, layers),
        out_shape=jax.ShapeDtypeStruct((19, EDGE, 8, 128), jnp.float32),
        in_specs=[SMEM, VMEM, VMEM],
        out_specs=VMEM,
        scratch_shapes=[tiles(EDGE, 19)] * 2
        + [tiles(10), tiles(5), tiles(5)] * STEPS
        + [tiles(4, 10), tiles(4, 5), tiles(4, 5)] * STEPS
        + [
            pltpu.VMEM((5, EDGE, 128), jnp.float32),
            pltpu.VMEM((5, EDGE + 8, 128), jnp.float32),
            pltpu.SemaphoreType.DMA((STEPS, 12)),
            pltpu.SemaphoreType.DMA((STEPS, 12)),
        ],
        compiler_params=pltpu.CompilerParams(
            collective_id=0, has_side_effects=True, vmem_limit_bytes=40 * 2**20
        ),
    )(neighbours, flags, state)
    return out.reshape(1, 19, EDGE * EDGE * EDGE)


def solution(mesh):
    in_specs = (P("blocks", None, None), P(), P("blocks", None), P("blocks", None))
    out_specs = P("blocks", None, None)
    return jax.shard_map(
        per_device, mesh=mesh, in_specs=in_specs, out_specs=out_specs, check_vma=False
    )
```

```python
import functools

import jax
import jax.numpy as jnp
import numpy as np
from jax import lax
from jax.experimental import pallas as pl
from jax.experimental.pallas import tpu as pltpu
from jax.sharding import PartitionSpec as P

EDGE = 32
STEPS = 2
MESH = pl.DeviceIdType.MESH

VELOCITY = (
    (0, 0, 0),
    (1, 0, 0),
    (-1, 0, 0),
    (0, 1, 0),
    (0, -1, 0),
    (0, 0, 1),
    (0, 0, -1),
    (1, 1, 0),
    (-1, -1, 0),
    (1, -1, 0),
    (-1, 1, 0),
    (1, 0, 1),
    (-1, 0, -1),
    (1, 0, -1),
    (-1, 0, 1),
    (0, 1, 1),
    (0, -1, -1),
    (0, 1, -1),
    (0, -1, 1),
)
WEIGHT_LIST = (1.0 / 3.0,) + (1.0 / 18.0,) * 6 + (1.0 / 36.0,) * 12
RELAXATION = (
    0.0,
    0.0,
    0.0,
    0.0,
    1.19,
    1.4,
    1.2,
    1.2,
    1.2,
    1.6,
    1.6,
    1.6,
    1.6,
    1.6,
    1.4,
    1.4,
    1.98,
    1.98,
    1.98,
)
INLET_SPEED = (0.0, 0.0, 0.05)

X_PLUS, X_MINUS = (1, 7, 9, 11, 13), (2, 8, 10, 12, 14)
Y_PLUS, Y_MINUS = (3, 7, 10, 15, 17), (4, 8, 9, 16, 18)
Z_PLUS, Z_MINUS = (5, 11, 14, 15, 18), (6, 12, 13, 16, 17)
ORBITS = ((0,), (1, 2), (3, 4), (5, 6), (7, 8, 9, 10), (11, 12, 13, 14), (15, 16, 17, 18))


def collision_table():
    lattice = np.array(VELOCITY) * 1.0
    along_x, along_y, along_z = (lattice[:, 0], lattice[:, 1], lattice[:, 2])
    squared = along_x * along_x + along_y * along_y + along_z * along_z
    monomials = [
        np.ones(19),
        along_x,
        along_y,
        along_z,
        squared,
        squared * squared,
        squared * along_x,
        squared * along_y,
        squared * along_z,
        3.0 * along_x * along_x - squared,
        along_y * along_y - along_z * along_z,
        along_x * along_y,
        along_y * along_z,
        along_x * along_z,
        squared * (3.0 * along_x * along_x - squared),
        squared * (along_y * along_y - along_z * along_z),
        (along_y * along_y - along_z * along_z) * along_x,
        (along_z * along_z - along_x * along_x) * along_y,
        (along_x * along_x - along_y * along_y) * along_z,
    ]
    orthonormal = []
    for vector in monomials:
        for earlier in orthonormal:
            vector = vector - np.dot(vector, earlier) * earlier
        orthonormal.append(vector / np.sqrt(np.dot(vector, vector)))
    stacked = np.stack(orthonormal)
    return stacked.T * np.array(RELAXATION) @ stacked


def opposite(index_value):
    if index_value == 0:
        return 0
    return index_value + 1 if index_value % 2 == 1 else index_value - 1


def code_of(offset):
    return VELOCITY.index(tuple(offset)) - 1


def collision_blocks():
    matrix = collision_table().astype(np.float32).astype(np.float64)
    even = [[float(np.mean([matrix[a[0], b] for b in group])) for group in ORBITS] for a in ORBITS]
    odd = []
    for axis in range(3):
        groups = [g for g in ORBITS if any(VELOCITY[b][axis] for b in g)]
        rows = []
        for a in groups:
            first = next(c for c in a if VELOCITY[c][axis] > 0)
            rows.append(
                [float(np.mean([VELOCITY[b][axis] * matrix[first, b] for b in g])) for g in groups]
            )
        odd.append(rows)
    mixed = []
    for group in ORBITS[4:]:
        signs = [1.0, 1.0, -1.0, -1.0]
        mixed.append(float(np.mean([s * matrix[group[0], b] for s, b in zip(signs, group)])))
    return even, odd, mixed


def dot(coefficients, terms):
    total = None
    for coefficient, term in zip(coefficients, terms):
        part = term * np.float32(coefficient)
        total = part if total is None else total + part
    return total


def collide(f):
    even, odd, mixed = collision_blocks()
    pair_sum = [f[i] + f[i + 1] for i in (1, 3, 5)]
    pair_dif = [f[i] - f[i + 1] for i in (1, 3, 5)]
    quad_sum, quad_mix, quad_one, quad_two = [], [], [], []
    for i in (7, 11, 15):
        sum_a, sum_b = f[i] + f[i + 1], f[i + 2] + f[i + 3]
        dif_a, dif_b = f[i] - f[i + 1], f[i + 2] - f[i + 3]
        quad_sum.append(sum_a + sum_b)
        quad_mix.append(sum_a - sum_b)
        quad_one.append(dif_a + dif_b)
        quad_two.append(dif_a - dif_b)
    odd_terms = [
        [pair_dif[0], quad_one[0], quad_one[1]],
        [pair_dif[1], quad_two[0], quad_one[2]],
        [pair_dif[2], quad_two[1], quad_two[2]],
    ]
    rho = f[0] + (pair_sum[0] + pair_sum[1] + pair_sum[2]) + (quad_sum[0] + quad_sum[1] + quad_sum[2])
    j = [t[0] + t[1] + t[2] for t in odd_terms]
    sq = [c * c for c in j]
    base = rho - 1.5 * (sq[0] + sq[1] + sq[2])
    sq45 = [4.5 * s for s in sq]
    w0, w1, w2 = 1.0 / 3.0, 1.0 / 18.0, 1.0 / 36.0
    even_terms = [f[0] - w0 * base]
    for a in range(3):
        even_terms.append(pair_sum[a] - (2.0 * w1) * (base + sq45[a]))
    for q, (a, b) in enumerate(((0, 1), (0, 2), (1, 2))):
        even_terms.append(quad_sum[q] - (4.0 * w2) * (base + sq45[a] + sq45[b]))
    mix = [
        (quad_mix[q] - j[a] * j[b]) * np.float32(mixed[q])
        for q, (a, b) in enumerate(((0, 1), (0, 2), (1, 2)))
    ]
    odd_out = []
    for a in range(3):
        third = j[a] * np.float32(1.0 / 3.0)
        terms = [t - third for t in odd_terms[a]]
        odd_out.append([dot(row, terms) for row in odd[a]])
    even_out = [dot(row, even_terms) for row in even]
    out = [f[0] - even_out[0]]
    for a in range(3):
        out.append(f[1 + 2 * a] - (even_out[1 + a] + odd_out[a][0]))
        out.append(f[2 + 2 * a] - (even_out[1 + a] - odd_out[a][0]))
    for q, (one, two) in enumerate(
        (
            (odd_out[0][1], odd_out[1][1]),
            (odd_out[0][2], odd_out[2][1]),
            (odd_out[1][2], odd_out[2][2]),
        )
    ):
        i = 7 + 4 * q
        plus, minus = even_out[4 + q] + mix[q], even_out[4 + q] - mix[q]
        both, apart = one + two, one - two
        out.append(f[i] - (plus + both))
        out.append(f[i + 1] - (plus - both))
        out.append(f[i + 2] - (minus + apart))
        out.append(f[i + 3] - (minus - apart))
    return out


def positions():
    lane = lax.broadcasted_iota(jnp.int32, (8, 128), 1)
    sub = lax.broadcasted_iota(jnp.int32, (8, 128), 0)
    return lane, sub


def shift_y(v, step, ghost, lane, sub):
    if step > 0:
        moved = pltpu.roll(v, 32, 1)
        out = jnp.where(lane < 32, pltpu.roll(moved, 1, 0), moved)
        return jnp.where((lane < 32) & (sub == 0), ghost, out)
    moved = pltpu.roll(v, 96, 1)
    out = jnp.where(lane >= 96, pltpu.roll(moved, 7, 0), moved)
    return jnp.where((lane >= 96) & (sub == 7), ghost, out)


def shift_z(v, step, ghost, z):
    moved = pltpu.roll(v, 1 if step > 0 else 127, 1)
    return jnp.where(z == (0 if step > 0 else 31), ghost, moved)


def unpack_ghosts(nbr, rxy, gy):
    lane, _ = positions()
    jy = jnp.maximum(nbr[0, 2], nbr[0, 3]) & 3
    jd = jnp.maximum(jnp.maximum(nbr[0, 6], nbr[0, 7]), jnp.maximum(nbr[0, 8], nbr[0, 9])) & 3
    for k in range(5):
        packed = rxy[jy, 5 + k]
        for g in range(4):
            low = pltpu.roll(packed, (128 - 32 * g) % 128, 1)
            high = pltpu.roll(packed, (96 - 32 * g) % 128, 1)
            gy[k, 1 + 8 * g : 9 + 8 * g, :] = jnp.where(lane < 64, low, high)
    for channel in (7, 8, 9, 10):
        cx, cy, _ = VELOCITY[channel]
        kx = (X_PLUS if cx > 0 else X_MINUS).index(channel)
        ky = (Y_PLUS if cy > 0 else Y_MINUS).index(channel)
        plane = rxy[jd, kx]
        row = pltpu.roll(plane, 32 if cy > 0 else 96, 1)
        row = row[7:8, :] if cy > 0 else row[0:1, :]
        spot = 0 if cx > 0 else 33
        gy[ky, spot : spot + 1, :] = row


def pull(x, nbr, c, rxy, rb, ra, flags, gy):
    lane, sub = positions()
    z = lane & 31
    jx = jnp.maximum(nbr[0, 0], nbr[0, 1]) & 3

    def wall(offset):
        return jnp.where(nbr[0, code_of(offset)] >= 0, 0, 1).astype(jnp.int32)

    def spot(offset):
        return nbr[0, code_of(offset)] & 3

    own = flags[x]
    values = [c[x, i] for i in range(19)]
    j = []
    for axis in range(3):
        plus = sum(values[i] for i in range(19) if VELOCITY[i][axis] > 0)
        minus = sum(values[i] for i in range(19) if VELOCITY[i][axis] < 0)
        j.append(plus - minus)
    calm = 1.0 - 1.5 * (j[0] * j[0] + j[1] * j[1] + j[2] * j[2])
    inlet_square = sum(p * p for p in INLET_SPEED)
    out = [jnp.where(own == 0, values[0], 0.0)]
    for i in range(1, 19):
        cx, cy, cz = VELOCITY[i]
        if cx:
            outside = x == (0 if cx > 0 else EDGE - 1)
            from_x = jnp.clip(x - cx, 0, EDGE - 1)
            kx = (X_PLUS if cx > 0 else X_MINUS).index(i)
            v = jnp.where(outside, rxy[jx, kx], c[from_x, i])
            kind = jnp.where(outside, wall((-cx, 0, 0)), flags[from_x])
        else:
            v, kind = values[i], own
        if cz:
            beyond = rb if cz > 0 else ra
            kz = (Z_PLUS if cz > 0 else Z_MINUS).index(i)
            block, blocked = spot((0, 0, -cz)), wall((0, 0, -cz))
            at = x
            if cx:
                block = jnp.where(outside, spot((-cx, 0, -cz)), block)
                blocked = jnp.where(outside, wall((-cx, 0, -cz)), blocked)
                at = (x - cx) & 31
            message = beyond[block, kz]
            amount = (128 - at) & 127 if cz > 0 else 31 - at
            v = shift_z(v, cz, pltpu.roll(message, amount, 1), z)
            kind = shift_z(kind, cz, blocked, z)
        if cy:
            ky = (Y_PLUS if cy > 0 else Y_MINUS).index(i)
            row = jnp.broadcast_to(gy[ky, pl.ds(x - cx + 1, 1), :], (8, 128))
            blocked = wall((0, -cy, 0))
            if cx:
                blocked = jnp.where(outside, wall((-cx, -cy, 0)), blocked)
            if cz:
                corner = beyond[spot((0, -cy, -cz)), kz]
                target = (0 if cy > 0 else 96) + (0 if cz > 0 else 31)
                source = (96 if cy > 0 else 0) + x
                corner = pltpu.roll(corner, (target - source + 256) & 127, 1)
                corner = corner[7:8, :] if cy > 0 else corner[0:1, :]
                row = shift_z(row, cz, jnp.broadcast_to(corner, (8, 128)), z)
                blocked = jnp.where(z == (0 if cz > 0 else 31), wall((0, -cy, -cz)), blocked)
            v = shift_y(v, cy, row, lane, sub)
            kind = shift_y(kind, cy, blocked, lane, sub)
        weight = WEIGHT_LIST[i]
        along = sum(a * b for a, b in zip(VELOCITY[i], INLET_SPEED))
        inlet = weight * (1.0 + 3.0 * along + 4.5 * along * along - 1.5 * inlet_square)
        speed = sum(a * b for a, b in zip(VELOCITY[i], j) if a)
        outlet = weight * (calm + speed * (3.0 + 4.5 * speed))
        new = jnp.where(
            kind == 0,
            v,
            jnp.where(kind == 1, values[opposite(i)], jnp.where(kind == 2, np.float32(inlet), outlet)),
        )
        out.append(jnp.where(own == 0, new, 0.0))
    return out


def note_faces(x, nbr, collided, zu, zd, rows):
    lane, _ = positions()
    here = (lane & 31) == x
    for k in range(5):
        up = pltpu.roll(collided[Z_PLUS[k]], (x + 97) & 127, 1)
        zu[k] = jnp.where(here, up, zu[k])
        zd[k] = jnp.where(here, pltpu.roll(collided[Z_MINUS[k]], x, 1), zd[k])
        high = collided[Y_PLUS[k]][7:8, :]
        low = collided[Y_MINUS[k]][0:1, :]
        rows[k, pl.ds(x, 1), :] = jnp.where(nbr[0, 2] >= 0, high, low)


def finish_faces(nbr, c, rows, xy):
    lane, _ = positions()
    ahead_x, ahead_y = nbr[0, 0] >= 0, nbr[0, 2] >= 0
    for k in range(5):
        xy[k] = jnp.where(ahead_x, c[EDGE - 1, X_PLUS[k]], c[0, X_MINUS[k]])
        packed = jnp.zeros((8, 128), jnp.float32)
        for g in range(4):
            part = rows[k, 8 * g : 8 * g + 8, :]
            high = pltpu.roll(part, (32 * (g + 1)) % 128, 1)
            low = pltpu.roll(part, 32 * g, 1)
            packed = jnp.where((lane >> 5) == g, jnp.where(ahead_y, high, low), packed)
        xy[5 + k] = packed


def steps_kernel(layers, nbr, flags, f, out, *scratch):
    c, messages, landed = scratch[:2], scratch[2 : 2 + 3 * STEPS], scratch[2 + 3 * STEPS : 2 + 6 * STEPS]
    rows, gy, send_sem, recv_sem = scratch[2 + 6 * STEPS :]
    wait_entry, send, receive, finish = exchanges(layers, messages, landed, send_sem, recv_sem)
    for step in range(STEPS):
        now, before = c[step % 2], c[(step + 1) % 2]
        xy, zu, zd = messages[3 * step : 3 * step + 3]
        zu[...] = jnp.zeros_like(zu)
        zd[...] = jnp.zeros_like(zd)
        if step > 0:
            rxy, rb, ra = landed[3 * step - 3 : 3 * step]
            unpack_ghosts(nbr, rxy, gy)

        def plane(x, carry):
            if step == 0:
                old = [f[x, i] for i in range(19)]
            else:
                old = pull(x, nbr, before, rxy, rb, ra, flags, gy)
            collided = collide(old)
            for i in range(19):
                now[x, i] = collided[i]
            note_faces(x, nbr, collided, zu, zd, rows)
            return carry

        lax.fori_loop(0, EDGE, plane, 0)
        finish_faces(nbr, now, rows, xy)
        if step == 0:
            wait_entry()
        send(step)
        receive(step)
    rxy, rb, ra = landed[3 * STEPS - 3 :]
    unpack_ghosts(nbr, rxy, gy)

    def last_plane(x, carry):
        new = pull(x, nbr, now, rxy, rb, ra, flags, gy)
        for i in range(19):
            out[i, x] = new[i]
        return carry

    lax.fori_loop(0, EDGE, last_plane, 0)
    for step in range(STEPS):
        finish(step)


def spread_kernel(planes, slots, old, out):
    def plane(x, carry):
        for slot in range(slots):
            for s in range(8):
                at = pl.multiple_of(x * 1024 + s * 128, 128)
                out[x, pl.ds(slot * 152 + s, 19, stride=8), :] = old[slot, :, pl.ds(at, 128)]
        return carry

    lax.fori_loop(0, planes, plane, 0)


def exchanges(layers, messages, landed, send_sem, recv_sem):
    me = lax.axis_index("blocks")
    layer, place = me // 4, me % 4
    above, below = layer + 1 < layers, layer > 0
    barrier = pltpu.get_barrier_semaphore()

    def greet(first, k):
        pl.semaphore_signal(
            barrier, inc=1, device_id=(first * 4 + (place + k) % 4,), device_id_type=MESH
        )

    for k in range(1, 4):
        greet(layer, k)

    @pl.when(above)
    def _():
        for k in range(4):
            greet(layer + 1, k)

    @pl.when(below)
    def _():
        for k in range(4):
            greet(layer - 1, k)

    def wait_entry():
        peers = 3 + 4 * above.astype(jnp.int32) + 4 * below.astype(jnp.int32)
        pl.semaphore_wait(barrier, peers)

    def copy(step, group, spot, first, k):
        return pltpu.make_async_remote_copy(
            src_ref=messages[3 * step + group],
            dst_ref=landed[3 * step + group].at[spot],
            send_sem=send_sem.at[step, 4 * group + k],
            recv_sem=recv_sem.at[step, 4 * group + k],
            device_id=(first * 4 + (place + k) % 4,),
            device_id_type=MESH,
        )

    def send(step):
        @pl.when(above)
        def _():
            for k in range(4):
                copy(step, 1, place, layer + 1, k).start()

        @pl.when(below)
        def _():
            for k in range(4):
                copy(step, 2, place, layer - 1, k).start()

        for k in range(1, 4):
            copy(step, 0, place, layer, k).start()

    def receive(step):
        for k in range(1, 4):
            copy(step, 0, (place + 4 - k) % 4, layer, k).wait_recv()

        @pl.when(below)
        def _():
            for k in range(4):
                copy(step, 1, (place + 4 - k) % 4, layer - 1, k).wait_recv()

        @pl.when(above)
        def _():
            for k in range(4):
                copy(step, 2, (place + 4 - k) % 4, layer + 1, k).wait_recv()

    def finish(step):
        @pl.when(above)
        def _():
            for k in range(4):
                copy(step, 1, place, layer + 1, k).wait_send()

        @pl.when(below)
        def _():
            for k in range(4):
                copy(step, 2, place, layer - 1, k).wait_send()

        for k in range(1, 4):
            copy(step, 0, place, layer, k).wait_send()

    return wait_entry, send, receive, finish


VMEM = pl.BlockSpec(memory_space=pltpu.VMEM)
SMEM = pl.BlockSpec(memory_space=pltpu.SMEM)
STATE = jax.ShapeDtypeStruct((EDGE, 19, 8, 128), jnp.float32)


CHUNKS = tuple((plane, low, high) for low, high in ((0, 10), (10, 19)) for plane in range(4))
CAPACITIES = (9, 10, 12, 16)
AHEAD = 3


def migrate_kernel(room, levels, plan, old, out, *scratch):
    parts = len(CHUNKS)
    held, up_out, up_in, down_out, down_in, sorted_ = (
        scratch[parts * n : parts * n + parts] for n in range(6)
    )
    sems = scratch[6 * parts :]
    own_sem, send_up, recv_up, send_down, recv_down = sems[:5]
    send_one, recv_one, send_three, recv_three = sems[5:]
    me = lax.axis_index("blocks")
    level, place = me // 8, me % 8
    above, below = level + 1 < levels, level > 0

    def peer(d):
        return (place + d) % 8

    def device(d):
        return (level * 8 + peer(d),)

    barrier = pltpu.get_barrier_semaphore()

    def greet(target):
        pl.semaphore_signal(barrier, inc=1, device_id=target, device_id_type=MESH)

    def each(body):
        def step(d, carry):
            body(d)
            return carry

        lax.fori_loop(1, 8, step, 0)

    each(lambda d: greet(device(d)))

    @pl.when(above)
    def _():
        greet((me + 8,))

    @pl.when(below)
    def _():
        greet((me - 8,))

    pl.semaphore_wait(barrier, 7 + above.astype(jnp.int32) + below.astype(jnp.int32))

    def piece(k, owner):
        plane, low, high = CHUNKS[k]
        return old.at[low:high, pl.ds(pl.multiple_of(64 * owner + 16 * plane, 16), 16)]

    def spread(k, d, owner):
        return pltpu.make_async_remote_copy(
            src_ref=piece(k, peer(d)),
            dst_ref=held[k].at[owner],
            send_sem=send_one.at[k, d],
            recv_sem=recv_one.at[k, d],
            device_id=device(d),
            device_id_type=MESH,
        )

    def keep(k):
        return pltpu.make_async_copy(piece(k, place), held[k].at[place], own_sem.at[k])

    def rise(k, target):
        return pltpu.make_async_remote_copy(
            src_ref=up_out[k],
            dst_ref=up_in[k],
            send_sem=send_up.at[k],
            recv_sem=recv_up.at[k],
            device_id=(target,),
            device_id_type=MESH,
        )

    def sink(k, target):
        return pltpu.make_async_remote_copy(
            src_ref=down_out[k],
            dst_ref=down_in[k],
            send_sem=send_down.at[k],
            recv_sem=recv_down.at[k],
            device_id=(target,),
            device_id_type=MESH,
        )

    def hand(k, d, owner):
        plane, low, high = CHUNKS[k]
        return pltpu.make_async_remote_copy(
            src_ref=sorted_[k].at[peer(d)],
            dst_ref=out.at[4 * owner + plane, low:high],
            send_sem=send_three.at[k, d],
            recv_sem=recv_three.at[k, d],
            device_id=device(d),
            device_id_type=MESH,
        )

    def slot_of(k, slot):
        first = held[k][slot // 2, :, pl.ds(0, 8, stride=2), :]
        second = held[k][slot // 2, :, pl.ds(1, 8, stride=2), :]
        return jnp.where(slot % 2 > 0, second, first)

    def go_up(k, wait):
        if wait:
            rise(k, me - 8).wait_recv()

        def pick(e, carry):
            new = slot_of(k, plan[1, e])
            up_out[k][e] = jnp.where(plan[0, e] > 0, up_in[k][plan[2, e]], new) if wait else new
            return carry

        lax.fori_loop(0, room, pick, 0)
        rise(k, me + 8).start()

    def go_down(k, wait):
        if wait:
            sink(k, me + 8).wait_recv()

        def pick(e, carry):
            new = slot_of(k, plan[4, e])
            down_out[k][e] = jnp.where(plan[3, e] > 0, down_in[k][plan[5, e]], new) if wait else new
            return carry

        lax.fori_loop(0, room, pick, 0)
        sink(k, me - 8).start()

    def deliver(k):
        plane, low, high = CHUNKS[k]

        @pl.when(level == levels - 1)
        def _():
            rise(k, me - 8).wait_recv()

        @pl.when(level == 0)
        def _():
            sink(k, me + 8).wait_recv()

        def choose(b, carry):
            kind = plan[6, b]
            value = jnp.where(kind == 1, up_in[k][plan[8, b]], down_in[k][plan[8, b]])
            sorted_[k][b] = jnp.where(kind == 0, slot_of(k, plan[7, b]), value)
            return carry

        lax.fori_loop(0, 8, choose, 0)
        each(lambda d: hand(k, d, place).start())
        out[4 * place + plane, low:high] = sorted_[k][place]

    def begin(k):
        keep(k).start()
        each(lambda d: spread(k, d, place).start())

    for k in range(AHEAD):
        begin(k)
    for turn in range(parts + levels - 1):
        if turn < parts:
            keep(turn).wait()
            each(lambda d: spread(turn, d, peer(8 - d)).wait_recv())
            if turn + AHEAD < parts:
                begin(turn + AHEAD)
        for lag in range(levels - 1):
            if 0 <= turn - lag < parts:

                @pl.when(level == lag)
                def _():
                    go_up(turn - lag, lag > 0)

                @pl.when(level == levels - 1 - lag)
                def _():
                    go_down(turn - lag, lag > 0)

        if turn >= levels - 1:
            deliver(turn - levels + 1)
    for k in range(parts):
        each(lambda d: hand(k, d, peer(8 - d)).wait_recv())
    for k in range(parts):
        each(lambda d: spread(k, d, place).wait_send())
        each(lambda d: hand(k, d, place).wait_send())

        @pl.when(above)
        def _():
            rise(k, me + 8).wait_send()

        @pl.when(below)
        def _():
            sink(k, me - 8).wait_send()


def migrate_with(room, number, plan, old):
    parts = len(CHUNKS)

    def buffers(count, rows=8):
        return [pltpu.VMEM((count, high - low, rows, 128), jnp.float32) for _, low, high in CHUNKS]

    dma = pltpu.SemaphoreType.DMA
    return pl.pallas_call(
        functools.partial(migrate_kernel, room, lax.axis_size("blocks") // 8),
        out_shape=STATE,
        in_specs=[SMEM, pl.BlockSpec(memory_space=pl.ANY)],
        out_specs=VMEM,
        scratch_shapes=buffers(8, 16)
        + buffers(room) * 4
        + buffers(8)
        + [dma((parts,))] * 5
        + [dma((parts, 8))] * 4,
        compiler_params=pltpu.CompilerParams(
            collective_id=number, has_side_effects=True, vmem_limit_bytes=48 * 2**20
        ),
    )(plan, old)


def plan_kernel(levels, old_slot, plan, branch):
    level = lax.axis_index("blocks") // 8
    for row in range(9):
        for e in range(16):
            plan[row, e] = 0

    def select(values, which):
        return sum(jnp.where(which == n, value, 0) for n, value in enumerate(values))

    def block(b, counts):
        ups, downs = counts
        slot = old_slot[b]
        source, target = slot // 16, b // 8
        local = slot % 16

        @pl.when((source <= level) & (target > level))
        def _():
            at = select(ups, level)
            plan[0, at] = (source < level).astype(jnp.int32)
            plan[1, at] = jnp.where(source == level, local, 0)
            plan[2, at] = jnp.where(source < level, select(ups, level - 1), 0)

        @pl.when((source >= level) & (target < level))
        def _():
            at = select(downs, level - 1)
            plan[3, at] = (source > level).astype(jnp.int32)
            plan[4, at] = jnp.where(source == level, local, 0)
            plan[5, at] = jnp.where(source > level, select(downs, level), 0)

        @pl.when(target == level)
        def _():
            at = b % 8
            rank = jnp.where(source < level, select(ups, level - 1), select(downs, level))
            plan[6, at] = jnp.where(source == level, 0, jnp.where(source < level, 1, 2))
            plan[7, at] = jnp.where(source == level, local, 0)
            plan[8, at] = jnp.where(source == level, 0, rank)

        ups = tuple(
            count + ((source <= n) & (target > n)).astype(jnp.int32) for n, count in enumerate(ups)
        )
        downs = tuple(
            count + ((source > n) & (target <= n)).astype(jnp.int32)
            for n, count in enumerate(downs)
        )
        return ups, downs

    zeros = (jnp.int32(0),) * (levels - 1)
    ups, downs = lax.fori_loop(0, 8 * levels, block, (zeros, zeros))
    most = functools.reduce(jnp.maximum, ups + downs)
    branch[0] = sum((most > room).astype(jnp.int32) for room in CAPACITIES[:-1])


def migrate(old_pdfs, old_slot):
    peers = lax.axis_size("blocks")
    slots = old_pdfs.shape[0]
    blocks = old_slot.shape[0]
    if peers == EDGE and slots == 2:
        plan, branch = pl.pallas_call(
            functools.partial(plan_kernel, peers // 8),
            out_shape=[
                jax.ShapeDtypeStruct((9, 16), jnp.int32),
                jax.ShapeDtypeStruct((1,), jnp.int32),
            ],
            in_specs=[SMEM],
            out_specs=[SMEM, SMEM],
        )(old_slot)
        old = old_pdfs.reshape(slots, 19, 256, 128).transpose(1, 2, 0, 3).reshape(19, 512, 128)
        calls = [
            functools.partial(migrate_with, room, 1 + number)
            for number, room in enumerate(CAPACITIES)
        ]
        return lax.switch(branch[0], calls, plan, old)
    planes = 4
    tiles = pl.pallas_call(
        functools.partial(spread_kernel, planes, slots),
        grid=(EDGE // planes,),
        out_shape=jax.ShapeDtypeStruct((EDGE, slots * 152, 128), jnp.float32),
        in_specs=[pl.BlockSpec((slots, 19, planes * 1024), lambda g: (0, 0, g))],
        out_specs=pl.BlockSpec((planes, slots * 152, 128), lambda g: (g, 0, 0)),
        compiler_params=pltpu.CompilerParams(vmem_limit_bytes=58 * 2**20),
    )(old_pdfs)
    parts = peers // EDGE
    rows = 8 // parts
    if parts > 1:
        tiles = tiles.reshape(EDGE, slots * 19, parts, rows, 128).transpose(0, 2, 1, 3, 4)
        tiles = tiles.reshape(peers, slots * 19 * rows, 128)
    spread = lax.all_to_all(tiles, "blocks", split_axis=0, concat_axis=0, tiled=True)
    spread = spread.reshape(peers * slots, 19 * rows, 128)
    ordered = spread.at[old_slot].get(mode="promise_in_bounds")
    arrived = lax.all_to_all(ordered, "blocks", split_axis=0, concat_axis=0, tiled=True)
    if parts > 1:
        arrived = arrived.reshape(EDGE, parts, 19, rows, 128).transpose(0, 2, 1, 3, 4)
    return arrived.reshape(EDGE, 19, 8, 128)


def per_device(old_pdfs, old_slot, neighbours, cell_flags):
    state = migrate(old_pdfs, old_slot)
    flags = cell_flags.reshape(EDGE, 8, 128)
    layers = lax.axis_size("blocks") // 4

    def tiles(*lead):
        return pltpu.VMEM(lead + (8, 128), jnp.float32)

    out = pl.pallas_call(
        functools.partial(steps_kernel, layers),
        out_shape=jax.ShapeDtypeStruct((19, EDGE, 8, 128), jnp.float32),
        in_specs=[SMEM, VMEM, VMEM],
        out_specs=VMEM,
        scratch_shapes=[tiles(EDGE, 19)] * 2
        + [tiles(10), tiles(5), tiles(5)] * STEPS
        + [tiles(4, 10), tiles(4, 5), tiles(4, 5)] * STEPS
        + [
            pltpu.VMEM((5, EDGE, 128), jnp.float32),
            pltpu.VMEM((5, EDGE + 8, 128), jnp.float32),
            pltpu.SemaphoreType.DMA((STEPS, 12)),
            pltpu.SemaphoreType.DMA((STEPS, 12)),
        ],
        compiler_params=pltpu.CompilerParams(
            collective_id=0, has_side_effects=True, vmem_limit_bytes=40 * 2**20
        ),
    )(neighbours, flags, state)
    return out.reshape(1, 19, EDGE * EDGE * EDGE)


def solution(mesh):
    in_specs = (P("blocks", None, None), P(), P("blocks", None), P("blocks", None))
    out_specs = P("blocks", None, None)
    return jax.shard_map(
        per_device, mesh=mesh, in_specs=in_specs, out_specs=out_specs, check_vma=False
    )
```

```python
import functools

import jax
import jax.numpy as jnp
import numpy as np
from jax import lax
from jax.experimental import pallas as pl
from jax.experimental.pallas import tpu as pltpu
from jax.sharding import PartitionSpec as P

EDGE = 32
STEPS = 2
MESH = pl.DeviceIdType.MESH

VELOCITY = (
    (0, 0, 0),
    (1, 0, 0),
    (-1, 0, 0),
    (0, 1, 0),
    (0, -1, 0),
    (0, 0, 1),
    (0, 0, -1),
    (1, 1, 0),
    (-1, -1, 0),
    (1, -1, 0),
    (-1, 1, 0),
    (1, 0, 1),
    (-1, 0, -1),
    (1, 0, -1),
    (-1, 0, 1),
    (0, 1, 1),
    (0, -1, -1),
    (0, 1, -1),
    (0, -1, 1),
)
WEIGHT_LIST = (1.0 / 3.0,) + (1.0 / 18.0,) * 6 + (1.0 / 36.0,) * 12
RELAXATION = (
    0.0,
    0.0,
    0.0,
    0.0,
    1.19,
    1.4,
    1.2,
    1.2,
    1.2,
    1.6,
    1.6,
    1.6,
    1.6,
    1.6,
    1.4,
    1.4,
    1.98,
    1.98,
    1.98,
)
INLET_SPEED = (0.0, 0.0, 0.05)

X_PLUS, X_MINUS = (1, 7, 9, 11, 13), (2, 8, 10, 12, 14)
Y_PLUS, Y_MINUS = (3, 7, 10, 15, 17), (4, 8, 9, 16, 18)
Z_PLUS, Z_MINUS = (5, 11, 14, 15, 18), (6, 12, 13, 16, 17)
ORBITS = ((0,), (1, 2), (3, 4), (5, 6), (7, 8, 9, 10), (11, 12, 13, 14), (15, 16, 17, 18))


def collision_table():
    lattice = np.array(VELOCITY) * 1.0
    along_x, along_y, along_z = (lattice[:, 0], lattice[:, 1], lattice[:, 2])
    squared = along_x * along_x + along_y * along_y + along_z * along_z
    monomials = [
        np.ones(19),
        along_x,
        along_y,
        along_z,
        squared,
        squared * squared,
        squared * along_x,
        squared * along_y,
        squared * along_z,
        3.0 * along_x * along_x - squared,
        along_y * along_y - along_z * along_z,
        along_x * along_y,
        along_y * along_z,
        along_x * along_z,
        squared * (3.0 * along_x * along_x - squared),
        squared * (along_y * along_y - along_z * along_z),
        (along_y * along_y - along_z * along_z) * along_x,
        (along_z * along_z - along_x * along_x) * along_y,
        (along_x * along_x - along_y * along_y) * along_z,
    ]
    orthonormal = []
    for vector in monomials:
        for earlier in orthonormal:
            vector = vector - np.dot(vector, earlier) * earlier
        orthonormal.append(vector / np.sqrt(np.dot(vector, vector)))
    stacked = np.stack(orthonormal)
    return stacked.T * np.array(RELAXATION) @ stacked


def opposite(index_value):
    if index_value == 0:
        return 0
    return index_value + 1 if index_value % 2 == 1 else index_value - 1


def code_of(offset):
    return VELOCITY.index(tuple(offset)) - 1


def collision_blocks():
    matrix = collision_table().astype(np.float32).astype(np.float64)
    even = [[float(np.mean([matrix[a[0], b] for b in group])) for group in ORBITS] for a in ORBITS]
    odd = []
    for axis in range(3):
        groups = [g for g in ORBITS if any(VELOCITY[b][axis] for b in g)]
        rows = []
        for a in groups:
            first = next(c for c in a if VELOCITY[c][axis] > 0)
            rows.append(
                [float(np.mean([VELOCITY[b][axis] * matrix[first, b] for b in g])) for g in groups]
            )
        odd.append(rows)
    mixed = []
    for group in ORBITS[4:]:
        signs = [1.0, 1.0, -1.0, -1.0]
        mixed.append(float(np.mean([s * matrix[group[0], b] for s, b in zip(signs, group)])))
    return even, odd, mixed


def dot(coefficients, terms):
    total = None
    for coefficient, term in zip(coefficients, terms):
        part = term * np.float32(coefficient)
        total = part if total is None else total + part
    return total


def collide(f):
    even, odd, mixed = collision_blocks()
    pair_sum = [f[i] + f[i + 1] for i in (1, 3, 5)]
    pair_dif = [f[i] - f[i + 1] for i in (1, 3, 5)]
    quad_sum, quad_mix, quad_one, quad_two = [], [], [], []
    for i in (7, 11, 15):
        sum_a, sum_b = f[i] + f[i + 1], f[i + 2] + f[i + 3]
        dif_a, dif_b = f[i] - f[i + 1], f[i + 2] - f[i + 3]
        quad_sum.append(sum_a + sum_b)
        quad_mix.append(sum_a - sum_b)
        quad_one.append(dif_a + dif_b)
        quad_two.append(dif_a - dif_b)
    odd_terms = [
        [pair_dif[0], quad_one[0], quad_one[1]],
        [pair_dif[1], quad_two[0], quad_one[2]],
        [pair_dif[2], quad_two[1], quad_two[2]],
    ]
    rho = f[0] + (pair_sum[0] + pair_sum[1] + pair_sum[2]) + (quad_sum[0] + quad_sum[1] + quad_sum[2])
    j = [t[0] + t[1] + t[2] for t in odd_terms]
    sq = [c * c for c in j]
    base = rho - 1.5 * (sq[0] + sq[1] + sq[2])
    sq45 = [4.5 * s for s in sq]
    w0, w1, w2 = 1.0 / 3.0, 1.0 / 18.0, 1.0 / 36.0
    even_terms = [f[0] - w0 * base]
    for a in range(3):
        even_terms.append(pair_sum[a] - (2.0 * w1) * (base + sq45[a]))
    for q, (a, b) in enumerate(((0, 1), (0, 2), (1, 2))):
        even_terms.append(quad_sum[q] - (4.0 * w2) * (base + sq45[a] + sq45[b]))
    mix = [
        (quad_mix[q] - j[a] * j[b]) * np.float32(mixed[q])
        for q, (a, b) in enumerate(((0, 1), (0, 2), (1, 2)))
    ]
    odd_out = []
    for a in range(3):
        third = j[a] * np.float32(1.0 / 3.0)
        terms = [t - third for t in odd_terms[a]]
        odd_out.append([dot(row, terms) for row in odd[a]])
    even_out = [dot(row, even_terms) for row in even]
    out = [f[0] - even_out[0]]
    for a in range(3):
        out.append(f[1 + 2 * a] - (even_out[1 + a] + odd_out[a][0]))
        out.append(f[2 + 2 * a] - (even_out[1 + a] - odd_out[a][0]))
    for q, (one, two) in enumerate(
        (
            (odd_out[0][1], odd_out[1][1]),
            (odd_out[0][2], odd_out[2][1]),
            (odd_out[1][2], odd_out[2][2]),
        )
    ):
        i = 7 + 4 * q
        plus, minus = even_out[4 + q] + mix[q], even_out[4 + q] - mix[q]
        both, apart = one + two, one - two
        out.append(f[i] - (plus + both))
        out.append(f[i + 1] - (plus - both))
        out.append(f[i + 2] - (minus + apart))
        out.append(f[i + 3] - (minus - apart))
    return out


def positions():
    lane = lax.broadcasted_iota(jnp.int32, (8, 128), 1)
    sub = lax.broadcasted_iota(jnp.int32, (8, 128), 0)
    return lane, sub


def shift_y(v, step, ghost, lane, sub):
    if step > 0:
        moved = pltpu.roll(v, 32, 1)
        out = jnp.where(lane < 32, pltpu.roll(moved, 1, 0), moved)
        return jnp.where((lane < 32) & (sub == 0), ghost, out)
    moved = pltpu.roll(v, 96, 1)
    out = jnp.where(lane >= 96, pltpu.roll(moved, 7, 0), moved)
    return jnp.where((lane >= 96) & (sub == 7), ghost, out)


def shift_z(v, step, ghost, z):
    moved = pltpu.roll(v, 1 if step > 0 else 127, 1)
    return jnp.where(z == (0 if step > 0 else 31), ghost, moved)


def unpack_ghosts(nbr, rxy, gy):
    lane, _ = positions()
    jy = jnp.maximum(nbr[0, 2], nbr[0, 3]) & 3
    jd = jnp.maximum(jnp.maximum(nbr[0, 6], nbr[0, 7]), jnp.maximum(nbr[0, 8], nbr[0, 9])) & 3
    for k in range(5):
        packed = rxy[jy, 5 + k]
        for g in range(4):
            low = pltpu.roll(packed, (128 - 32 * g) % 128, 1)
            high = pltpu.roll(packed, (96 - 32 * g) % 128, 1)
            gy[k, 1 + 8 * g : 9 + 8 * g, :] = jnp.where(lane < 64, low, high)
    for channel in (7, 8, 9, 10):
        cx, cy, _ = VELOCITY[channel]
        kx = (X_PLUS if cx > 0 else X_MINUS).index(channel)
        ky = (Y_PLUS if cy > 0 else Y_MINUS).index(channel)
        plane = rxy[jd, kx]
        row = pltpu.roll(plane, 32 if cy > 0 else 96, 1)
        row = row[7:8, :] if cy > 0 else row[0:1, :]
        spot = 0 if cx > 0 else 33
        gy[ky, spot : spot + 1, :] = row


def pull(x, nbr, c, rxy, rb, ra, flags, gy):
    lane, sub = positions()
    z = lane & 31
    jx = jnp.maximum(nbr[0, 0], nbr[0, 1]) & 3

    def wall(offset):
        return jnp.where(nbr[0, code_of(offset)] >= 0, 0, 1).astype(jnp.int32)

    def spot(offset):
        return nbr[0, code_of(offset)] & 3

    own = flags[x]
    values = [c[x, i] for i in range(19)]
    j = []
    for axis in range(3):
        plus = sum(values[i] for i in range(19) if VELOCITY[i][axis] > 0)
        minus = sum(values[i] for i in range(19) if VELOCITY[i][axis] < 0)
        j.append(plus - minus)
    calm = 1.0 - 1.5 * (j[0] * j[0] + j[1] * j[1] + j[2] * j[2])
    inlet_square = sum(p * p for p in INLET_SPEED)
    out = [jnp.where(own == 0, values[0], 0.0)]
    for i in range(1, 19):
        cx, cy, cz = VELOCITY[i]
        if cx:
            outside = x == (0 if cx > 0 else EDGE - 1)
            from_x = jnp.clip(x - cx, 0, EDGE - 1)
            kx = (X_PLUS if cx > 0 else X_MINUS).index(i)
            v = jnp.where(outside, rxy[jx, kx], c[from_x, i])
            kind = jnp.where(outside, wall((-cx, 0, 0)), flags[from_x])
        else:
            v, kind = values[i], own
        if cz:
            beyond = rb if cz > 0 else ra
            kz = (Z_PLUS if cz > 0 else Z_MINUS).index(i)
            block, blocked = spot((0, 0, -cz)), wall((0, 0, -cz))
            at = x
            if cx:
                block = jnp.where(outside, spot((-cx, 0, -cz)), block)
                blocked = jnp.where(outside, wall((-cx, 0, -cz)), blocked)
                at = (x - cx) & 31
            message = beyond[block, kz]
            amount = (128 - at) & 127 if cz > 0 else 31 - at
            v = shift_z(v, cz, pltpu.roll(message, amount, 1), z)
            kind = shift_z(kind, cz, blocked, z)
        if cy:
            ky = (Y_PLUS if cy > 0 else Y_MINUS).index(i)
            row = jnp.broadcast_to(gy[ky, pl.ds(x - cx + 1, 1), :], (8, 128))
            blocked = wall((0, -cy, 0))
            if cx:
                blocked = jnp.where(outside, wall((-cx, -cy, 0)), blocked)
            if cz:
                corner = beyond[spot((0, -cy, -cz)), kz]
                target = (0 if cy > 0 else 96) + (0 if cz > 0 else 31)
                source = (96 if cy > 0 else 0) + x
                corner = pltpu.roll(corner, (target - source + 256) & 127, 1)
                corner = corner[7:8, :] if cy > 0 else corner[0:1, :]
                row = shift_z(row, cz, jnp.broadcast_to(corner, (8, 128)), z)
                blocked = jnp.where(z == (0 if cz > 0 else 31), wall((0, -cy, -cz)), blocked)
            v = shift_y(v, cy, row, lane, sub)
            kind = shift_y(kind, cy, blocked, lane, sub)
        weight = WEIGHT_LIST[i]
        along = sum(a * b for a, b in zip(VELOCITY[i], INLET_SPEED))
        inlet = weight * (1.0 + 3.0 * along + 4.5 * along * along - 1.5 * inlet_square)
        speed = sum(a * b for a, b in zip(VELOCITY[i], j) if a)
        outlet = weight * (calm + speed * (3.0 + 4.5 * speed))
        new = jnp.where(
            kind == 0,
            v,
            jnp.where(kind == 1, values[opposite(i)], jnp.where(kind == 2, np.float32(inlet), outlet)),
        )
        out.append(jnp.where(own == 0, new, 0.0))
    return out


def note_faces(x, nbr, collided, zu, zd, rows):
    lane, _ = positions()
    here = (lane & 31) == x
    for k in range(5):
        up = pltpu.roll(collided[Z_PLUS[k]], (x + 97) & 127, 1)
        zu[k] = jnp.where(here, up, zu[k])
        zd[k] = jnp.where(here, pltpu.roll(collided[Z_MINUS[k]], x, 1), zd[k])
        high = collided[Y_PLUS[k]][7:8, :]
        low = collided[Y_MINUS[k]][0:1, :]
        rows[k, pl.ds(x, 1), :] = jnp.where(nbr[0, 2] >= 0, high, low)


def finish_faces(nbr, c, rows, xy):
    lane, _ = positions()
    ahead_x, ahead_y = nbr[0, 0] >= 0, nbr[0, 2] >= 0
    for k in range(5):
        xy[k] = jnp.where(ahead_x, c[EDGE - 1, X_PLUS[k]], c[0, X_MINUS[k]])
        packed = jnp.zeros((8, 128), jnp.float32)
        for g in range(4):
            part = rows[k, 8 * g : 8 * g + 8, :]
            high = pltpu.roll(part, (32 * (g + 1)) % 128, 1)
            low = pltpu.roll(part, 32 * g, 1)
            packed = jnp.where((lane >> 5) == g, jnp.where(ahead_y, high, low), packed)
        xy[5 + k] = packed


def steps_kernel(layers, nbr, flags, f, out, *scratch):
    c, messages, landed = scratch[:2], scratch[2 : 2 + 3 * STEPS], scratch[2 + 3 * STEPS : 2 + 6 * STEPS]
    rows, gy, send_sem, recv_sem = scratch[2 + 6 * STEPS :]
    wait_entry, send, receive, finish = exchanges(layers, messages, landed, send_sem, recv_sem)
    for step in range(STEPS):
        now, before = c[step % 2], c[(step + 1) % 2]
        xy, zu, zd = messages[3 * step : 3 * step + 3]
        zu[...] = jnp.zeros_like(zu)
        zd[...] = jnp.zeros_like(zd)
        if step > 0:
            rxy, rb, ra = landed[3 * step - 3 : 3 * step]
            unpack_ghosts(nbr, rxy, gy)

        def plane(x, carry):
            if step == 0:
                old = [f[x, i] for i in range(19)]
            else:
                old = pull(x, nbr, before, rxy, rb, ra, flags, gy)
            collided = collide(old)
            for i in range(19):
                now[x, i] = collided[i]
            note_faces(x, nbr, collided, zu, zd, rows)
            return carry

        lax.fori_loop(0, EDGE, plane, 0, unroll=2)
        finish_faces(nbr, now, rows, xy)
        if step == 0:
            wait_entry()
        send(step)
        receive(step)
    rxy, rb, ra = landed[3 * STEPS - 3 :]
    unpack_ghosts(nbr, rxy, gy)

    def last_plane(x, carry):
        new = pull(x, nbr, now, rxy, rb, ra, flags, gy)
        for i in range(19):
            out[i, x] = new[i]
        return carry

    lax.fori_loop(0, EDGE, last_plane, 0, unroll=2)
    for step in range(STEPS):
        finish(step)


def spread_kernel(planes, slots, old, out):
    def plane(x, carry):
        for slot in range(slots):
            for s in range(8):
                at = pl.multiple_of(x * 1024 + s * 128, 128)
                out[x, pl.ds(slot * 152 + s, 19, stride=8), :] = old[slot, :, pl.ds(at, 128)]
        return carry

    lax.fori_loop(0, planes, plane, 0)


def exchanges(layers, messages, landed, send_sem, recv_sem):
    me = lax.axis_index("blocks")
    layer, place = me // 4, me % 4
    above, below = layer + 1 < layers, layer > 0
    barrier = pltpu.get_barrier_semaphore()

    def greet(first, k):
        pl.semaphore_signal(
            barrier, inc=1, device_id=(first * 4 + (place + k) % 4,), device_id_type=MESH
        )

    for k in range(1, 4):
        greet(layer, k)

    @pl.when(above)
    def _():
        for k in range(4):
            greet(layer + 1, k)

    @pl.when(below)
    def _():
        for k in range(4):
            greet(layer - 1, k)

    def wait_entry():
        peers = 3 + 4 * above.astype(jnp.int32) + 4 * below.astype(jnp.int32)
        pl.semaphore_wait(barrier, peers)

    def copy(step, group, spot, first, k):
        return pltpu.make_async_remote_copy(
            src_ref=messages[3 * step + group],
            dst_ref=landed[3 * step + group].at[spot],
            send_sem=send_sem.at[step, 4 * group + k],
            recv_sem=recv_sem.at[step, 4 * group + k],
            device_id=(first * 4 + (place + k) % 4,),
            device_id_type=MESH,
        )

    def send(step):
        @pl.when(above)
        def _():
            for k in range(4):
                copy(step, 1, place, layer + 1, k).start()

        @pl.when(below)
        def _():
            for k in range(4):
                copy(step, 2, place, layer - 1, k).start()

        for k in range(1, 4):
            copy(step, 0, place, layer, k).start()

    def receive(step):
        for k in range(1, 4):
            copy(step, 0, (place + 4 - k) % 4, layer, k).wait_recv()

        @pl.when(below)
        def _():
            for k in range(4):
                copy(step, 1, (place + 4 - k) % 4, layer - 1, k).wait_recv()

        @pl.when(above)
        def _():
            for k in range(4):
                copy(step, 2, (place + 4 - k) % 4, layer + 1, k).wait_recv()

    def finish(step):
        @pl.when(above)
        def _():
            for k in range(4):
                copy(step, 1, place, layer + 1, k).wait_send()

        @pl.when(below)
        def _():
            for k in range(4):
                copy(step, 2, place, layer - 1, k).wait_send()

        for k in range(1, 4):
            copy(step, 0, place, layer, k).wait_send()

    return wait_entry, send, receive, finish


VMEM = pl.BlockSpec(memory_space=pltpu.VMEM)
SMEM = pl.BlockSpec(memory_space=pltpu.SMEM)
STATE = jax.ShapeDtypeStruct((EDGE, 19, 8, 128), jnp.float32)


CHUNKS = tuple((plane, low, high) for low, high in ((0, 7), (7, 13), (13, 19)) for plane in range(4))
CAPACITIES = (9, 10, 12, 16)
AHEAD = 4


def migrate_kernel(room, levels, plan, old, out, *scratch):
    parts = len(CHUNKS)
    held, up_out, up_in, down_out, down_in, sorted_ = (
        scratch[parts * n : parts * n + parts] for n in range(6)
    )
    sems = scratch[6 * parts :]
    own_sem, send_up, recv_up, send_down, recv_down = sems[:5]
    send_one, recv_one, send_three, recv_three = sems[5:]
    me = lax.axis_index("blocks")
    level, place = me // 8, me % 8
    above, below = level + 1 < levels, level > 0

    def peer(d):
        return (place + d) % 8

    def device(d):
        return (level * 8 + peer(d),)

    barrier = pltpu.get_barrier_semaphore()

    def greet(target):
        pl.semaphore_signal(barrier, inc=1, device_id=target, device_id_type=MESH)

    def each(body):
        def step(d, carry):
            body(d)
            return carry

        lax.fori_loop(1, 8, step, 0)

    each(lambda d: greet(device(d)))

    @pl.when(above)
    def _():
        greet((me + 8,))

    @pl.when(below)
    def _():
        greet((me - 8,))

    pl.semaphore_wait(barrier, 7 + above.astype(jnp.int32) + below.astype(jnp.int32))

    def piece(k, owner):
        plane, low, high = CHUNKS[k]
        return old.at[low:high, pl.ds(pl.multiple_of(64 * owner + 16 * plane, 16), 16)]

    def spread(k, d, owner):
        return pltpu.make_async_remote_copy(
            src_ref=piece(k, peer(d)),
            dst_ref=held[k].at[owner],
            send_sem=send_one.at[k, d],
            recv_sem=recv_one.at[k, d],
            device_id=device(d),
            device_id_type=MESH,
        )

    def keep(k):
        return pltpu.make_async_copy(piece(k, place), held[k].at[place], own_sem.at[k])

    def rise(k, target):
        return pltpu.make_async_remote_copy(
            src_ref=up_out[k],
            dst_ref=up_in[k],
            send_sem=send_up.at[k],
            recv_sem=recv_up.at[k],
            device_id=(target,),
            device_id_type=MESH,
        )

    def sink(k, target):
        return pltpu.make_async_remote_copy(
            src_ref=down_out[k],
            dst_ref=down_in[k],
            send_sem=send_down.at[k],
            recv_sem=recv_down.at[k],
            device_id=(target,),
            device_id_type=MESH,
        )

    def hand(k, d, owner):
        plane, low, high = CHUNKS[k]
        return pltpu.make_async_remote_copy(
            src_ref=sorted_[k].at[peer(d)],
            dst_ref=out.at[4 * owner + plane, low:high],
            send_sem=send_three.at[k, d],
            recv_sem=recv_three.at[k, d],
            device_id=device(d),
            device_id_type=MESH,
        )

    def slot_of(k, slot):
        first = held[k][slot >> 1, :, pl.ds(0, 8, stride=2), :]
        second = held[k][slot >> 1, :, pl.ds(1, 8, stride=2), :]
        return jnp.where((slot & 1) > 0, second, first)

    def go_up(k, wait):
        if wait:
            rise(k, me - 8).wait_recv()

        def pick(e, carry):
            new = slot_of(k, plan[1, e])
            up_out[k][e] = jnp.where(plan[0, e] > 0, up_in[k][plan[2, e]], new) if wait else new
            return carry

        lax.fori_loop(0, room, pick, 0)
        rise(k, me + 8).start()

    def go_down(k, wait):
        if wait:
            sink(k, me + 8).wait_recv()

        def pick(e, carry):
            new = slot_of(k, plan[4, e])
            down_out[k][e] = jnp.where(plan[3, e] > 0, down_in[k][plan[5, e]], new) if wait else new
            return carry

        lax.fori_loop(0, room, pick, 0)
        sink(k, me - 8).start()

    def deliver(k):
        plane, low, high = CHUNKS[k]

        @pl.when(level == levels - 1)
        def _():
            rise(k, me - 8).wait_recv()

        @pl.when(level == 0)
        def _():
            sink(k, me + 8).wait_recv()

        def choose(b, carry):
            kind = plan[6, b]
            value = jnp.where(kind == 1, up_in[k][plan[8, b]], down_in[k][plan[8, b]])
            sorted_[k][b] = jnp.where(kind == 0, slot_of(k, plan[7, b]), value)
            return carry

        lax.fori_loop(0, 8, choose, 0)
        each(lambda d: hand(k, d, place).start())
        out[4 * place + plane, low:high] = sorted_[k][place]

    def begin(k):
        keep(k).start()
        each(lambda d: spread(k, d, place).start())

    for k in range(AHEAD):
        begin(k)
    for turn in range(parts + levels - 1):
        if turn < parts:
            keep(turn).wait()
            each(lambda d: spread(turn, d, peer(8 - d)).wait_recv())
            if turn + AHEAD < parts:
                begin(turn + AHEAD)
        for lag in range(levels - 1):
            if 0 <= turn - lag < parts:

                @pl.when(level == lag)
                def _():
                    go_up(turn - lag, lag > 0)

                @pl.when(level == levels - 1 - lag)
                def _():
                    go_down(turn - lag, lag > 0)

        if turn >= levels - 1:
            deliver(turn - levels + 1)
    for k in range(parts):
        each(lambda d: hand(k, d, peer(8 - d)).wait_recv())
    for k in range(parts):
        each(lambda d: spread(k, d, place).wait_send())
        each(lambda d: hand(k, d, place).wait_send())

        @pl.when(above)
        def _():
            rise(k, me + 8).wait_send()

        @pl.when(below)
        def _():
            sink(k, me - 8).wait_send()


def migrate_with(room, number, plan, old):
    parts = len(CHUNKS)

    def buffers(count, rows=8):
        return [pltpu.VMEM((count, high - low, rows, 128), jnp.float32) for _, low, high in CHUNKS]

    dma = pltpu.SemaphoreType.DMA
    return pl.pallas_call(
        functools.partial(migrate_kernel, room, lax.axis_size("blocks") // 8),
        out_shape=STATE,
        in_specs=[SMEM, pl.BlockSpec(memory_space=pl.ANY)],
        out_specs=VMEM,
        scratch_shapes=buffers(8, 16)
        + buffers(room) * 4
        + buffers(8)
        + [dma((parts,))] * 5
        + [dma((parts, 8))] * 4,
        compiler_params=pltpu.CompilerParams(
            collective_id=number, has_side_effects=True, vmem_limit_bytes=48 * 2**20
        ),
    )(plan, old)


def plan_kernel(levels, old_slot, plan, branch):
    level = lax.axis_index("blocks") // 8
    for row in range(9):
        for e in range(16):
            plan[row, e] = 0

    def select(values, which):
        return sum(jnp.where(which == n, value, 0) for n, value in enumerate(values))

    def block(b, counts):
        ups, downs = counts
        slot = old_slot[b]
        source, target = slot >> 4, b >> 3
        local = slot & 15

        @pl.when((source <= level) & (target > level))
        def _():
            at = select(ups, level)
            plan[0, at] = (source < level).astype(jnp.int32)
            plan[1, at] = jnp.where(source == level, local, 0)
            plan[2, at] = jnp.where(source < level, select(ups, level - 1), 0)

        @pl.when((source >= level) & (target < level))
        def _():
            at = select(downs, level - 1)
            plan[3, at] = (source > level).astype(jnp.int32)
            plan[4, at] = jnp.where(source == level, local, 0)
            plan[5, at] = jnp.where(source > level, select(downs, level), 0)

        @pl.when(target == level)
        def _():
            at = b & 7
            rank = jnp.where(source < level, select(ups, level - 1), select(downs, level))
            plan[6, at] = jnp.where(source == level, 0, jnp.where(source < level, 1, 2))
            plan[7, at] = jnp.where(source == level, local, 0)
            plan[8, at] = jnp.where(source == level, 0, rank)

        ups = tuple(
            count + ((source <= n) & (target > n)).astype(jnp.int32) for n, count in enumerate(ups)
        )
        downs = tuple(
            count + ((source > n) & (target <= n)).astype(jnp.int32)
            for n, count in enumerate(downs)
        )
        return ups, downs

    zeros = (jnp.int32(0),) * (levels - 1)
    ups, downs = lax.fori_loop(0, 8 * levels, block, (zeros, zeros))
    most = functools.reduce(jnp.maximum, ups + downs)
    branch[0] = sum((most > room).astype(jnp.int32) for room in CAPACITIES[:-1])


def migrate(old_pdfs, old_slot):
    peers = lax.axis_size("blocks")
    slots = old_pdfs.shape[0]
    blocks = old_slot.shape[0]
    if peers == EDGE and slots == 2:
        plan, branch = pl.pallas_call(
            functools.partial(plan_kernel, peers // 8),
            out_shape=[
                jax.ShapeDtypeStruct((9, 16), jnp.int32),
                jax.ShapeDtypeStruct((1,), jnp.int32),
            ],
            in_specs=[SMEM],
            out_specs=[SMEM, SMEM],
        )(old_slot)
        old = old_pdfs.reshape(slots, 19, 256, 128).transpose(1, 2, 0, 3).reshape(19, 512, 128)
        calls = [
            functools.partial(migrate_with, room, 1 + number)
            for number, room in enumerate(CAPACITIES)
        ]
        return lax.switch(branch[0], calls, plan, old)
    planes = 4
    tiles = pl.pallas_call(
        functools.partial(spread_kernel, planes, slots),
        grid=(EDGE // planes,),
        out_shape=jax.ShapeDtypeStruct((EDGE, slots * 152, 128), jnp.float32),
        in_specs=[pl.BlockSpec((slots, 19, planes * 1024), lambda g: (0, 0, g))],
        out_specs=pl.BlockSpec((planes, slots * 152, 128), lambda g: (g, 0, 0)),
        compiler_params=pltpu.CompilerParams(vmem_limit_bytes=58 * 2**20),
    )(old_pdfs)
    parts = peers // EDGE
    rows = 8 // parts
    if parts > 1:
        tiles = tiles.reshape(EDGE, slots * 19, parts, rows, 128).transpose(0, 2, 1, 3, 4)
        tiles = tiles.reshape(peers, slots * 19 * rows, 128)
    spread = lax.all_to_all(tiles, "blocks", split_axis=0, concat_axis=0, tiled=True)
    spread = spread.reshape(peers * slots, 19 * rows, 128)
    ordered = spread.at[old_slot].get(mode="promise_in_bounds")
    arrived = lax.all_to_all(ordered, "blocks", split_axis=0, concat_axis=0, tiled=True)
    if parts > 1:
        arrived = arrived.reshape(EDGE, parts, 19, rows, 128).transpose(0, 2, 1, 3, 4)
    return arrived.reshape(EDGE, 19, 8, 128)


def per_device(old_pdfs, old_slot, neighbours, cell_flags):
    state = migrate(old_pdfs, old_slot)
    flags = cell_flags.reshape(EDGE, 8, 128)
    layers = lax.axis_size("blocks") // 4

    def tiles(*lead):
        return pltpu.VMEM(lead + (8, 128), jnp.float32)

    out = pl.pallas_call(
        functools.partial(steps_kernel, layers),
        out_shape=jax.ShapeDtypeStruct((19, EDGE, 8, 128), jnp.float32),
        in_specs=[SMEM, VMEM, VMEM],
        out_specs=VMEM,
        scratch_shapes=[tiles(EDGE, 19)] * 2
        + [tiles(10), tiles(5), tiles(5)] * STEPS
        + [tiles(4, 10), tiles(4, 5), tiles(4, 5)] * STEPS
        + [
            pltpu.VMEM((5, EDGE, 128), jnp.float32),
            pltpu.VMEM((5, EDGE + 8, 128), jnp.float32),
            pltpu.SemaphoreType.DMA((STEPS, 12)),
            pltpu.SemaphoreType.DMA((STEPS, 12)),
        ],
        compiler_params=pltpu.CompilerParams(
            collective_id=0, has_side_effects=True, vmem_limit_bytes=40 * 2**20
        ),
    )(neighbours, flags, state)
    return out.reshape(1, 19, EDGE * EDGE * EDGE)


def solution(mesh):
    in_specs = (P("blocks", None, None), P(), P("blocks", None), P("blocks", None))
    out_specs = P("blocks", None, None)
    return jax.shard_map(
        per_device, mesh=mesh, in_specs=in_specs, out_specs=out_specs, check_vma=False
    )
```

```python
import functools

import jax
import jax.numpy as jnp
import numpy as np
from jax import lax
from jax.experimental import pallas as pl
from jax.experimental.pallas import tpu as pltpu
from jax.sharding import PartitionSpec as P

EDGE = 32
STEPS = 2
MESH = pl.DeviceIdType.MESH

VELOCITY = (
    (0, 0, 0),
    (1, 0, 0),
    (-1, 0, 0),
    (0, 1, 0),
    (0, -1, 0),
    (0, 0, 1),
    (0, 0, -1),
    (1, 1, 0),
    (-1, -1, 0),
    (1, -1, 0),
    (-1, 1, 0),
    (1, 0, 1),
    (-1, 0, -1),
    (1, 0, -1),
    (-1, 0, 1),
    (0, 1, 1),
    (0, -1, -1),
    (0, 1, -1),
    (0, -1, 1),
)
WEIGHT_LIST = (1.0 / 3.0,) + (1.0 / 18.0,) * 6 + (1.0 / 36.0,) * 12
RELAXATION = (
    0.0,
    0.0,
    0.0,
    0.0,
    1.19,
    1.4,
    1.2,
    1.2,
    1.2,
    1.6,
    1.6,
    1.6,
    1.6,
    1.6,
    1.4,
    1.4,
    1.98,
    1.98,
    1.98,
)
INLET_SPEED = (0.0, 0.0, 0.05)

X_PLUS, X_MINUS = (1, 7, 9, 11, 13), (2, 8, 10, 12, 14)
Y_PLUS, Y_MINUS = (3, 7, 10, 15, 17), (4, 8, 9, 16, 18)
Z_PLUS, Z_MINUS = (5, 11, 14, 15, 18), (6, 12, 13, 16, 17)
ORBITS = ((0,), (1, 2), (3, 4), (5, 6), (7, 8, 9, 10), (11, 12, 13, 14), (15, 16, 17, 18))


def collision_table():
    lattice = np.array(VELOCITY) * 1.0
    along_x, along_y, along_z = (lattice[:, 0], lattice[:, 1], lattice[:, 2])
    squared = along_x * along_x + along_y * along_y + along_z * along_z
    monomials = [
        np.ones(19),
        along_x,
        along_y,
        along_z,
        squared,
        squared * squared,
        squared * along_x,
        squared * along_y,
        squared * along_z,
        3.0 * along_x * along_x - squared,
        along_y * along_y - along_z * along_z,
        along_x * along_y,
        along_y * along_z,
        along_x * along_z,
        squared * (3.0 * along_x * along_x - squared),
        squared * (along_y * along_y - along_z * along_z),
        (along_y * along_y - along_z * along_z) * along_x,
        (along_z * along_z - along_x * along_x) * along_y,
        (along_x * along_x - along_y * along_y) * along_z,
    ]
    orthonormal = []
    for vector in monomials:
        for earlier in orthonormal:
            vector = vector - np.dot(vector, earlier) * earlier
        orthonormal.append(vector / np.sqrt(np.dot(vector, vector)))
    stacked = np.stack(orthonormal)
    return stacked.T * np.array(RELAXATION) @ stacked


def opposite(index_value):
    if index_value == 0:
        return 0
    return index_value + 1 if index_value % 2 == 1 else index_value - 1


def code_of(offset):
    return VELOCITY.index(tuple(offset)) - 1


def collision_blocks():
    matrix = collision_table().astype(np.float32).astype(np.float64)
    even = [[float(np.mean([matrix[a[0], b] for b in group])) for group in ORBITS] for a in ORBITS]
    odd = []
    for axis in range(3):
        groups = [g for g in ORBITS if any(VELOCITY[b][axis] for b in g)]
        rows = []
        for a in groups:
            first = next(c for c in a if VELOCITY[c][axis] > 0)
            rows.append(
                [float(np.mean([VELOCITY[b][axis] * matrix[first, b] for b in g])) for g in groups]
            )
        odd.append(rows)
    mixed = []
    for group in ORBITS[4:]:
        signs = [1.0, 1.0, -1.0, -1.0]
        mixed.append(float(np.mean([s * matrix[group[0], b] for s, b in zip(signs, group)])))
    return even, odd, mixed


def dot(coefficients, terms):
    total = None
    for coefficient, term in zip(coefficients, terms):
        part = term * np.float32(coefficient)
        total = part if total is None else total + part
    return total


def collide(f):
    even, odd, mixed = collision_blocks()
    pair_sum = [f[i] + f[i + 1] for i in (1, 3, 5)]
    pair_dif = [f[i] - f[i + 1] for i in (1, 3, 5)]
    quad_sum, quad_mix, quad_one, quad_two = [], [], [], []
    for i in (7, 11, 15):
        sum_a, sum_b = f[i] + f[i + 1], f[i + 2] + f[i + 3]
        dif_a, dif_b = f[i] - f[i + 1], f[i + 2] - f[i + 3]
        quad_sum.append(sum_a + sum_b)
        quad_mix.append(sum_a - sum_b)
        quad_one.append(dif_a + dif_b)
        quad_two.append(dif_a - dif_b)
    odd_terms = [
        [pair_dif[0], quad_one[0], quad_one[1]],
        [pair_dif[1], quad_two[0], quad_one[2]],
        [pair_dif[2], quad_two[1], quad_two[2]],
    ]
    rho = f[0] + (pair_sum[0] + pair_sum[1] + pair_sum[2]) + (quad_sum[0] + quad_sum[1] + quad_sum[2])
    j = [t[0] + t[1] + t[2] for t in odd_terms]
    sq = [c * c for c in j]
    base = rho - 1.5 * (sq[0] + sq[1] + sq[2])
    sq45 = [4.5 * s for s in sq]
    w0, w1, w2 = 1.0 / 3.0, 1.0 / 18.0, 1.0 / 36.0
    even_terms = [f[0] - w0 * base]
    for a in range(3):
        even_terms.append(pair_sum[a] - (2.0 * w1) * (base + sq45[a]))
    for q, (a, b) in enumerate(((0, 1), (0, 2), (1, 2))):
        even_terms.append(quad_sum[q] - (4.0 * w2) * (base + sq45[a] + sq45[b]))
    mix = [
        (quad_mix[q] - j[a] * j[b]) * np.float32(mixed[q])
        for q, (a, b) in enumerate(((0, 1), (0, 2), (1, 2)))
    ]
    odd_out = []
    for a in range(3):
        third = j[a] * np.float32(1.0 / 3.0)
        terms = [t - third for t in odd_terms[a]]
        odd_out.append([dot(row, terms) for row in odd[a]])
    even_out = [dot(row, even_terms) for row in even]
    out = [f[0] - even_out[0]]
    for a in range(3):
        out.append(f[1 + 2 * a] - (even_out[1 + a] + odd_out[a][0]))
        out.append(f[2 + 2 * a] - (even_out[1 + a] - odd_out[a][0]))
    for q, (one, two) in enumerate(
        (
            (odd_out[0][1], odd_out[1][1]),
            (odd_out[0][2], odd_out[2][1]),
            (odd_out[1][2], odd_out[2][2]),
        )
    ):
        i = 7 + 4 * q
        plus, minus = even_out[4 + q] + mix[q], even_out[4 + q] - mix[q]
        both, apart = one + two, one - two
        out.append(f[i] - (plus + both))
        out.append(f[i + 1] - (plus - both))
        out.append(f[i + 2] - (minus + apart))
        out.append(f[i + 3] - (minus - apart))
    return out


def positions():
    lane = lax.broadcasted_iota(jnp.int32, (8, 128), 1)
    sub = lax.broadcasted_iota(jnp.int32, (8, 128), 0)
    return lane, sub


def shift_y(v, step, ghost, lane, sub):
    if step > 0:
        moved = pltpu.roll(v, 32, 1)
        out = jnp.where(lane < 32, pltpu.roll(moved, 1, 0), moved)
        return jnp.where((lane < 32) & (sub == 0), ghost, out)
    moved = pltpu.roll(v, 96, 1)
    out = jnp.where(lane >= 96, pltpu.roll(moved, 7, 0), moved)
    return jnp.where((lane >= 96) & (sub == 7), ghost, out)


def shift_z(v, step, ghost, z):
    moved = pltpu.roll(v, 1 if step > 0 else 127, 1)
    return jnp.where(z == (0 if step > 0 else 31), ghost, moved)


def unpack_ghosts(nbr, rxy, gy):
    lane, _ = positions()
    jy = jnp.maximum(nbr[0, 2], nbr[0, 3]) & 3
    jd = jnp.maximum(jnp.maximum(nbr[0, 6], nbr[0, 7]), jnp.maximum(nbr[0, 8], nbr[0, 9])) & 3
    for k in range(5):
        packed = rxy[jy, 5 + k]
        for g in range(4):
            low = pltpu.roll(packed, (128 - 32 * g) % 128, 1)
            high = pltpu.roll(packed, (96 - 32 * g) % 128, 1)
            gy[k, 1 + 8 * g : 9 + 8 * g, :] = jnp.where(lane < 64, low, high)
    for channel in (7, 8, 9, 10):
        cx, cy, _ = VELOCITY[channel]
        kx = (X_PLUS if cx > 0 else X_MINUS).index(channel)
        ky = (Y_PLUS if cy > 0 else Y_MINUS).index(channel)
        plane = rxy[jd, kx]
        row = pltpu.roll(plane, 32 if cy > 0 else 96, 1)
        row = row[7:8, :] if cy > 0 else row[0:1, :]
        spot = 0 if cx > 0 else 33
        gy[ky, spot : spot + 1, :] = row


def pull(x, nbr, c, rxy, rb, ra, flags, gy):
    lane, sub = positions()
    z = lane & 31
    jx = jnp.maximum(nbr[0, 0], nbr[0, 1]) & 3

    def wall(offset):
        return jnp.where(nbr[0, code_of(offset)] >= 0, 0, 1).astype(jnp.int32)

    def spot(offset):
        return nbr[0, code_of(offset)] & 3

    own = flags[x]
    values = [c[x, i] for i in range(19)]
    j = []
    for axis in range(3):
        plus = sum(values[i] for i in range(19) if VELOCITY[i][axis] > 0)
        minus = sum(values[i] for i in range(19) if VELOCITY[i][axis] < 0)
        j.append(plus - minus)
    calm = 1.0 - 1.5 * (j[0] * j[0] + j[1] * j[1] + j[2] * j[2])
    inlet_square = sum(p * p for p in INLET_SPEED)
    out = [jnp.where(own == 0, values[0], 0.0)]
    for i in range(1, 19):
        cx, cy, cz = VELOCITY[i]
        if cx:
            outside = x == (0 if cx > 0 else EDGE - 1)
            from_x = jnp.clip(x - cx, 0, EDGE - 1)
            kx = (X_PLUS if cx > 0 else X_MINUS).index(i)
            v = jnp.where(outside, rxy[jx, kx], c[from_x, i])
            kind = jnp.where(outside, wall((-cx, 0, 0)), flags[from_x])
        else:
            v, kind = values[i], own
        if cz:
            beyond = rb if cz > 0 else ra
            kz = (Z_PLUS if cz > 0 else Z_MINUS).index(i)
            block, blocked = spot((0, 0, -cz)), wall((0, 0, -cz))
            at = x
            if cx:
                block = jnp.where(outside, spot((-cx, 0, -cz)), block)
                blocked = jnp.where(outside, wall((-cx, 0, -cz)), blocked)
                at = (x - cx) & 31
            message = beyond[block, kz]
            amount = (128 - at) & 127 if cz > 0 else 31 - at
            v = shift_z(v, cz, pltpu.roll(message, amount, 1), z)
            kind = shift_z(kind, cz, blocked, z)
        if cy:
            ky = (Y_PLUS if cy > 0 else Y_MINUS).index(i)
            row = jnp.broadcast_to(gy[ky, pl.ds(x - cx + 1, 1), :], (8, 128))
            blocked = wall((0, -cy, 0))
            if cx:
                blocked = jnp.where(outside, wall((-cx, -cy, 0)), blocked)
            if cz:
                corner = beyond[spot((0, -cy, -cz)), kz]
                target = (0 if cy > 0 else 96) + (0 if cz > 0 else 31)
                source = (96 if cy > 0 else 0) + x
                corner = pltpu.roll(corner, (target - source + 256) & 127, 1)
                corner = corner[7:8, :] if cy > 0 else corner[0:1, :]
                row = shift_z(row, cz, jnp.broadcast_to(corner, (8, 128)), z)
                blocked = jnp.where(z == (0 if cz > 0 else 31), wall((0, -cy, -cz)), blocked)
            v = shift_y(v, cy, row, lane, sub)
            kind = shift_y(kind, cy, blocked, lane, sub)
        weight = WEIGHT_LIST[i]
        along = sum(a * b for a, b in zip(VELOCITY[i], INLET_SPEED))
        inlet = weight * (1.0 + 3.0 * along + 4.5 * along * along - 1.5 * inlet_square)
        speed = sum(a * b for a, b in zip(VELOCITY[i], j) if a)
        outlet = weight * (calm + speed * (3.0 + 4.5 * speed))
        new = jnp.where(
            kind == 0,
            v,
            jnp.where(kind == 1, values[opposite(i)], jnp.where(kind == 2, np.float32(inlet), outlet)),
        )
        out.append(jnp.where(own == 0, new, 0.0))
    return out


def note_faces(x, nbr, collided, zu, zd, rows):
    lane, _ = positions()
    here = (lane & 31) == x
    for k in range(5):
        up = pltpu.roll(collided[Z_PLUS[k]], (x + 97) & 127, 1)
        zu[k] = jnp.where(here, up, zu[k])
        zd[k] = jnp.where(here, pltpu.roll(collided[Z_MINUS[k]], x, 1), zd[k])
        high = collided[Y_PLUS[k]][7:8, :]
        low = collided[Y_MINUS[k]][0:1, :]
        rows[k, pl.ds(x, 1), :] = jnp.where(nbr[0, 2] >= 0, high, low)


def finish_faces(nbr, c, rows, xy):
    lane, _ = positions()
    ahead_x, ahead_y = nbr[0, 0] >= 0, nbr[0, 2] >= 0
    for k in range(5):
        xy[k] = jnp.where(ahead_x, c[EDGE - 1, X_PLUS[k]], c[0, X_MINUS[k]])
        packed = jnp.zeros((8, 128), jnp.float32)
        for g in range(4):
            part = rows[k, 8 * g : 8 * g + 8, :]
            high = pltpu.roll(part, (32 * (g + 1)) % 128, 1)
            low = pltpu.roll(part, 32 * g, 1)
            packed = jnp.where((lane >> 5) == g, jnp.where(ahead_y, high, low), packed)
        xy[5 + k] = packed


def steps_kernel(layers, nbr, flags, f, out, *scratch):
    c, messages, landed = scratch[:2], scratch[2 : 2 + 3 * STEPS], scratch[2 + 3 * STEPS : 2 + 6 * STEPS]
    rows, gy, send_sem, recv_sem = scratch[2 + 6 * STEPS :]
    wait_entry, send, receive, finish = exchanges(layers, messages, landed, send_sem, recv_sem)
    for step in range(STEPS):
        now, before = c[step % 2], c[(step + 1) % 2]
        xy, zu, zd = messages[3 * step : 3 * step + 3]
        zu[...] = jnp.zeros_like(zu)
        zd[...] = jnp.zeros_like(zd)
        if step > 0:
            rxy, rb, ra = landed[3 * step - 3 : 3 * step]
            unpack_ghosts(nbr, rxy, gy)

        def plane(x, carry):
            if step == 0:
                old = [f[x, i] for i in range(19)]
            else:
                old = pull(x, nbr, before, rxy, rb, ra, flags, gy)
            collided = collide(old)
            for i in range(19):
                now[x, i] = collided[i]
            note_faces(x, nbr, collided, zu, zd, rows)
            return carry

        lax.fori_loop(0, EDGE, plane, 0, unroll=2)
        finish_faces(nbr, now, rows, xy)
        if step == 0:
            wait_entry()
        send(step)
        receive(step)
    rxy, rb, ra = landed[3 * STEPS - 3 :]
    unpack_ghosts(nbr, rxy, gy)

    def last_plane(x, carry):
        new = pull(x, nbr, now, rxy, rb, ra, flags, gy)
        for i in range(19):
            out[i, x] = new[i]
        return carry

    lax.fori_loop(0, EDGE, last_plane, 0, unroll=2)
    for step in range(STEPS):
        finish(step)


def spread_kernel(planes, slots, old, out):
    def plane(x, carry):
        for slot in range(slots):
            for s in range(8):
                at = pl.multiple_of(x * 1024 + s * 128, 128)
                out[x, pl.ds(slot * 152 + s, 19, stride=8), :] = old[slot, :, pl.ds(at, 128)]
        return carry

    lax.fori_loop(0, planes, plane, 0)


def exchanges(layers, messages, landed, send_sem, recv_sem):
    me = lax.axis_index("blocks")
    layer, place = me // 4, me % 4
    above, below = layer + 1 < layers, layer > 0
    barrier = pltpu.get_barrier_semaphore()

    def greet(first, k):
        pl.semaphore_signal(
            barrier, inc=1, device_id=(first * 4 + (place + k) % 4,), device_id_type=MESH
        )

    for k in range(1, 4):
        greet(layer, k)

    @pl.when(above)
    def _():
        for k in range(4):
            greet(layer + 1, k)

    @pl.when(below)
    def _():
        for k in range(4):
            greet(layer - 1, k)

    def wait_entry():
        peers = 3 + 4 * above.astype(jnp.int32) + 4 * below.astype(jnp.int32)
        pl.semaphore_wait(barrier, peers)

    def copy(step, group, spot, first, k):
        return pltpu.make_async_remote_copy(
            src_ref=messages[3 * step + group],
            dst_ref=landed[3 * step + group].at[spot],
            send_sem=send_sem.at[step, 4 * group + k],
            recv_sem=recv_sem.at[step, 4 * group + k],
            device_id=(first * 4 + (place + k) % 4,),
            device_id_type=MESH,
        )

    def send(step):
        @pl.when(above)
        def _():
            for k in range(4):
                copy(step, 1, place, layer + 1, k).start()

        @pl.when(below)
        def _():
            for k in range(4):
                copy(step, 2, place, layer - 1, k).start()

        for k in range(1, 4):
            copy(step, 0, place, layer, k).start()

    def receive(step):
        for k in range(1, 4):
            copy(step, 0, (place + 4 - k) % 4, layer, k).wait_recv()

        @pl.when(below)
        def _():
            for k in range(4):
                copy(step, 1, (place + 4 - k) % 4, layer - 1, k).wait_recv()

        @pl.when(above)
        def _():
            for k in range(4):
                copy(step, 2, (place + 4 - k) % 4, layer + 1, k).wait_recv()

    def finish(step):
        @pl.when(above)
        def _():
            for k in range(4):
                copy(step, 1, place, layer + 1, k).wait_send()

        @pl.when(below)
        def _():
            for k in range(4):
                copy(step, 2, place, layer - 1, k).wait_send()

        for k in range(1, 4):
            copy(step, 0, place, layer, k).wait_send()

    return wait_entry, send, receive, finish


VMEM = pl.BlockSpec(memory_space=pltpu.VMEM)
SMEM = pl.BlockSpec(memory_space=pltpu.SMEM)
STATE = jax.ShapeDtypeStruct((EDGE, 19, 8, 128), jnp.float32)


CHUNKS = tuple((plane, low, high) for low, high in ((0, 7), (7, 13), (13, 19)) for plane in range(4))
CAPACITIES = (9, 10, 11, 13, 16)
AHEAD = 2


def migrate_kernel(room, levels, plan, old, out, *scratch):
    parts = len(CHUNKS)
    held, up_out, up_in, down_out, down_in, sorted_ = (
        scratch[parts * n : parts * n + parts] for n in range(6)
    )
    sems = scratch[6 * parts :]
    own_sem, send_up, recv_up, send_down, recv_down = sems[:5]
    send_one, recv_one, send_three, recv_three = sems[5:]
    me = lax.axis_index("blocks")
    level, place = me // 8, me % 8
    above, below = level + 1 < levels, level > 0

    def peer(d):
        return (place + d) % 8

    def device(d):
        return (level * 8 + peer(d),)

    barrier = pltpu.get_barrier_semaphore()

    def greet(target):
        pl.semaphore_signal(barrier, inc=1, device_id=target, device_id_type=MESH)

    def each(body):
        def step(d, carry):
            body(d)
            return carry

        lax.fori_loop(1, 8, step, 0)

    each(lambda d: greet(device(d)))

    @pl.when(above)
    def _():
        greet((me + 8,))

    @pl.when(below)
    def _():
        greet((me - 8,))

    pl.semaphore_wait(barrier, 7 + above.astype(jnp.int32) + below.astype(jnp.int32))

    def piece(k, owner):
        plane, low, high = CHUNKS[k]
        return old.at[low:high, pl.ds(pl.multiple_of(64 * owner + 16 * plane, 16), 16)]

    def spread(k, d, owner):
        return pltpu.make_async_remote_copy(
            src_ref=piece(k, peer(d)),
            dst_ref=held[k].at[owner],
            send_sem=send_one.at[k, d],
            recv_sem=recv_one.at[k, d],
            device_id=device(d),
            device_id_type=MESH,
        )

    def keep(k):
        return pltpu.make_async_copy(piece(k, place), held[k].at[place], own_sem.at[k])

    def rise(k, target):
        return pltpu.make_async_remote_copy(
            src_ref=up_out[k],
            dst_ref=up_in[k],
            send_sem=send_up.at[k],
            recv_sem=recv_up.at[k],
            device_id=(target,),
            device_id_type=MESH,
        )

    def sink(k, target):
        return pltpu.make_async_remote_copy(
            src_ref=down_out[k],
            dst_ref=down_in[k],
            send_sem=send_down.at[k],
            recv_sem=recv_down.at[k],
            device_id=(target,),
            device_id_type=MESH,
        )

    def hand(k, d, owner):
        plane, low, high = CHUNKS[k]
        return pltpu.make_async_remote_copy(
            src_ref=sorted_[k].at[peer(d)],
            dst_ref=out.at[4 * owner + plane, low:high],
            send_sem=send_three.at[k, d],
            recv_sem=recv_three.at[k, d],
            device_id=device(d),
            device_id_type=MESH,
        )

    def slot_of(k, slot):
        first = held[k][slot >> 1, :, pl.ds(0, 8, stride=2), :]
        second = held[k][slot >> 1, :, pl.ds(1, 8, stride=2), :]
        return jnp.where((slot & 1) > 0, second, first)

    def go_up(k, wait):
        if wait:
            rise(k, me - 8).wait_recv()

        def pick(e, carry):
            new = slot_of(k, plan[1, e])
            up_out[k][e] = jnp.where(plan[0, e] > 0, up_in[k][plan[2, e]], new) if wait else new
            return carry

        lax.fori_loop(0, room, pick, 0)
        rise(k, me + 8).start()

    def go_down(k, wait):
        if wait:
            sink(k, me + 8).wait_recv()

        def pick(e, carry):
            new = slot_of(k, plan[4, e])
            down_out[k][e] = jnp.where(plan[3, e] > 0, down_in[k][plan[5, e]], new) if wait else new
            return carry

        lax.fori_loop(0, room, pick, 0)
        sink(k, me - 8).start()

    def deliver(k):
        plane, low, high = CHUNKS[k]

        @pl.when(level == levels - 1)
        def _():
            rise(k, me - 8).wait_recv()

        @pl.when(level == 0)
        def _():
            sink(k, me + 8).wait_recv()

        def choose(b, carry):
            kind = plan[6, b]
            value = jnp.where(kind == 1, up_in[k][plan[8, b]], down_in[k][plan[8, b]])
            sorted_[k][b] = jnp.where(kind == 0, slot_of(k, plan[7, b]), value)
            return carry

        lax.fori_loop(0, 8, choose, 0)
        each(lambda d: hand(k, d, place).start())
        out[4 * place + plane, low:high] = sorted_[k][place]

    def begin(k):
        keep(k).start()
        each(lambda d: spread(k, d, place).start())

    for k in range(AHEAD):
        begin(k)
    for turn in range(parts + levels - 1):
        if turn < parts:
            keep(turn).wait()
            each(lambda d: spread(turn, d, peer(8 - d)).wait_recv())
            if turn + AHEAD < parts:
                begin(turn + AHEAD)
        for lag in range(levels - 1):
            if 0 <= turn - lag < parts:

                @pl.when(level == lag)
                def _():
                    go_up(turn - lag, lag > 0)

                @pl.when(level == levels - 1 - lag)
                def _():
                    go_down(turn - lag, lag > 0)

        if turn >= levels - 1:
            deliver(turn - levels + 1)
    for k in range(parts):
        each(lambda d: hand(k, d, peer(8 - d)).wait_recv())
    for k in range(parts):
        each(lambda d: spread(k, d, place).wait_send())
        each(lambda d: hand(k, d, place).wait_send())

        @pl.when(above)
        def _():
            rise(k, me + 8).wait_send()

        @pl.when(below)
        def _():
            sink(k, me - 8).wait_send()


def migrate_with(room, number, plan, old):
    parts = len(CHUNKS)

    def buffers(count, rows=8):
        return [pltpu.VMEM((count, high - low, rows, 128), jnp.float32) for _, low, high in CHUNKS]

    dma = pltpu.SemaphoreType.DMA
    return pl.pallas_call(
        functools.partial(migrate_kernel, room, lax.axis_size("blocks") // 8),
        out_shape=STATE,
        in_specs=[SMEM, pl.BlockSpec(memory_space=pl.ANY)],
        out_specs=VMEM,
        scratch_shapes=buffers(8, 16)
        + buffers(room) * 4
        + buffers(8)
        + [dma((parts,))] * 5
        + [dma((parts, 8))] * 4,
        compiler_params=pltpu.CompilerParams(
            collective_id=number, has_side_effects=True, vmem_limit_bytes=48 * 2**20
        ),
    )(plan, old)


def plan_kernel(levels, old_slot, plan, branch):
    level = lax.axis_index("blocks") // 8
    for row in range(9):
        for e in range(16):
            plan[row, e] = 0

    def select(values, which):
        return sum(jnp.where(which == n, value, 0) for n, value in enumerate(values))

    def block(b, counts):
        ups, downs = counts
        slot = old_slot[b]
        source, target = slot >> 4, b >> 3
        local = slot & 15

        @pl.when((source <= level) & (target > level))
        def _():
            at = select(ups, level)
            plan[0, at] = (source < level).astype(jnp.int32)
            plan[1, at] = jnp.where(source == level, local, 0)
            plan[2, at] = jnp.where(source < level, select(ups, level - 1), 0)

        @pl.when((source >= level) & (target < level))
        def _():
            at = select(downs, level - 1)
            plan[3, at] = (source > level).astype(jnp.int32)
            plan[4, at] = jnp.where(source == level, local, 0)
            plan[5, at] = jnp.where(source > level, select(downs, level), 0)

        @pl.when(target == level)
        def _():
            at = b & 7
            rank = jnp.where(source < level, select(ups, level - 1), select(downs, level))
            plan[6, at] = jnp.where(source == level, 0, jnp.where(source < level, 1, 2))
            plan[7, at] = jnp.where(source == level, local, 0)
            plan[8, at] = jnp.where(source == level, 0, rank)

        ups = tuple(
            count + ((source <= n) & (target > n)).astype(jnp.int32) for n, count in enumerate(ups)
        )
        downs = tuple(
            count + ((source > n) & (target <= n)).astype(jnp.int32)
            for n, count in enumerate(downs)
        )
        return ups, downs

    zeros = (jnp.int32(0),) * (levels - 1)
    ups, downs = lax.fori_loop(0, 8 * levels, block, (zeros, zeros))
    most = functools.reduce(jnp.maximum, ups + downs)
    branch[0] = sum((most > room).astype(jnp.int32) for room in CAPACITIES[:-1])


def migrate(old_pdfs, old_slot):
    peers = lax.axis_size("blocks")
    slots = old_pdfs.shape[0]
    blocks = old_slot.shape[0]
    if peers == EDGE and slots == 2:
        plan, branch = pl.pallas_call(
            functools.partial(plan_kernel, peers // 8),
            out_shape=[
                jax.ShapeDtypeStruct((9, 16), jnp.int32),
                jax.ShapeDtypeStruct((1,), jnp.int32),
            ],
            in_specs=[SMEM],
            out_specs=[SMEM, SMEM],
        )(old_slot)
        old = old_pdfs.reshape(slots, 19, 256, 128).transpose(1, 2, 0, 3).reshape(19, 512, 128)
        calls = [
            functools.partial(migrate_with, room, 1 + number)
            for number, room in enumerate(CAPACITIES)
        ]
        return lax.switch(branch[0], calls, plan, old)
    planes = 4
    tiles = pl.pallas_call(
        functools.partial(spread_kernel, planes, slots),
        grid=(EDGE // planes,),
        out_shape=jax.ShapeDtypeStruct((EDGE, slots * 152, 128), jnp.float32),
        in_specs=[pl.BlockSpec((slots, 19, planes * 1024), lambda g: (0, 0, g))],
        out_specs=pl.BlockSpec((planes, slots * 152, 128), lambda g: (g, 0, 0)),
        compiler_params=pltpu.CompilerParams(vmem_limit_bytes=58 * 2**20),
    )(old_pdfs)
    parts = peers // EDGE
    rows = 8 // parts
    if parts > 1:
        tiles = tiles.reshape(EDGE, slots * 19, parts, rows, 128).transpose(0, 2, 1, 3, 4)
        tiles = tiles.reshape(peers, slots * 19 * rows, 128)
    spread = lax.all_to_all(tiles, "blocks", split_axis=0, concat_axis=0, tiled=True)
    spread = spread.reshape(peers * slots, 19 * rows, 128)
    ordered = spread.at[old_slot].get(mode="promise_in_bounds")
    arrived = lax.all_to_all(ordered, "blocks", split_axis=0, concat_axis=0, tiled=True)
    if parts > 1:
        arrived = arrived.reshape(EDGE, parts, 19, rows, 128).transpose(0, 2, 1, 3, 4)
    return arrived.reshape(EDGE, 19, 8, 128)


def per_device(old_pdfs, old_slot, neighbours, cell_flags):
    state = migrate(old_pdfs, old_slot)
    flags = cell_flags.reshape(EDGE, 8, 128)
    layers = lax.axis_size("blocks") // 4

    def tiles(*lead):
        return pltpu.VMEM(lead + (8, 128), jnp.float32)

    out = pl.pallas_call(
        functools.partial(steps_kernel, layers),
        out_shape=jax.ShapeDtypeStruct((19, EDGE, 8, 128), jnp.float32),
        in_specs=[SMEM, VMEM, VMEM],
        out_specs=VMEM,
        scratch_shapes=[tiles(EDGE, 19)] * 2
        + [tiles(10), tiles(5), tiles(5)] * STEPS
        + [tiles(4, 10), tiles(4, 5), tiles(4, 5)] * STEPS
        + [
            pltpu.VMEM((5, EDGE, 128), jnp.float32),
            pltpu.VMEM((5, EDGE + 8, 128), jnp.float32),
            pltpu.SemaphoreType.DMA((STEPS, 12)),
            pltpu.SemaphoreType.DMA((STEPS, 12)),
        ],
        compiler_params=pltpu.CompilerParams(
            collective_id=0, has_side_effects=True, vmem_limit_bytes=40 * 2**20
        ),
    )(neighbours, flags, state)
    return out.reshape(1, 19, EDGE * EDGE * EDGE)


def solution(mesh):
    in_specs = (P("blocks", None, None), P(), P("blocks", None), P("blocks", None))
    out_specs = P("blocks", None, None)
    return jax.shard_map(
        per_device, mesh=mesh, in_specs=in_specs, out_specs=out_specs, check_vma=False
    )
```
